32 devices in a mesh: dp: 16 (over z, y, core), tensor: 2 (over x).
Axes of the slice: x: 2, y: 2, z: 4, core: 2. Of those that a mesh axis runs over, the one named last changes fastest.
Arguments:
- tokens: bfloat16 [32, 1024, 768], P('dp'), may hold values from -6 to 6
- cotangent: bfloat16 [32, 1024, 768], P('dp'), may hold values from -6 to 6
- prev_att: float32 [32, 768], P('dp'), may hold values from -6 to 6
- prev_ffn: float32 [32, 768], P('dp'), may hold values from -6 to 6
- numerator_state: float32 [32, 768], P('dp', 'tensor'), may hold values from -6 to 6
- denominator_state: float32 [32, 768], P('dp', 'tensor'), may hold values from 0.5 to 4
- exponent_offset_state: float32 [32, 768], P('dp', 'tensor'), may hold values from -1 to 1
- ln1_gain: float32 [768], replicated, may hold values from 0.1 to 1.9
- ln1_bias: float32 [768], replicated, may hold values from -4 to 4
- ln2_gain: float32 [768], replicated, may hold values from 0.1 to 1.9
- ln2_bias: float32 [768], replicated, may hold values from -4 to 4
- mix_key: float32 [768], replicated, may hold values from 0.05 to 0.95
- mix_value: float32 [768], replicated, may hold values from 0.05 to 0.95
- mix_recept: float32 [768], replicated, may hold values from 0.05 to 0.95
- mix2_key: float32 [768], replicated, may hold values from 0.05 to 0.95
- mix2_recept: float32 [768], replicated, may hold values from 0.05 to 0.95
- time_decay: float32 [768], P('tensor'), may hold values from -7.5 to -1.5
- time_first: float32 [768], P('tensor'), may hold values from -1 to 1
- key_weight: bfloat16 [768, 768], P(None, 'tensor'), may hold values from -0.21875 to 0.21875
- value_weight: bfloat16 [768, 768], P(None, 'tensor'), may hold values from -0.21875 to 0.21875
- receptance_weight: bfloat16 [768, 768], P(None, 'tensor'), may hold values from -0.21875 to 0.21875
- output_weight: bfloat16 [768, 768], P('tensor'), may hold values from -0.625 to 0.625
- channel_key_weight: bfloat16 [768, 3072], P(None, 'tensor'), may hold values from -0.21875 to 0.21875
- channel_receptance_weight: bfloat16 [768, 768], P(None, 'tensor'), may hold values from -0.21875 to 0.21875
- channel_value_weight: bfloat16 [3072, 768], P('tensor'), may hold values from -0.109375 to 0.109375
Outputs:
- mixed_out: bfloat16 [32, 1024, 768], P('dp', None, 'tensor')
- grad_tokens: float32 [32, 1024, 768], P('dp')
- final_num: float32 [32, 768], P('dp', 'tensor')
- final_den: float32 [32, 768], P('dp', 'tensor')
- final_max: float32 [32, 768], P('dp', 'tensor')
- last_att: float32 [32, 768], P('dp')
- last_ffn: float32 [32, 768], P('dp')
- grad_ln1_gain: float32 [768], replicated
- grad_ln1_bias: float32 [768], replicated
- grad_ln2_gain: float32 [768], replicated
- grad_ln2_bias: float32 [768], replicated
- grad_mix_key: float32 [768], replicated
- grad_mix_value: float32 [768], replicated
- grad_mix_recept: float32 [768], replicated
- grad_mix2_key: float32 [768], replicated
- grad_mix2_recept: float32 [768], replicated
- grad_time_decay: float32 [768], replicated
- grad_time_first: float32 [768], replicated
- key_weight_gradient: float32 [768, 768], P('dp', 'tensor')
- value_weight_gradient: float32 [768, 768], P('dp', 'tensor')
- receptance_weight_gradient: float32 [768, 768], P('dp', 'tensor')
- output_weight_gradient: float32 [768, 768], P('tensor', 'dp')
- channel_key_gradient: float32 [768, 3072], P('dp', 'tensor')
- channel_receptance_gradient: float32 [768, 768], P('dp', 'tensor')
- channel_value_gradient: float32 [3072, 768], P('tensor', 'dp')
The draws below stay inside these ranges and needn't reach their ends.
All inputs are finite; a program needn't handle non-finite values.
Results may differ from the reference program's by a relative error of at most 0.012.
Values may be sent and summed in bfloat16 or wider, within the bound.
No kernel may reach another device: no remote copies, remote signals or barrier semaphores. Data moves between devices by JAX's collectives and lax.ppermute only.
A program may use at most 192 MiB of HBM per device.

```python
import math
import jax
import jax.numpy as jnp
from jax import lax

D = 768
FF = 3072
LEN = 1024
SEGS_DEV = 2
SEGS = 32


def raised(drawn, key, source, target, shards_of, factor):
    owner, partner = [(jnp.arange(drawn.shape[dim]) // (drawn.shape[dim] // shards_of)).reshape([-1 if axis == dim else 1 for axis in range(drawn.ndim)]) for dim in (source, target)]
    chosen = jax.random.permutation(key, shards_of)[partner]
    strong = (owner == chosen) | (owner == (partner + shards_of // 2) % shards_of)
    return jnp.where(strong, factor * drawn, drawn)


def shard_levels(own_key, extent, cuts, low, high):
    loudness = 1.0
    for axis_at, parts in cuts:
        draws = jax.random.uniform(jax.random.fold_in(jax.random.fold_in(own_key, 6), axis_at), (parts,), jnp.float32, low / len(cuts), high / len(cuts))
        loudness = loudness * jnp.repeat(jnp.exp(draws), extent[axis_at] // parts).reshape((-1,) + (1,) * (len(extent) - 1 - axis_at))
    return loudness


def noise(own_key, shape, width, bound, pieces=(), kind=jnp.bfloat16):
    values = jax.random.normal(own_key, shape, jnp.float32) * width
    if len(pieces) > 0:
        values = shard_levels(own_key, shape, pieces, -0.22, 0.18) * values
    return jnp.clip(values, min=-bound, max=bound).astype(kind)


def bell_draw_with(own_key, dims, deviation, limit, cuts, heavy, held_as=jnp.bfloat16):
    drawn = deviation * jax.random.normal(own_key, dims, jnp.float32)
    if cuts:
        drawn = drawn * shard_levels(own_key, dims, cuts, -0.22, 0.18)
    return jnp.clip(raised(drawn, jax.random.fold_in(own_key, 3), *heavy), -limit, limit).astype(held_as)


def setup_inputs(seed: int = 0) -> dict:
    key_of = jax.random.split(jax.random.key(seed), 26)
    tokens = bell_draw_with(key_of[0], (SEGS, LEN, D), 1.0, 6.0, ((0, 16),), (0, 2, 16, 2.0))
    cotangent = bell_draw_with(key_of[1], (SEGS, LEN, D), 1.0, 6.0, ((0, 16),), (0, 2, 16, 2.0))
    prev_att = noise(key_of[2], (SEGS, D), 1.0, 6.0, ((0, 16),), jnp.float32)
    prev_ffn = noise(key_of[3], (SEGS, D), 1.0, 6.0, ((0, 16),), jnp.float32)
    numerator_state = noise(key_of[4], (SEGS, D), 1.0, 6.0, ((0, 16), (1, 2)), jnp.float32)
    denominator_state = jnp.clip(jnp.exp(math.log(4.0) - 2.0794415 * jax.random.uniform(key_of[5], (SEGS, D), jnp.float32) ** shard_levels(key_of[5], (SEGS, D), ((0, 16), (1, 2)), -0.2, 0.2)), 0.5, 4.0)
    exponent_offset_state = jnp.clip(jax.random.uniform(key_of[6], (SEGS, D), jnp.float32, -1.0, 1.0) * shard_levels(key_of[6], (SEGS, D), ((0, 16), (1, 2)), -0.4, 0.0), -1.0, 1.0)
    ln1_gain = jnp.clip(1.0 + 0.18 * jax.random.normal(key_of[7], (D,), jnp.float32), 0.1, 1.9)
    ln1_bias = noise(key_of[8], (D,), 0.3, 4.0, (), jnp.float32)
    ln2_gain = jnp.clip(1.0 + 0.18 * jax.random.normal(key_of[9], (D,), jnp.float32), 0.1, 1.9)
    ln2_bias = noise(key_of[10], (D,), 0.3, 4.0, (), jnp.float32)
    mix_key = jnp.clip(jax.random.uniform(key_of[11], (D,), jnp.float32, 0.05, 0.95), 0.05, 0.95)
    mix_value = jnp.clip(jax.random.uniform(key_of[12], (D,), jnp.float32, 0.05, 0.95), 0.05, 0.95)
    mix_recept = jnp.clip(jax.random.uniform(key_of[13], (D,), jnp.float32, 0.05, 0.95), 0.05, 0.95)
    mix2_key = jnp.clip(jax.random.uniform(key_of[14], (D,), jnp.float32, 0.05, 0.95), 0.05, 0.95)
    mix2_recept = jnp.clip(jax.random.uniform(key_of[15], (D,), jnp.float32, 0.05, 0.95), 0.05, 0.95)
    time_decay = jnp.clip(-7.5 + 6.0 * jax.random.uniform(key_of[16], (D,), jnp.float32) ** shard_levels(key_of[16], (D,), ((0, 2),), -0.2, 0.2), -7.5, -1.5)
    time_first = jnp.clip(jax.random.uniform(key_of[17], (D,), jnp.float32, -1.0, 1.0) * shard_levels(key_of[17], (D,), ((0, 2),), -0.4, 0.0), -1.0, 1.0)
    key_weight = noise(key_of[18], (D, D), D ** -0.5, 0.21875, ((1, 2),))
    value_weight = noise(key_of[19], (D, D), D ** -0.5, 0.21875, ((1, 2),))
    receptance_weight = noise(key_of[20], (D, D), D ** -0.5, 0.21875, ((1, 2),))
    output_weight = noise(key_of[21], (D, D), (D // 8) ** -0.5, 0.625, ((0, 2),))
    channel_key_weight = noise(key_of[22], (D, FF), D ** -0.5, 0.21875, ((1, 2),))
    channel_receptance_weight = noise(key_of[23], (D, D), D ** -0.5, 0.21875, ((1, 2),))
    channel_value_weight = noise(key_of[24], (FF, D), FF ** -0.5, 0.109375, ((0, 2),))
    return {"tokens": tokens, "cotangent": cotangent, "prev_att": prev_att, "prev_ffn": prev_ffn, "numerator_state": numerator_state, "denominator_state": denominator_state, "exponent_offset_state": exponent_offset_state, "ln1_gain": ln1_gain, "ln1_bias": ln1_bias, "ln2_gain": ln2_gain, "ln2_bias": ln2_bias, "mix_key": mix_key, "mix_value": mix_value, "mix_recept": mix_recept, "mix2_key": mix2_key, "mix2_recept": mix2_recept, "time_decay": time_decay, "time_first": time_first, "key_weight": key_weight, "value_weight": value_weight, "receptance_weight": receptance_weight, "output_weight": output_weight, "channel_key_weight": channel_key_weight, "channel_receptance_weight": channel_receptance_weight, "channel_value_weight": channel_value_weight}


@jax.custom_vjp
def low(v):
    return lax.optimization_barrier(v.astype(jnp.bfloat16)).astype(jnp.float32)

@jax.custom_vjp
def low_back(v):
    return v

def low_keep(v):
    return (low(v), None)

def low_pass(kept, grad):
    return (grad,)

def back_keep(v):
    return (v, None)

def back_low(kept, grad):
    return (low(grad),)
low.defvjp(low_keep, low_pass)
low_back.defvjp(back_keep, back_low)

def matmul(left, right):
    return jnp.matmul(left, right, precision=lax.Precision.HIGHEST)

def layer_norm(value_matrix, gain, bias):
    center = value_matrix - lax.optimization_barrier(jnp.mean(value_matrix, axis=-1, keepdims=True))
    spread = lax.optimization_barrier(jnp.mean(center * center, axis=-1, keepdims=True))
    return center * lax.rsqrt(spread + 1e-05) * gain + bias

def shifted(value_matrix, previous):
    return jnp.concatenate([previous[:, None, :], value_matrix[:, :-1, :]], axis=1)

def blend(current, before, weight):
    return current * weight + before * (1.0 - weight)

def weighted_value_sweep(key_matrix, value_matrix, decay_rates, first_token_boost, numerator_begin, denominator_begin, maximum_begin):
    rate = jnp.exp(decay_rates)

    @jax.checkpoint
    def advance(carry, pair):
        numer, denom, upper_bound = carry
        current_key, value_now = pair
        plus_first_boost = first_token_boost + current_key
        running_peak = jnp.maximum(upper_bound, plus_first_boost)
        old_part = jnp.exp(upper_bound - running_peak)
        fresh_portion = jnp.exp(plus_first_boost - running_peak)
        result = (old_part * numer + fresh_portion * value_now) / (old_part * denom + fresh_portion)
        decayed = upper_bound - rate
        next_top = jnp.maximum(decayed, current_key)
        old_keep = jnp.exp(decayed - next_top)
        new_keep = jnp.exp(current_key - next_top)
        return ((old_keep * numer + new_keep * value_now, old_keep * denom + new_keep, next_top), result)
    carry, results = lax.scan(advance, (numerator_begin, denominator_begin, maximum_begin), (jnp.swapaxes(key_matrix, 0, 1), jnp.swapaxes(value_matrix, 0, 1)))
    return (jnp.swapaxes(results, 0, 1), carry[0], carry[1], carry[2])

def forward(tokens, params, prev_att, prev_ffn, numerator_begin, denominator_begin, maximum_begin):
    ln1_gain, ln1_bias, ln2_gain, ln2_bias, mix_key, mix_value, mix_recept, mix2_key, mix2_recept, time_decay, time_first, key_weight, value_weight, receptance_weight, output_weight, channel_key_weight, channel_receptance_weight, channel_value_weight = params
    normed = layer_norm(tokens, ln1_gain, ln1_bias)
    before = shifted(normed, prev_att)
    key_input = low(blend(normed, before, mix_key))
    value_input = low(blend(normed, before, mix_value))
    receptance_input = low(blend(normed, before, mix_recept))
    key_matrix = low_back(matmul(key_input, key_weight))
    value_matrix = low_back(matmul(value_input, value_weight))
    receptance_rows = low_back(matmul(receptance_input, receptance_weight))
    mixed, numer, denom, upper_bound = weighted_value_sweep(key_matrix, value_matrix, time_decay, time_first, numerator_begin, denominator_begin, maximum_begin)
    gated = low(jax.nn.sigmoid(receptance_rows) * mixed)
    middle = tokens + low_back(matmul(gated, output_weight))
    normed2 = layer_norm(middle, ln2_gain, ln2_bias)
    before2 = shifted(normed2, prev_ffn)
    second_key_input = low(blend(normed2, before2, mix2_key))
    second_receptance_input = low(blend(normed2, before2, mix2_recept))
    hidden_preactivation = low_back(matmul(second_key_input, channel_key_weight))
    hidden_activation = low(jnp.square(jax.nn.relu(hidden_preactivation)))
    ffn_values = low_back(matmul(hidden_activation, channel_value_weight))
    channel_gate = jax.nn.sigmoid(low_back(matmul(second_receptance_input, channel_receptance_weight)))
    return (middle + channel_gate * ffn_values, (numer, denom, upper_bound, normed[:, -1], normed2[:, -1]))

def reference(tokens, cotangent, prev_att, prev_ffn, numerator_state, denominator_state, exponent_offset_state, ln1_gain, ln1_bias, ln2_gain, ln2_bias, mix_key, mix_value, mix_recept, mix2_key, mix2_recept, time_decay, time_first, key_weight, value_weight, receptance_weight, output_weight, channel_key_weight, channel_receptance_weight, channel_value_weight):
    params = tuple((item.astype(jnp.float32) for item in (ln1_gain, ln1_bias, ln2_gain, ln2_bias, mix_key, mix_value, mix_recept, mix2_key, mix2_recept, time_decay, time_first, key_weight, value_weight, receptance_weight, output_weight, channel_key_weight, channel_receptance_weight, channel_value_weight)))
    groups = SEGS // SEGS_DEV

    def split(array):
        return array.reshape((groups, SEGS_DEV) + array.shape[1:])
    items = tuple((split(array) for array in (tokens, cotangent, prev_att, prev_ffn, numerator_state, denominator_state, exponent_offset_state)))

    def one_group(totals, item):
        seg_tokens, seg_cot, seg_prev_att, seg_prev_ffn, seg_num, seg_den, seg_max = item

        def run(inputs, weights):
            return forward(inputs, weights, seg_prev_att, seg_prev_ffn, seg_num, seg_den, seg_max)
        output, pull, extras = jax.vjp(run, seg_tokens.astype(jnp.float32), params, has_aux=True)
        grad_in, grad_params = pull(seg_cot.astype(jnp.float32))
        totals = tuple((total + grad for total, grad in zip(totals, grad_params)))
        return (totals, (output.astype(jnp.bfloat16), grad_in) + tuple(extras))
    totals, results = lax.scan(one_group, tuple((jnp.zeros_like(item) for item in params)), items)
    merged = tuple((result.reshape((SEGS,) + result.shape[2:]) for result in results))
    return (merged[0], merged[1], merged[2], merged[3], merged[4], merged[5], merged[6], totals[0], totals[1], totals[2], totals[3], totals[4], totals[5], totals[6], totals[7], totals[8], totals[9], totals[10], totals[11], totals[12], totals[13], totals[14], totals[15], totals[16], totals[17])
```

```python
import functools

import jax
import jax.numpy as jnp
from jax import lax
from jax.experimental import pallas as pl
from jax.experimental.pallas import tpu as pltpu
from jax.sharding import PartitionSpec as P

F32 = jnp.float32
BF16 = jnp.bfloat16
STEP = 8
MIB = 1 << 20


def nn(left, right):
    return jnp.dot(left, right, preferred_element_type=F32)


def nt(left, right):
    return lax.dot_general(left, right, (((1,), (1,)), ((), ())), preferred_element_type=F32)


def sigmoid(x):
    return 1.0 / (1.0 + jnp.exp(-x))


def row_sum(x):
    return jnp.sum(x, axis=0, keepdims=True)


def lane_mean(x):
    return jnp.mean(x, axis=-1, keepdims=True)


def normalize(x):
    center = x - lane_mean(x)
    scale = lax.rsqrt(lane_mean(center * center) + 1e-05)
    return center * scale, scale


def order_matrix(count, turned=False):
    chunks = count // STEP
    row = lax.broadcasted_iota(jnp.int32, (count, count), 1 if turned else 0)
    token = lax.broadcasted_iota(jnp.int32, (count, count), 0 if turned else 1)
    return (token == (row % chunks) * STEP + row // chunks).astype(BF16)


def row_before(x, first):
    chunks = x.shape[0] // STEP
    ends = x[-chunks:, :]
    rows = lax.broadcasted_iota(jnp.int32, ends.shape, 0)
    head = jnp.where(rows == 0, first, pltpu.roll(ends, 1, 0))
    return jnp.concatenate([head, x[:-chunks, :]])


def row_after(x, last):
    chunks = x.shape[0] // STEP
    starts = x[:chunks, :]
    rows = lax.broadcasted_iota(jnp.int32, starts.shape, 0)
    tail = jnp.where(rows == chunks - 1, last, pltpu.roll(starts, chunks - 1, 0))
    return jnp.concatenate([x[chunks:, :], tail])


def wkv_forward(first_block, k_ref, channel_ref, save_ref, start_ref, final_ref, carry, work):
    chunks = start_ref.shape[1]
    rate = jnp.exp(channel_ref[0:1, :])
    boost = channel_ref[1:2, :]

    @pl.when(first_block)
    def _():
        carry[0:3, :] = channel_ref[2:5, :]

    def keys(step):
        return k_ref[step * chunks : (step + 1) * chunks, :]

    peak = keys(STEP - 1)
    for step in range(STEP - 1):
        peak = jnp.maximum(peak, keys(step) - (STEP - 1.0 - step) * rate)
    number = jnp.zeros_like(peak)
    weight = jnp.zeros_like(peak)
    for step in range(STEP):
        part = jnp.exp(keys(step) - (STEP - 1.0 - step) * rate - peak)
        number = number + part * save_ref[0, step * chunks : (step + 1) * chunks, :]
        weight = weight + part
    work[0, 0:chunks, :] = peak
    top = carry[2:3, :]
    for chunk in range(chunks):
        work[1, chunk : chunk + 1, :] = top
        top = jnp.maximum(top - STEP * rate, work[0, chunk : chunk + 1, :])
    work[1, chunks : chunks + 1, :] = top
    tops = work[1, 0:chunks, :]
    later = work[1, 1 : chunks + 1, :]
    fresh = jnp.exp(peak - later)
    work[0, 0:chunks, :] = jnp.exp(tops - STEP * rate - later)
    work[2, 0:chunks, :] = fresh * number
    work[3, 0:chunks, :] = fresh * weight
    num = carry[0:1, :]
    den = carry[1:2, :]
    for chunk in range(chunks):
        at = slice(chunk, chunk + 1)
        start_ref[0, at, :] = num
        start_ref[1, at, :] = den
        num = work[0, at, :] * num + work[2, at, :]
        den = work[0, at, :] * den + work[3, at, :]
    carry[0:1, :] = num
    carry[1:2, :] = den
    carry[2:3, :] = top
    final_ref[0:3, :] = carry[0:3, :]

    num = start_ref[0, :, :]
    den = start_ref[1, :, :]
    top = tops
    for step in range(STEP):
        at = slice(step * chunks, (step + 1) * chunks)
        key = keys(step)
        value = save_ref[0, at, :]
        gap = top - (boost + key)
        small = jnp.exp(-jnp.abs(gap))
        state_wins = gap > 0
        old = jnp.where(state_wins, 1.0, small)
        now = jnp.where(state_wins, small, 1.0)
        inverse = 1.0 / (old * den + now)
        old = old * inverse
        now = now * inverse
        save_ref[1, at, :] = old * num + now * value
        save_ref[3, at, :] = old
        save_ref[4, at, :] = now
        faded = top - rate
        gap = faded - key
        small = jnp.exp(-jnp.abs(gap))
        state_wins = gap > 0
        keep = jnp.where(state_wins, 1.0, small)
        fresh = jnp.where(state_wins, small, 1.0)
        save_ref[5, at, :] = keep
        save_ref[6, at, :] = fresh
        num = keep * num + fresh * value
        den = keep * den + fresh
        top = jnp.maximum(faded, key)


def project_and_scan(inputs, weights, channel_ref, gated_ref, save_ref, start_ref, final_ref, k_ref, carry, work):
    k_ref[...] = nn(inputs[0], weights[0])
    save_ref[0, :, :] = nn(inputs[1], weights[1])
    gate = sigmoid(nn(inputs[2], weights[2]))
    save_ref[2, :, :] = gate
    wkv_forward(pl.program_id(0) == 0, k_ref, channel_ref, save_ref, start_ref, final_ref, carry, work)
    gated_ref[...] = (gate * save_ref[1, :, :]).astype(BF16)


def first_kernel(
    meta, tokens_ref, vector_ref, wk_ref, wv_ref, wr_ref, channel_ref,
    mix_ref, bound_ref, last_ref, gated_ref, save_ref, start_ref, final_ref,
    k_ref, carry, work, row,
):
    @pl.when(pl.program_id(0) == 0)
    def _():
        row[...] = vector_ref[5:6, :]

    tokens = nn(order_matrix(tokens_ref.shape[0]), tokens_ref[...])
    hat, _ = normalize(tokens)
    normed = hat * vector_ref[0:1, :] + vector_ref[1:2, :]
    first = row[...]
    bound_ref[0, :, :] = jnp.broadcast_to(first, bound_ref.shape[1:])
    before = row_before(normed, first)
    step = normed - before
    count = normed.shape[0]
    row[...] = normed[count - 1 : count, :]
    last_ref[...] = normed[count - 1 : count, :]
    mixed = [(before + step * vector_ref[2 + n : 3 + n, :]).astype(BF16) for n in range(3)]
    for n in range(3):
        mix_ref[n, :, :] = mixed[n]
    project_and_scan(
        mixed, (wk_ref[...], wv_ref[...], wr_ref[...]), channel_ref,
        gated_ref, save_ref, start_ref, final_ref, k_ref, carry, work,
    )


def second_kernel(
    mix_ref, weight_ref, channel_ref, gated_ref, save_ref, start_ref, final_ref, k_ref, carry, work
):
    project_and_scan(
        [mix_ref[n, :, :] for n in range(3)], [weight_ref[n, :, :] for n in range(3)], channel_ref,
        gated_ref, save_ref, start_ref, final_ref, k_ref, carry, work,
    )


def middle_kernel(
    meta, tokens_ref, own_ref, far_ref, wo_own_ref, wo_far_ref, vector_ref,
    middle_ref, mix_ref, bound_ref, last_ref, row,
):
    @pl.when(pl.program_id(0) == 0)
    def _():
        row[...] = vector_ref[4:5, :]

    middle = (
        nn(order_matrix(tokens_ref.shape[0]), tokens_ref[...])
        + nn(own_ref[...], wo_own_ref[...])
        + nn(far_ref[...], wo_far_ref[...])
    )
    middle_ref[...] = middle
    hat, _ = normalize(middle)
    normed = hat * vector_ref[0:1, :] + vector_ref[1:2, :]
    first = row[...]
    bound_ref[0, :, :] = jnp.broadcast_to(first, bound_ref.shape[1:])
    before = row_before(normed, first)
    step = normed - before
    count = normed.shape[0]
    row[...] = normed[count - 1 : count, :]
    last_ref[...] = normed[count - 1 : count, :]
    for n in range(2):
        mix_ref[n, :, :] = (before + step * vector_ref[2 + n : 3 + n, :]).astype(BF16)


def norm_backward(x, vectors, bound, grads, weights, row, sums_ref):
    gain, bias = vectors
    hat, scale = normalize(x)
    normed = hat * gain + bias
    step = normed - row_before(normed, bound)
    total = grads[0]
    current = grads[0] * weights[0]
    sums_ref[2:3, :] += row_sum(grads[0] * step)
    for n in range(1, len(grads)):
        total = total + grads[n]
        current = current + grads[n] * weights[n]
        sums_ref[2 + n : 3 + n, :] += row_sum(grads[n] * step)
    shifted = total - current
    flow = current + row_after(shifted, row[...])
    row[...] = shifted[0:1, :]
    sums_ref[0:1, :] += row_sum(flow * hat)
    sums_ref[1:2, :] += row_sum(flow)
    inner = flow * gain
    return scale * (inner - lane_mean(inner) - hat * lane_mean(inner * hat))


def channel_kernel(
    meta, cot_ref, middle_ref, mix_ref, bound_ref, vector_ref,
    ck_own_ref, ck_far_ref, cv_own_ref, cv_far_ref, cr_ref, wo_own_ref, wo_far_ref,
    mixed_ref, h_own_ref, h_far_ref, dp_own_ref, dp_far_ref, dval_ref, drec_ref,
    dmid_ref, datt_ref, dg_own_ref, dg_far_ref, sums_ref, row,
):
    @pl.when(pl.program_id(0) == 0)
    def _():
        row[...] = jnp.zeros_like(row)
        sums_ref[...] = jnp.zeros_like(sums_ref)

    key_in = mix_ref[0, :, :]
    relu_own = jnp.maximum(nn(key_in, ck_own_ref[...]), 0.0)
    hidden = (relu_own * relu_own).astype(BF16)
    h_own_ref[...] = hidden
    values = nn(hidden, cv_own_ref[...])
    relu_far = jnp.maximum(nn(key_in, ck_far_ref[...]), 0.0)
    hidden = (relu_far * relu_far).astype(BF16)
    h_far_ref[...] = hidden
    values = values + nn(hidden, cv_far_ref[...])
    gate = sigmoid(nn(mix_ref[1, :, :], cr_ref[...]))
    middle = middle_ref[...]
    count = middle.shape[0]
    mixed = (middle + gate * values).astype(BF16)
    mixed_ref[...] = nn(order_matrix(count, True), mixed).astype(BF16)
    grad = nn(order_matrix(count), cot_ref[...])
    passed = grad * gate
    d_values = passed.astype(BF16)
    dval_ref[...] = d_values
    d_rec = (passed * values * (1.0 - gate)).astype(BF16)
    drec_ref[...] = d_rec
    d_pre = (2.0 * relu_own * nt(d_values, cv_own_ref[...])).astype(BF16)
    dp_own_ref[...] = d_pre
    d_key = nt(d_pre, ck_own_ref[...])
    d_pre = (2.0 * relu_far * nt(d_values, cv_far_ref[...])).astype(BF16)
    dp_far_ref[...] = d_pre
    d_key = d_key + nt(d_pre, ck_far_ref[...])
    d_recept = nt(d_rec, cr_ref[...])
    d_middle = grad + norm_backward(
        middle, (vector_ref[0:1, :], vector_ref[1:2, :]), bound_ref[0, 0:1, :],
        (d_key, d_recept), (vector_ref[2:3, :], vector_ref[3:4, :]), row, sums_ref,
    )
    dmid_ref[...] = d_middle
    d_att = d_middle.astype(BF16)
    datt_ref[...] = d_att
    dg_own_ref[...] = nt(d_att, wo_own_ref[...])
    dg_far_ref[...] = nt(d_att, wo_far_ref[...])


def scan_back_kernel(
    dg_ref, save_ref, start_ref, channel_ref, out_ref, sums_ref, dy_ref, dk_ref, dv_ref, carry, work
):
    chunks = start_ref.shape[1]

    @pl.when(pl.program_id(0) == 0)
    def _():
        carry[...] = jnp.zeros_like(carry)
        sums_ref[...] = jnp.zeros_like(sums_ref)

    gate = save_ref[2, :, :]
    dy = dg_ref[...] * gate
    dy_ref[...] = dy
    out_ref[2, :, :] = (dy * save_ref[1, :, :] * (1.0 - gate)).astype(BF16)

    def at(step):
        return slice(step * chunks, (step + 1) * chunks)

    gn = jnp.zeros((chunks, dy.shape[1]), F32)
    gd = jnp.zeros_like(gn)
    product = jnp.ones_like(gn)
    for step in reversed(range(STEP)):
        part = save_ref[3, at(step), :] * dy_ref[at(step), :]
        keep = save_ref[5, at(step), :]
        gn = part + keep * gn
        gd = keep * gd - part * save_ref[1, at(step), :]
        product = product * keep
    work[0, 0:chunks, :] = gn
    work[1, 0:chunks, :] = gd
    work[2, 0:chunks, :] = product
    gn = carry[0:1, :]
    gd = carry[1:2, :]
    for chunk in reversed(range(chunks)):
        row = slice(chunk, chunk + 1)
        work[3, row, :] = gn
        work[4, row, :] = gd
        gn = work[0, row, :] + work[2, row, :] * gn
        gd = work[1, row, :] + work[2, row, :] * gd
    carry[0:1, :] = gn
    carry[1:2, :] = gd
    work[0, 0:chunks, :] = start_ref[0, :, :]
    work[1, 0:chunks, :] = start_ref[1, :, :]
    work[0, chunks : chunks + 1, :] = carry[2:3, :]
    work[1, chunks : chunks + 1, :] = carry[3:4, :]
    carry[2:3, :] = start_ref[0, 0:1, :]
    carry[3:4, :] = start_ref[1, 0:1, :]
    gn = work[3, 0:chunks, :]
    gd = work[4, 0:chunks, :]
    decay = STEP * (gn * work[0, 1 : chunks + 1, :] + gd * work[1, 1 : chunks + 1, :])
    first = jnp.zeros_like(gn)
    for step in reversed(range(STEP)):
        place = at(step)
        dy = dy_ref[place, :]
        value = save_ref[0, place, :]
        wkv = save_ref[1, place, :]
        share = save_ref[4, place, :] * dy
        bonus = share * (value - wkv)
        fresh = save_ref[6, place, :]
        through = fresh * (gn * value + gd)
        d_key = bonus + through
        dk_ref[place, :] = d_key
        dv_ref[place, :] = share + fresh * gn
        first = first + bonus
        decay = decay - through - float(step) * d_key
        part = save_ref[3, place, :] * dy
        keep = save_ref[5, place, :]
        gn = part + keep * gn
        gd = keep * gd - part * wkv
    sums_ref[0:1, :] -= row_sum(decay) * jnp.exp(channel_ref[0:1, :])
    sums_ref[1:2, :] += row_sum(first)
    out_ref[0, :, :] = dk_ref[...].astype(BF16)
    out_ref[1, :, :] = dv_ref[...].astype(BF16)


def last_kernel(
    meta, tokens_ref, dmid_ref, own_ref, far_ref, wk_ref, wv_ref, wr_ref, weight_ref, bound_ref,
    vector_ref, grad_ref, sums_ref, row,
):
    @pl.when(pl.program_id(0) == 0)
    def _():
        row[...] = jnp.zeros_like(row)
        sums_ref[...] = jnp.zeros_like(sums_ref)

    grads = [
        nt(own_ref[n, :, :], w_ref[...]) + nt(far_ref[n, :, :], weight_ref[n, :, :])
        for n, w_ref in enumerate((wk_ref, wv_ref, wr_ref))
    ]
    part = norm_backward(
        nn(order_matrix(tokens_ref.shape[0]), tokens_ref[...]), (vector_ref[0:1, :], vector_ref[1:2, :]), bound_ref[0, 0:1, :],
        grads, [vector_ref[2 + n : 3 + n, :] for n in range(3)], row, sums_ref,
    )
    grad = (dmid_ref[...] + part).astype(BF16)
    grad_ref[...] = nn(order_matrix(grad.shape[0], True), grad).astype(BF16)


def weight_gradient_kernel(order, groups, meta, left_ref, right_ref, out_ref, turned, placed):
    @pl.when(pl.program_id(1) == 0)
    def _():
        whole = left_ref.shape[1]
        for col in range(0, whole, 128):
            turned[col : col + 128, :] = left_ref[:, col : col + 128].T
        if groups > 1:
            rows = whole // groups
            for spot, other in enumerate(order):
                start = pl.multiple_of((meta[1] ^ other) * rows, rows)
                placed[spot * rows : (spot + 1) * rows, :] = turned[pl.ds(start, rows), :]

    source = placed if groups > 1 else turned
    out_ref[...] = nn(source[...], right_ref[...]).astype(BF16)


def params(mib, steps=None):
    return pltpu.CompilerParams(vmem_limit_bytes=mib * MIB, dimension_semantics=steps)


def whole(shape):
    return pl.BlockSpec(shape, lambda *_: (0,) * len(shape))


def weight_gradient(order, groups, meta, lefts, rights, tile):
    many, length, width = lefts.shape
    wide = rights.shape[2]
    tiles = wide // tile
    return pl.pallas_call(
        functools.partial(weight_gradient_kernel, order, groups),
        grid_spec=pltpu.PrefetchScalarGridSpec(
            num_scalar_prefetch=1,
            grid=(many, tiles),
            in_specs=[
                pl.BlockSpec((None, length, width), lambda m, n, meta: (m, 0, 0)),
                pl.BlockSpec((None, length, tile), lambda m, n, meta: (m, 0, n)),
            ],
            out_specs=pl.BlockSpec((width, tile), lambda m, n, meta: (0, m * tiles + n)),
            scratch_shapes=[pltpu.VMEM((width, length), BF16), pltpu.VMEM((width, length), BF16)],
        ),
        out_shape=jax.ShapeDtypeStruct((width, many * wide), BF16),
        compiler_params=params(40),
        cost_estimate=pl.CostEstimate(
            flops=2 * many * length * width * wide, bytes_accessed=4 * many * length * width, transcendentals=0
        ),
        name="weight_gradient",
    )(meta, lefts, rights)


def swapped(array):
    return lax.ppermute(array, "tensor", [(0, 1), (1, 0)])


def crossed(array, size, bit):
    return lax.ppermute(array, "dp", [(n, n ^ bit) for n in range(size)])


def added(mine, theirs, kind):
    return (mine.astype(F32) + theirs.astype(F32)).astype(kind)


def partner_copy(weight, core, size):
    rows = weight.shape[0] // 2
    half = swapped(lax.dynamic_slice_in_dim(weight, core * rows, rows, 0))
    other = crossed(half, size, 1)
    return jnp.where(core == 0, jnp.concatenate([half, other]), jnp.concatenate([other, half]))


def summed_everywhere(array, size):
    bit = 1
    array = array + crossed(array, size, bit)
    array = array + swapped(array)
    bit = 2
    while bit < size:
        array = array + crossed(array, size, bit)
        bit *= 2
    return array


def scattered_sum(own, far, size, groups):
    if groups == 1:
        total = own.astype(F32) + swapped(far).astype(F32)
        return lax.psum_scatter(total, "dp", scatter_dimension=0, tiled=True)
    half = own.shape[0] // 2
    own_in = crossed(own[half:], size, 1)
    far_in = crossed(far[half:], size, 1)
    far = added(far[:half], far_in, BF16)
    own = added(own[:half], own_in, BF16)
    own = added(own, swapped(far), BF16)
    bit = 2
    while bit < size:
        half = own.shape[0] // 2
        kind = F32 if bit * 2 == size else BF16
        own = added(own[:half], crossed(own[half:], size, bit), kind)
        bit *= 2
    return own


def shards(
    size, tokens, cotangent, prev_att, prev_ffn, numerator_state, denominator_state, exponent_offset_state,
    ln1_gain, ln1_bias, ln2_gain, ln2_bias, mix_key, mix_value, mix_recept, mix2_key, mix2_recept,
    time_decay, time_first, key_weight, value_weight, receptance_weight, output_weight,
    channel_key_weight, channel_receptance_weight, channel_value_weight,
):
    _, length, width = tokens.shape
    half = key_weight.shape[1]
    units = channel_key_weight.shape[1]
    block = min(256, length)
    blocks = length // block
    chunks = block // STEP
    side = lax.axis_index("tensor")
    place = lax.axis_index("dp")
    core = place % 2
    meta = jnp.stack([side, place]).astype(jnp.int32)
    rows = width // size
    groups = size if rows % 16 == 0 else 1
    order = []
    for spot in range(size):
        other, bit = 0, size // 2
        while bit:
            other |= (spot & 1) * bit
            spot //= 2
            bit //= 2
        order.append(other)

    def mine(array):
        return lax.dynamic_index_in_dim(array, side, 0, keepdims=False)

    def theirs(array):
        return lax.dynamic_index_in_dim(array, 1 - side, 0, keepdims=False)

    states = (numerator_state, denominator_state, exponent_offset_state)
    empty = jnp.zeros((half,), F32)
    own_channels = jnp.stack([time_decay, time_first] + [mine(item) for item in states] + [empty] * 3)
    far_channels = swapped(jnp.stack([time_decay, time_first] + [theirs(item) for item in states] + [empty] * 3))
    blank = jnp.zeros((width,), F32)
    vectors1 = jnp.stack([ln1_gain, ln1_bias, mix_key, mix_value, mix_recept, mine(prev_att), blank, blank])
    vectors2 = jnp.stack([ln2_gain, ln2_bias, mix2_key, mix2_recept, mine(prev_ffn), blank, blank, blank])

    far_kvr = jnp.stack(
        [partner_copy(item, core, size) for item in (key_weight, value_weight, receptance_weight)]
    )
    wo_far = partner_copy(output_weight, core, size)
    cr_far = partner_copy(channel_receptance_weight, core, size)
    ck_far = partner_copy(channel_key_weight, core, size)
    cv_far = partner_copy(channel_value_weight, core, size)
    cr = jnp.where(
        side == 0,
        jnp.concatenate([channel_receptance_weight, cr_far], axis=1),
        jnp.concatenate([cr_far, channel_receptance_weight], axis=1),
    )

    def segment_spec(index=lambda i: i):
        return pl.BlockSpec((None, block, width), lambda i, meta: (meta[0], index(i), 0))

    def rows_spec(columns, index=lambda i: i):
        return pl.BlockSpec((block, columns), lambda i, *_: (index(i), 0))

    def stack_spec(count, columns, index=lambda i: i, size_of=block):
        return pl.BlockSpec((count, size_of, columns), lambda i, *_: (0, index(i), 0))

    def bound_spec(index=lambda i: i):
        return pl.BlockSpec((1, 8, width), lambda i, *_: (index(i), 0, 0))

    def back(i):
        return blocks - 1 - i

    def shape(dims, kind):
        return jax.ShapeDtypeStruct(dims, kind)

    scan_shapes = [
        shape((length, half), BF16), shape((7, length, half), F32),
        shape((2, length // STEP, half), F32), shape((8, half), F32),
    ]
    scan_specs = [rows_spec(half), stack_spec(7, half), stack_spec(2, half, size_of=chunks), whole((8, half))]
    scan_scratch = [
        pltpu.VMEM((block, half), F32), pltpu.VMEM((8, half), F32), pltpu.VMEM((4, chunks + 8, half), F32),
    ]
    mix1, bounds1, last_att, gated_own, save_own, start_own, final_own = pl.pallas_call(
        first_kernel,
        grid_spec=pltpu.PrefetchScalarGridSpec(
            num_scalar_prefetch=1,
            grid=(blocks,),
            in_specs=[segment_spec(), whole((8, width))] + [whole((width, half))] * 3 + [whole((8, half))],
            out_specs=[stack_spec(3, width), bound_spec(), whole((1, width))] + scan_specs,
            scratch_shapes=scan_scratch + [pltpu.VMEM((1, width), F32)],
        ),
        out_shape=[
            shape((3, length, width), BF16), shape((blocks, 8, width), F32), shape((1, width), F32),
        ] + scan_shapes,
        compiler_params=params(48),
        name="time_mix_own",
    )(meta, tokens, vectors1, key_weight, value_weight, receptance_weight, own_channels)

    gated_far, save_far, start_far, final_far = pl.pallas_call(
        second_kernel,
        grid=(blocks,),
        in_specs=[stack_spec(3, width), whole((3, width, half)), whole((8, half))],
        out_specs=scan_specs,
        out_shape=scan_shapes,
        scratch_shapes=scan_scratch,
        compiler_params=params(48),
        name="time_mix_far",
    )(mix1, far_kvr, far_channels)

    middle, mix2, bounds2, last_ffn = pl.pallas_call(
        middle_kernel,
        grid_spec=pltpu.PrefetchScalarGridSpec(
            num_scalar_prefetch=1,
            grid=(blocks,),
            in_specs=[segment_spec(), rows_spec(half), rows_spec(half)]
            + [whole((half, width))] * 2 + [whole((8, width))],
            out_specs=[rows_spec(width), stack_spec(2, width), bound_spec(), whole((1, width))],
            scratch_shapes=[pltpu.VMEM((1, width), F32)],
        ),
        out_shape=[
            shape((length, width), F32), shape((2, length, width), BF16),
            shape((blocks, 8, width), F32), shape((1, width), F32),
        ],
        compiler_params=params(48),
        name="middle",
    )(meta, tokens, gated_own, gated_far, output_weight, wo_far, vectors2)

    (
        mixed, h_own, h_far, dpre_own, dpre_far, d_values, d_rec, d_middle, d_att, dg_own, dg_far, sums2,
    ) = pl.pallas_call(
        channel_kernel,
        grid_spec=pltpu.PrefetchScalarGridSpec(
            num_scalar_prefetch=1,
            grid=(blocks,),
            in_specs=[
                segment_spec(back), rows_spec(width, back), stack_spec(2, width, back), bound_spec(back),
                whole((8, width)), whole((width, units)), whole((width, units)),
                whole((units, width)), whole((units, width)), whole((width, width)),
                whole((half, width)), whole((half, width)),
            ],
            out_specs=[
                rows_spec(width, back), rows_spec(units, back), rows_spec(units, back),
                rows_spec(units, back), rows_spec(units, back), rows_spec(width, back),
                rows_spec(width, back), rows_spec(width, back), rows_spec(width, back),
                rows_spec(half, back), rows_spec(half, back), whole((8, width)),
            ],
            scratch_shapes=[pltpu.VMEM((1, width), F32)],
        ),
        out_shape=[
            shape((length, width), BF16), shape((length, units), BF16), shape((length, units), BF16),
            shape((length, units), BF16), shape((length, units), BF16), shape((length, width), BF16),
            shape((length, width), BF16), shape((length, width), F32), shape((length, width), BF16),
            shape((length, half), F32), shape((length, half), F32), shape((8, width), F32),
        ],
        compiler_params=params(60),
        name="channel_mix",
    )(
        meta, cotangent, middle, mix2, bounds2, vectors2, channel_key_weight, ck_far,
        channel_value_weight, cv_far, cr, output_weight, wo_far,
    )

    def gradients(left, right, tile):
        return weight_gradient(order, groups, meta, left, right, tile)

    def halves(array, axis):
        own = lax.dynamic_slice_in_dim(array, side * half, half, axis)
        far = lax.dynamic_slice_in_dim(array, (1 - side) * half, half, axis)
        return own, far

    g_ck = [gradients(mix2[0:1], item[None], 512) for item in (dpre_own, dpre_far)]
    g_cv = [gradients(d_values[None], item[None], 512) for item in (h_own, h_far)]
    g_cr = [gradients(mix2[1:2], item[None], half) for item in halves(d_rec, 1)]
    g_wo = [gradients(d_att[None], item[None], half) for item in (gated_own, gated_far)]

    def scan_back(grads, saved, starts, channels):
        return pl.pallas_call(
            scan_back_kernel,
            grid=(blocks,),
            in_specs=[
                rows_spec(half, back), stack_spec(7, half, back),
                stack_spec(2, half, back, size_of=chunks), whole((8, half)),
            ],
            out_specs=[stack_spec(3, half, back), whole((8, half))],
            out_shape=[shape((3, length, half), BF16), shape((8, half), F32)],
            scratch_shapes=[pltpu.VMEM((block, half), F32)] * 3
            + [pltpu.VMEM((8, half), F32), pltpu.VMEM((5, chunks + 8, half), F32)],
            compiler_params=params(48),
            name="scan_back",
        )(grads, saved, starts, channels)

    d_far, channel_sums_far = scan_back(dg_far, save_far, start_far, far_channels)
    d_own, channel_sums_own = scan_back(dg_own, save_own, start_own, own_channels)
    g_kvr = [gradients(mix1, item, half) for item in (d_own, d_far)]

    grad_part, sums1 = pl.pallas_call(
        last_kernel,
        grid_spec=pltpu.PrefetchScalarGridSpec(
            num_scalar_prefetch=1,
            grid=(blocks,),
            in_specs=[
                segment_spec(back), rows_spec(width, back), stack_spec(3, half, back), stack_spec(3, half, back),
                whole((width, half)), whole((width, half)), whole((width, half)), whole((3, width, half)),
                bound_spec(back), whole((8, width)),
            ],
            out_specs=[rows_spec(width, back), whole((8, width))],
            scratch_shapes=[pltpu.VMEM((1, width), F32)],
        ),
        out_shape=[shape((length, width), BF16), shape((8, width), F32)],
        compiler_params=params(48),
        name="time_mix_back",
    )(
        meta, tokens, d_middle, d_own, d_far, key_weight, value_weight, receptance_weight, far_kvr,
        bounds1, vectors1,
    )

    def both(own, far):
        return jnp.where(side == 0, jnp.stack([own, far]), jnp.stack([far, own]))

    grad_tokens = both(grad_part, swapped(grad_part)).astype(F32)
    mixed_own, mixed_far = halves(mixed, 1)
    mixed_out = both(mixed_own, swapped(mixed_far))

    back_states = swapped(final_far)
    finals = [both(final_own[n], back_states[n]) for n in range(3)]
    last_rows = jnp.concatenate([last_att, last_ffn])
    last_rows = both(last_rows, swapped(last_rows))

    def full(own, far):
        return jnp.where(side == 0, jnp.concatenate([own, far]), jnp.concatenate([far, own]))

    small = jnp.concatenate([
        sums1[0:2], sums2[0:2], sums1[2:5], sums2[2:4],
        jnp.stack([full(channel_sums_own[n], channel_sums_far[n]) for n in range(2)]),
    ])
    small = summed_everywhere(small, size)

    big = [scattered_sum(own, far, size, groups) for own, far in (g_ck, g_cv, g_cr, g_wo, g_kvr)]
    return (
        (mixed_out, grad_tokens, *finals, last_rows[:, 0], last_rows[:, 1])
        + tuple(small[n] for n in range(11))
        + tuple(big[4][:, n * half : (n + 1) * half] for n in range(3))
        + (big[3].T, big[0], big[2], big[1].T)
    )


def solution(mesh):
    split = P("dp", "tensor")
    turned = P("tensor", "dp")
    return jax.shard_map(
        functools.partial(shards, mesh.shape["dp"]),
        mesh=mesh,
        in_specs=(P("dp"), P("dp"), P("dp"), P("dp"), split, split, split)
        + (P(),) * 9
        + (P("tensor"), P("tensor"))
        + (P(None, "tensor"),) * 3
        + (P("tensor"), P(None, "tensor"), P(None, "tensor"), P("tensor")),
        out_specs=(P("dp", None, "tensor"), P("dp"), split, split, split, P("dp"), P("dp"))
        + (P(),) * 11
        + (split, split, split, turned, split, split, turned),
        check_vma=False,
    )
```

```python
import functools

import jax
import jax.numpy as jnp
from jax import lax
from jax.experimental import pallas as pl
from jax.experimental.pallas import tpu as pltpu
from jax.sharding import PartitionSpec as P

F32 = jnp.float32
BF16 = jnp.bfloat16
STEP = 8
MIB = 1 << 20


def nn(left, right):
    return jnp.dot(left, right, preferred_element_type=F32)


def nt(left, right):
    return lax.dot_general(left, right, (((1,), (1,)), ((), ())), preferred_element_type=F32)


def sigmoid(x):
    return 1.0 / (1.0 + jnp.exp(-x))


def row_sum(x):
    return jnp.sum(x, axis=0, keepdims=True)


def lane_mean(x):
    return jnp.mean(x, axis=-1, keepdims=True)


def normalize(x):
    center = x - lane_mean(x)
    scale = lax.rsqrt(lane_mean(center * center) + 1e-05)
    return center * scale, scale


def order_matrix(count, turned=False):
    chunks = count // STEP
    row = lax.broadcasted_iota(jnp.int32, (count, count), 1 if turned else 0)
    token = lax.broadcasted_iota(jnp.int32, (count, count), 0 if turned else 1)
    return (token == (row % chunks) * STEP + row // chunks).astype(BF16)


def row_before(x, first):
    chunks = x.shape[0] // STEP
    ends = x[-chunks:, :]
    rows = lax.broadcasted_iota(jnp.int32, ends.shape, 0)
    head = jnp.where(rows == 0, first, pltpu.roll(ends, 1, 0))
    return jnp.concatenate([head, x[:-chunks, :]])


def row_after(x, last):
    chunks = x.shape[0] // STEP
    starts = x[:chunks, :]
    rows = lax.broadcasted_iota(jnp.int32, starts.shape, 0)
    tail = jnp.where(rows == chunks - 1, last, pltpu.roll(starts, chunks - 1, 0))
    return jnp.concatenate([x[chunks:, :], tail])


def put_quarters(meta, target, pieces):
    core, side = meta[1] % 2, (meta[1] // 2) % 2
    rows = target.shape[-2] // 4
    spots = (2 * core + side, 2 * core + 1 - side, 2 - 2 * core + side, 3 - 2 * core - side)
    for spot, piece in zip(spots, pieces):
        at = pl.ds(pl.multiple_of(spot * rows, rows), rows)
        if len(target.shape) == 3:
            target[:, at, :] = piece[...]
        else:
            target[at, :] = piece[...]


def put_halves(meta, target, mine, other):
    core = meta[1] % 2
    half = target.shape[0] // 2
    for start, pieces in ((core * half, mine), ((1 - core) * half, other)):
        for piece in pieces:
            rows = piece.shape[0]
            target[pl.ds(pl.multiple_of(start, 16), rows), :] = piece[...]
            start = start + rows


def wkv_forward(first_block, k_ref, channel_ref, save_ref, start_ref, final_ref, carry, work):
    chunks = start_ref.shape[1]
    rate = jnp.exp(channel_ref[0:1, :])
    boost = channel_ref[1:2, :]

    @pl.when(first_block)
    def _():
        carry[0:3, :] = channel_ref[2:5, :]

    def keys(step):
        return k_ref[step * chunks : (step + 1) * chunks, :]

    peak = keys(STEP - 1)
    for step in range(STEP - 1):
        peak = jnp.maximum(peak, keys(step) - (STEP - 1.0 - step) * rate)
    number = jnp.zeros_like(peak)
    weight = jnp.zeros_like(peak)
    for step in range(STEP):
        part = jnp.exp(keys(step) - (STEP - 1.0 - step) * rate - peak)
        number = number + part * save_ref[0, step * chunks : (step + 1) * chunks, :]
        weight = weight + part
    work[0, 0:chunks, :] = peak
    top = carry[2:3, :]
    for chunk in range(chunks):
        work[1, chunk : chunk + 1, :] = top
        top = jnp.maximum(top - STEP * rate, work[0, chunk : chunk + 1, :])
    work[1, chunks : chunks + 1, :] = top
    tops = work[1, 0:chunks, :]
    later = work[1, 1 : chunks + 1, :]
    fresh = jnp.exp(peak - later)
    work[0, 0:chunks, :] = jnp.exp(tops - STEP * rate - later)
    work[2, 0:chunks, :] = fresh * number
    work[3, 0:chunks, :] = fresh * weight
    num = carry[0:1, :]
    den = carry[1:2, :]
    for chunk in range(chunks):
        at = slice(chunk, chunk + 1)
        start_ref[0, at, :] = num
        start_ref[1, at, :] = den
        num = work[0, at, :] * num + work[2, at, :]
        den = work[0, at, :] * den + work[3, at, :]
    carry[0:1, :] = num
    carry[1:2, :] = den
    carry[2:3, :] = top
    final_ref[0:3, :] = carry[0:3, :]

    num = start_ref[0, :, :]
    den = start_ref[1, :, :]
    top = tops
    for step in range(STEP):
        at = slice(step * chunks, (step + 1) * chunks)
        key = keys(step)
        value = save_ref[0, at, :]
        gap = top - (boost + key)
        small = jnp.exp(-jnp.abs(gap))
        state_wins = gap > 0
        old = jnp.where(state_wins, 1.0, small)
        now = jnp.where(state_wins, small, 1.0)
        inverse = 1.0 / (old * den + now)
        old = old * inverse
        now = now * inverse
        save_ref[1, at, :] = old * num + now * value
        save_ref[3, at, :] = old
        save_ref[4, at, :] = now
        faded = top - rate
        gap = faded - key
        small = jnp.exp(-jnp.abs(gap))
        state_wins = gap > 0
        keep = jnp.where(state_wins, 1.0, small)
        fresh = jnp.where(state_wins, small, 1.0)
        save_ref[5, at, :] = keep
        save_ref[6, at, :] = fresh
        num = keep * num + fresh * value
        den = keep * den + fresh
        top = jnp.maximum(faded, key)


def project_and_scan(inputs, weights, channel_ref, gated_ref, save_ref, start_ref, final_ref, k_ref, carry, work):
    k_ref[...] = nn(inputs[0], weights[0])
    save_ref[0, :, :] = nn(inputs[1], weights[1])
    gate = sigmoid(nn(inputs[2], weights[2]))
    save_ref[2, :, :] = gate
    wkv_forward(pl.program_id(0) == 0, k_ref, channel_ref, save_ref, start_ref, final_ref, carry, work)
    gated_ref[...] = (gate * save_ref[1, :, :]).astype(BF16)


def first_kernel(
    meta, tokens_ref, vector_ref, wk_ref, wv_ref, wr_ref, channel_ref,
    mix_ref, bound_ref, last_ref, gated_ref, save_ref, start_ref, final_ref,
    k_ref, carry, work, row,
):
    @pl.when(pl.program_id(0) == 0)
    def _():
        row[...] = vector_ref[5:6, :]

    tokens = nn(order_matrix(tokens_ref.shape[0]), tokens_ref[...])
    hat, _ = normalize(tokens)
    normed = hat * vector_ref[0:1, :] + vector_ref[1:2, :]
    first = row[...]
    bound_ref[0, :, :] = jnp.broadcast_to(first, bound_ref.shape[1:])
    before = row_before(normed, first)
    step = normed - before
    count = normed.shape[0]
    row[...] = normed[count - 1 : count, :]
    last_ref[...] = normed[count - 1 : count, :]
    mixed = [(before + step * vector_ref[2 + n : 3 + n, :]).astype(BF16) for n in range(3)]
    for n in range(3):
        mix_ref[n, :, :] = mixed[n]
    project_and_scan(
        mixed, (wk_ref[...], wv_ref[...], wr_ref[...]), channel_ref,
        gated_ref, save_ref, start_ref, final_ref, k_ref, carry, work,
    )


def second_kernel(
    meta, mix_ref, one_ref, two_ref, three_ref, four_ref, channel_ref,
    weight_ref, wo_ref, gated_ref, save_ref, start_ref, final_ref, k_ref, carry, work,
):
    @pl.when(pl.program_id(0) == 0)
    def _():
        pieces = (one_ref, two_ref, three_ref, four_ref)
        put_quarters(meta, weight_ref, [piece.at[0:3] for piece in pieces])
        rows, half = wo_ref.shape[0] // 4, weight_ref.shape[2]
        for n in range(2):
            put_quarters(
                meta, wo_ref.at[:, n * half : (n + 1) * half],
                [piece.at[3, n * rows : (n + 1) * rows, :] for piece in pieces],
            )

    project_and_scan(
        [mix_ref[n, :, :] for n in range(3)], [weight_ref[n, :, :] for n in range(3)], channel_ref,
        gated_ref, save_ref, start_ref, final_ref, k_ref, carry, work,
    )


def middle_kernel(
    meta, tokens_ref, own_ref, far_ref, wo_own_ref, wo_far_ref, vector_ref,
    middle_ref, mix_ref, bound_ref, last_ref, row,
):
    @pl.when(pl.program_id(0) == 0)
    def _():
        row[...] = vector_ref[4:5, :]

    middle = (
        nn(order_matrix(tokens_ref.shape[0]), tokens_ref[...])
        + nn(own_ref[...], wo_own_ref[...])
        + nn(far_ref[...], wo_far_ref[...])
    )
    middle_ref[...] = middle
    hat, _ = normalize(middle)
    normed = hat * vector_ref[0:1, :] + vector_ref[1:2, :]
    first = row[...]
    bound_ref[0, :, :] = jnp.broadcast_to(first, bound_ref.shape[1:])
    before = row_before(normed, first)
    step = normed - before
    count = normed.shape[0]
    row[...] = normed[count - 1 : count, :]
    last_ref[...] = normed[count - 1 : count, :]
    for n in range(2):
        mix_ref[n, :, :] = (before + step * vector_ref[2 + n : 3 + n, :]).astype(BF16)


def norm_backward(x, vectors, bound, grads, weights, row, sums_ref):
    gain, bias = vectors
    hat, scale = normalize(x)
    normed = hat * gain + bias
    step = normed - row_before(normed, bound)
    total = grads[0]
    current = grads[0] * weights[0]
    sums_ref[2:3, :] += row_sum(grads[0] * step)
    for n in range(1, len(grads)):
        total = total + grads[n]
        current = current + grads[n] * weights[n]
        sums_ref[2 + n : 3 + n, :] += row_sum(grads[n] * step)
    shifted = total - current
    flow = current + row_after(shifted, row[...])
    row[...] = shifted[0:1, :]
    sums_ref[0:1, :] += row_sum(flow * hat)
    sums_ref[1:2, :] += row_sum(flow)
    inner = flow * gain
    return scale * (inner - lane_mean(inner) - hat * lane_mean(inner * hat))


def channel_kernel(
    meta, cot_ref, middle_ref, mix_ref, bound_ref, vector_ref,
    ck_own_ref, cr_own_ref, one_ref, two_ref, three_ref, four_ref,
    cv_own_ref, cv_near_ref, cv_next_ref, cv_other_ref, cv_last_ref, wo_own_ref, wo_far_ref,
    mixed_ref, h_own_ref, h_far_ref, dp_own_ref, dp_far_ref, dval_ref, drec_own_ref, drec_far_ref,
    dmid_ref, datt_ref, dg_own_ref, dg_far_ref, sums_ref, row, ck_far_ref, cr_ref, cv_far_ref,
):
    @pl.when(pl.program_id(0) == 0)
    def _():
        row[...] = jnp.zeros_like(row)
        sums_ref[...] = jnp.zeros_like(sums_ref)
        units, half = ck_own_ref.shape[1], cr_own_ref.shape[1]
        pieces = (one_ref, two_ref, three_ref, four_ref)
        put_quarters(meta, ck_far_ref, [piece.at[:, :units] for piece in pieces])
        own_at = pl.ds(pl.multiple_of(meta[0] * half, 128), half)
        far_at = pl.ds(pl.multiple_of((1 - meta[0]) * half, 128), half)
        cr_ref[:, own_at] = cr_own_ref[...]
        put_quarters(meta, cr_ref.at[:, far_at], [piece.at[:, units:] for piece in pieces])
        put_halves(meta, cv_far_ref, (cv_near_ref, cv_next_ref), (cv_other_ref, cv_last_ref))

    key_in = mix_ref[0, :, :]
    relu_own = jnp.maximum(nn(key_in, ck_own_ref[...]), 0.0)
    hidden = (relu_own * relu_own).astype(BF16)
    h_own_ref[...] = hidden
    values = nn(hidden, cv_own_ref[...])
    relu_far = jnp.maximum(nn(key_in, ck_far_ref[...]), 0.0)
    hidden = (relu_far * relu_far).astype(BF16)
    h_far_ref[...] = hidden
    values = values + nn(hidden, cv_far_ref[...])
    gate = sigmoid(nn(mix_ref[1, :, :], cr_ref[...]))
    middle = middle_ref[...]
    count = middle.shape[0]
    mixed = (middle + gate * values).astype(BF16)
    mixed_ref[...] = nn(order_matrix(count, True), mixed).astype(BF16)
    grad = nn(order_matrix(count), cot_ref[...])
    passed = grad * gate
    d_values = passed.astype(BF16)
    dval_ref[...] = d_values
    d_rec = (passed * values * (1.0 - gate)).astype(BF16)
    low, high = d_rec[:, : drec_own_ref.shape[1]], d_rec[:, drec_own_ref.shape[1] :]
    drec_own_ref[...] = jnp.where(meta[0] == 0, low, high)
    drec_far_ref[...] = jnp.where(meta[0] == 0, high, low)
    d_pre = (2.0 * relu_own * nt(d_values, cv_own_ref[...])).astype(BF16)
    dp_own_ref[...] = d_pre
    d_key = nt(d_pre, ck_own_ref[...])
    d_pre = (2.0 * relu_far * nt(d_values, cv_far_ref[...])).astype(BF16)
    dp_far_ref[...] = d_pre
    d_key = d_key + nt(d_pre, ck_far_ref[...])
    d_recept = nt(d_rec, cr_ref[...])
    d_middle = grad + norm_backward(
        middle, (vector_ref[0:1, :], vector_ref[1:2, :]), bound_ref[0, 0:1, :],
        (d_key, d_recept), (vector_ref[2:3, :], vector_ref[3:4, :]), row, sums_ref,
    )
    dmid_ref[...] = d_middle
    d_att = d_middle.astype(BF16)
    datt_ref[...] = d_att
    dg_own_ref[...] = nt(d_att, wo_own_ref[...])
    dg_far_ref[...] = nt(d_att, wo_far_ref[...])


def scan_back_kernel(
    dg_ref, save_ref, start_ref, channel_ref, out_ref, sums_ref, dy_ref, dk_ref, dv_ref, carry, work
):
    chunks = start_ref.shape[1]

    @pl.when(pl.program_id(0) == 0)
    def _():
        carry[...] = jnp.zeros_like(carry)
        sums_ref[...] = jnp.zeros_like(sums_ref)

    gate = save_ref[2, :, :]
    dy = dg_ref[...] * gate
    dy_ref[...] = dy
    out_ref[2, :, :] = (dy * save_ref[1, :, :] * (1.0 - gate)).astype(BF16)

    def at(step):
        return slice(step * chunks, (step + 1) * chunks)

    gn = jnp.zeros((chunks, dy.shape[1]), F32)
    gd = jnp.zeros_like(gn)
    product = jnp.ones_like(gn)
    for step in reversed(range(STEP)):
        part = save_ref[3, at(step), :] * dy_ref[at(step), :]
        keep = save_ref[5, at(step), :]
        gn = part + keep * gn
        gd = keep * gd - part * save_ref[1, at(step), :]
        product = product * keep
    work[0, 0:chunks, :] = gn
    work[1, 0:chunks, :] = gd
    work[2, 0:chunks, :] = product
    gn = carry[0:1, :]
    gd = carry[1:2, :]
    for chunk in reversed(range(chunks)):
        row = slice(chunk, chunk + 1)
        work[3, row, :] = gn
        work[4, row, :] = gd
        gn = work[0, row, :] + work[2, row, :] * gn
        gd = work[1, row, :] + work[2, row, :] * gd
    carry[0:1, :] = gn
    carry[1:2, :] = gd
    work[0, 0:chunks, :] = start_ref[0, :, :]
    work[1, 0:chunks, :] = start_ref[1, :, :]
    work[0, chunks : chunks + 1, :] = carry[2:3, :]
    work[1, chunks : chunks + 1, :] = carry[3:4, :]
    carry[2:3, :] = start_ref[0, 0:1, :]
    carry[3:4, :] = start_ref[1, 0:1, :]
    gn = work[3, 0:chunks, :]
    gd = work[4, 0:chunks, :]
    decay = STEP * (gn * work[0, 1 : chunks + 1, :] + gd * work[1, 1 : chunks + 1, :])
    first = jnp.zeros_like(gn)
    for step in reversed(range(STEP)):
        place = at(step)
        dy = dy_ref[place, :]
        value = save_ref[0, place, :]
        wkv = save_ref[1, place, :]
        share = save_ref[4, place, :] * dy
        bonus = share * (value - wkv)
        fresh = save_ref[6, place, :]
        through = fresh * (gn * value + gd)
        d_key = bonus + through
        dk_ref[place, :] = d_key
        dv_ref[place, :] = share + fresh * gn
        first = first + bonus
        decay = decay - through - float(step) * d_key
        part = save_ref[3, place, :] * dy
        keep = save_ref[5, place, :]
        gn = part + keep * gn
        gd = keep * gd - part * wkv
    sums_ref[0:1, :] -= row_sum(decay) * jnp.exp(channel_ref[0:1, :])
    sums_ref[1:2, :] += row_sum(first)
    out_ref[0, :, :] = dk_ref[...].astype(BF16)
    out_ref[1, :, :] = dv_ref[...].astype(BF16)


def last_kernel(
    meta, tokens_ref, dmid_ref, own_ref, far_ref, wk_ref, wv_ref, wr_ref, weight_ref, bound_ref,
    vector_ref, grad_ref, sums_ref, row,
):
    @pl.when(pl.program_id(0) == 0)
    def _():
        row[...] = jnp.zeros_like(row)
        sums_ref[...] = jnp.zeros_like(sums_ref)

    grads = [
        nt(own_ref[n, :, :], w_ref[...]) + nt(far_ref[n, :, :], weight_ref[n, :, :])
        for n, w_ref in enumerate((wk_ref, wv_ref, wr_ref))
    ]
    part = norm_backward(
        nn(order_matrix(tokens_ref.shape[0]), tokens_ref[...]), (vector_ref[0:1, :], vector_ref[1:2, :]), bound_ref[0, 0:1, :],
        grads, [vector_ref[2 + n : 3 + n, :] for n in range(3)], row, sums_ref,
    )
    grad = (dmid_ref[...] + part).astype(BF16)
    grad_ref[...] = nn(order_matrix(grad.shape[0], True), grad).astype(BF16)


def weight_gradient_kernel(order, groups, meta, *refs):
    *refs, send_ref, keep_ref, turned, placed = refs
    count = len(refs) // 3
    lefts, fars, owns = refs[:count], refs[count : 2 * count], refs[2 * count :]
    at, side, tile = (pl.program_id(n) for n in range(3))
    whole = turned.shape[0]

    def turn(left_ref):
        for col in range(0, whole, 128):
            turned[col : col + 128, :] = left_ref[:, col : col + 128].T
        if groups > 1:
            rows = whole // groups
            for spot, other in enumerate(order):
                start = pl.multiple_of((meta[1] ^ other) * rows, rows)
                placed[spot * rows : (spot + 1) * rows, :] = turned[pl.ds(start, rows), :]

    source = placed if groups > 1 else turned

    def product(right_ref):
        part = nn(source[...], right_ref[...]).astype(BF16)
        keep_ref[0, :, :] = part[: whole // 2, :]
        send_ref[0, :, :] = part[whole // 2 :, :]

    for index in range(count):
        pl.when((at == index) & (side == 0) & (tile == 0))(functools.partial(turn, lefts[index]))
        pl.when((at == index) & (side == 0))(functools.partial(product, fars[index]))
        pl.when((at == index) & (side == 1))(functools.partial(product, owns[index]))


def params(mib, steps=None):
    return pltpu.CompilerParams(vmem_limit_bytes=mib * MIB, dimension_semantics=steps)


def whole(shape):
    return pl.BlockSpec(shape, lambda *_: (0,) * len(shape), pipeline_mode=pl.Buffered(1))


def weight_gradient(order, groups, meta, tasks, tile, name):
    lefts, fars, owns = zip(*tasks)
    length, width = lefts[0][0].shape[-2:]
    wide = fars[0][0].shape[-1]
    tiles = wide // tile
    count = len(tasks)

    def spec(item, columns, index):
        array, lead = item
        if lead is None:
            return pl.BlockSpec((length, columns), lambda *ids: (0, index(*ids[:3])))
        return pl.BlockSpec((None, length, columns), lambda *ids: (lead, 0, index(*ids[:3])))

    def far_tile(task):
        def index(at, side, n):
            now = jnp.where(side == 0, n, tiles - 1)
            return jnp.where(at == task, now, jnp.where(at < task, 0, tiles - 1))
        return index

    def own_tile(task):
        def index(at, side, n):
            now = jnp.where(side == 1, n, 0)
            return jnp.where(at == task, now, jnp.where(at < task, 0, tiles - 1))
        return index

    half_spec = pl.BlockSpec((1, width // 2, tile), lambda at, side, n, meta: (side, 0, at * tiles + n))
    half_shape = jax.ShapeDtypeStruct((2, width // 2, count * wide), BF16)
    return pl.pallas_call(
        functools.partial(weight_gradient_kernel, order, groups),
        grid_spec=pltpu.PrefetchScalarGridSpec(
            num_scalar_prefetch=1,
            grid=(count, 2, tiles),
            in_specs=[spec(item, width, lambda *_: 0) for item in lefts]
            + [spec(item, tile, far_tile(n)) for n, item in enumerate(fars)]
            + [spec(item, tile, own_tile(n)) for n, item in enumerate(owns)],
            out_specs=[half_spec, half_spec],
            scratch_shapes=[pltpu.VMEM((width, length), BF16), pltpu.VMEM((width, length), BF16)],
        ),
        out_shape=[half_shape, half_shape],
        compiler_params=params(48),
        cost_estimate=pl.CostEstimate(
            flops=4 * count * length * width * wide, bytes_accessed=8 * count * length * width, transcendentals=0
        ),
        name=name,
    )(meta, *[item[0] for item in lefts + fars + owns])


def together(*trees):
    return lax.optimization_barrier(trees)


def swapped(array):
    return lax.ppermute(array, "tensor", [(0, 1), (1, 0)])


def crossed(array, size, bit):
    return lax.ppermute(array, "dp", [(n, n ^ bit) for n in range(size)])


def added(mine, theirs, kind):
    return (mine.astype(F32) + theirs.astype(F32)).astype(kind)


def part_of(array, part, parts, axis=0):
    rows = array.shape[axis] // parts
    return lax.dynamic_slice_in_dim(array, part * rows, rows, axis)


def halving_steps(size, steps):
    steps = [bit for bit in steps if bit < size]
    known = max(steps)
    while known * 2 < size:
        known *= 2
        steps.append(known)
    return steps


def halving_order(size, steps):
    order = []
    for spot in range(size):
        other = 0
        for bit in reversed([bit for bit in steps if bit]):
            other |= bit * (spot % 2)
            spot //= 2
        order.append(other)
    return order


class Halving:
    def __init__(self, send, keep, size, steps, groups):
        self.size, self.steps, self.groups = size, steps if groups > 1 else [], groups
        self.send, self.keep = (send, keep) if groups > 1 else (None, jnp.concatenate([keep, send], axis=1))

    def exchange(self):
        if not self.steps:
            return jnp.zeros((8, 128), F32)
        bit = self.steps[0]
        return crossed(self.send, self.size, bit) if bit else swapped(self.send)

    def add(self, got):
        if not self.steps:
            return
        self.steps = self.steps[1:]
        total = added(self.keep, got, BF16 if self.steps else F32)
        if not self.steps:
            self.keep, self.send = total, None
        elif self.steps[0] == 0:
            self.send, self.keep = total[0], total[1]
        else:
            axis = total.ndim - 2
            half = total.shape[axis] // 2
            self.keep = lax.slice_in_dim(total, 0, half, axis=axis)
            self.send = lax.slice_in_dim(total, half, 2 * half, axis=axis)

    def result(self):
        if self.groups == 1:
            total = self.keep[1].astype(F32) + swapped(self.keep[0]).astype(F32)
            return lax.psum_scatter(total, "dp", scatter_dimension=0, tiled=True)
        assert not self.steps
        return self.keep


def shards(
    size, tokens, cotangent, prev_att, prev_ffn, numerator_state, denominator_state, exponent_offset_state,
    ln1_gain, ln1_bias, ln2_gain, ln2_bias, mix_key, mix_value, mix_recept, mix2_key, mix2_recept,
    time_decay, time_first, key_weight, value_weight, receptance_weight, output_weight,
    channel_key_weight, channel_receptance_weight, channel_value_weight,
):
    _, length, width = tokens.shape
    half = key_weight.shape[1]
    units = channel_key_weight.shape[1]
    block = min(256, length)
    blocks = length // block
    chunks = block // STEP
    side = lax.axis_index("tensor")
    place = lax.axis_index("dp")
    core = place % 2
    meta = jnp.stack([side, place]).astype(jnp.int32)
    rows = width // size
    groups = size if rows % 16 == 0 else 1
    def mine(array):
        return lax.dynamic_index_in_dim(array, side, 0, keepdims=False)

    def theirs(array):
        return lax.dynamic_index_in_dim(array, 1 - side, 0, keepdims=False)

    states = (numerator_state, denominator_state, exponent_offset_state)
    empty = jnp.zeros((half,), F32)
    own_channels = jnp.stack([time_decay, time_first] + [mine(item) for item in states] + [empty] * 3)
    sent_channels = jnp.stack([time_decay, time_first] + [theirs(item) for item in states] + [empty] * 3)
    blank = jnp.zeros((width,), F32)
    vectors1 = jnp.stack([ln1_gain, ln1_bias, mix_key, mix_value, mix_recept, mine(prev_att), blank, blank])
    vectors2 = jnp.stack([ln2_gain, ln2_bias, mix2_key, mix2_recept, mine(prev_ffn), blank, blank, blank])

    quarter = 2 * core + (place // 2) % 2
    projections = jnp.stack(
        [part_of(item, quarter, 4) for item in (key_weight, value_weight, receptance_weight)]
        + [part_of(output_weight, quarter, 4).reshape(-1, 2, half).swapaxes(0, 1).reshape(-1, half)]
    )
    ckr_part = jnp.concatenate(
        [part_of(item, quarter, 4) for item in (channel_key_weight, channel_receptance_weight)], axis=1
    )
    cut = units // 2 * 5 // 8
    cv_part = part_of(channel_value_weight, core, 2)
    cv_parts = cv_part[:cut], cv_part[cut:]

    def segment_spec(index=lambda i: i):
        return pl.BlockSpec((None, block, width), lambda i, meta: (meta[0], index(i), 0))

    def rows_spec(columns, index=lambda i: i):
        return pl.BlockSpec((block, columns), lambda i, *_: (index(i), 0))

    def stack_spec(count, columns, index=lambda i: i, size_of=block):
        return pl.BlockSpec((count, size_of, columns), lambda i, *_: (0, index(i), 0))

    def bound_spec(index=lambda i: i):
        return pl.BlockSpec((1, 8, width), lambda i, *_: (index(i), 0, 0))

    def back(i):
        return blocks - 1 - i

    def shape(dims, kind):
        return jax.ShapeDtypeStruct(dims, kind)

    scan_shapes = [
        shape((length, half), BF16), shape((7, length, half), F32),
        shape((2, length // STEP, half), F32), shape((8, half), F32),
    ]
    scan_specs = [rows_spec(half), stack_spec(7, half), stack_spec(2, half, size_of=chunks), whole((8, half))]
    scan_scratch = [
        pltpu.VMEM((block, half), F32), pltpu.VMEM((8, half), F32), pltpu.VMEM((4, chunks + 8, half), F32),
    ]
    mix1, bounds1, last_att, gated_own, save_own, start_own, final_own = pl.pallas_call(
        first_kernel,
        grid_spec=pltpu.PrefetchScalarGridSpec(
            num_scalar_prefetch=1,
            grid=(blocks,),
            in_specs=[segment_spec(), whole((8, width))] + [whole((width, half))] * 3 + [whole((8, half))],
            out_specs=[stack_spec(3, width), bound_spec(), whole((1, width))] + scan_specs,
            scratch_shapes=scan_scratch + [pltpu.VMEM((1, width), F32)],
        ),
        out_shape=[
            shape((3, length, width), BF16), shape((blocks, 8, width), F32), shape((1, width), F32),
        ] + scan_shapes,
        compiler_params=params(48),
        name="time_mix_own",
    )(meta, tokens, vectors1, key_weight, value_weight, receptance_weight, own_channels)

    proj_one, far_channels, mix1, ckr_part, cv_parts = together(
        swapped(projections), swapped(sent_channels), mix1, ckr_part, cv_parts
    )
    proj_two, proj_three, ckr_one, cv_parts = together(
        crossed(proj_one, size, 2), crossed(proj_one, size, 1), swapped(ckr_part), cv_parts
    )
    proj_four, ckr_three, ckr_one, mix1, cv_parts = together(
        crossed(proj_two, size, 1), crossed(ckr_one, size, 1), ckr_one, mix1, cv_parts
    )
    ckr_two = crossed(ckr_one, size, 2)
    cv_near = swapped(cv_parts[0])
    far_kvr, wo_far, gated_far, save_far, start_far, final_far = pl.pallas_call(
        second_kernel,
        grid_spec=pltpu.PrefetchScalarGridSpec(
            num_scalar_prefetch=1,
            grid=(blocks,),
            in_specs=[stack_spec(3, width)] + [whole((4, width // 4, half))] * 4 + [whole((8, half))],
            out_specs=[whole((3, width, half)), whole((half, width))] + scan_specs,
            scratch_shapes=scan_scratch,
        ),
        out_shape=[shape((3, width, half), BF16), shape((half, width), BF16)] + scan_shapes,
        compiler_params=params(48),
        name="time_mix_far",
    )(meta, mix1, proj_one, proj_two, proj_three, proj_four, far_channels)

    middle, mix2, bounds2, last_ffn = pl.pallas_call(
        middle_kernel,
        grid_spec=pltpu.PrefetchScalarGridSpec(
            num_scalar_prefetch=1,
            grid=(blocks,),
            in_specs=[segment_spec(), rows_spec(half), rows_spec(half)]
            + [whole((half, width))] * 2 + [whole((8, width))],
            out_specs=[rows_spec(width), stack_spec(2, width), bound_spec(), whole((1, width))],
            scratch_shapes=[pltpu.VMEM((1, width), F32)],
        ),
        out_shape=[
            shape((length, width), F32), shape((2, length, width), BF16),
            shape((blocks, 8, width), F32), shape((1, width), F32),
        ],
        compiler_params=params(48),
        name="middle",
    )(meta, tokens, gated_own, gated_far, output_weight, wo_far, vectors2)
    ckr_two, cv_near, mix2, cv_rest = together(ckr_two, cv_near, mix2, cv_parts[1])
    ckr_four, cv_next, cv_other = together(crossed(ckr_two, size, 1), swapped(cv_rest), crossed(cv_near, size, 1))
    cv_last = crossed(cv_next, size, 1)

    (
        mixed, h_own, h_far, dpre_own, dpre_far, d_values, rec_own, rec_far, d_middle, d_att, dg_own, dg_far, sums2,
    ) = pl.pallas_call(
        channel_kernel,
        grid_spec=pltpu.PrefetchScalarGridSpec(
            num_scalar_prefetch=1,
            grid=(blocks,),
            in_specs=[
                segment_spec(back), rows_spec(width, back), stack_spec(2, width, back), bound_spec(back),
                whole((8, width)), whole((width, units)), whole((width, half)),
            ] + [whole((width // 4, units + half))] * 4 + [
                whole((units, width)), whole((cut, width)), whole((units // 2 - cut, width)),
                whole((cut, width)), whole((units // 2 - cut, width)),
                whole((half, width)), whole((half, width)),
            ],
            out_specs=[
                rows_spec(width, back), rows_spec(units, back), rows_spec(units, back),
                rows_spec(units, back), rows_spec(units, back), rows_spec(width, back),
                rows_spec(half, back), rows_spec(half, back), rows_spec(width, back), rows_spec(width, back),
                rows_spec(half, back), rows_spec(half, back), whole((8, width)),
            ],
            scratch_shapes=[
                pltpu.VMEM((1, width), F32), pltpu.VMEM((width, units), BF16),
                pltpu.VMEM((width, width), BF16), pltpu.VMEM((units, width), BF16),
            ],
        ),
        out_shape=[
            shape((length, width), BF16), shape((length, units), BF16), shape((length, units), BF16),
            shape((length, units), BF16), shape((length, units), BF16), shape((length, width), BF16),
            shape((length, half), BF16), shape((length, half), BF16),
            shape((length, width), F32), shape((length, width), BF16),
            shape((length, half), F32), shape((length, half), F32), shape((8, width), F32),
        ],
        compiler_params=params(60),
        name="channel_mix",
    )(
        meta, cotangent, middle, mix2, bounds2, vectors2, channel_key_weight, channel_receptance_weight,
        ckr_one, ckr_two, ckr_three, ckr_four, channel_value_weight, cv_near, cv_next, cv_other, cv_last,
        output_weight, wo_far,
    )

    def gradients(steps, tasks, tile, name):
        steps = halving_steps(size, steps)
        send, keep = weight_gradient(halving_order(size, steps), groups, meta, tasks, tile, name)
        return Halving(send, keep, size, steps, groups)

    def halves(array, axis):
        own = lax.dynamic_slice_in_dim(array, side * half, half, axis)
        far = lax.dynamic_slice_in_dim(array, (1 - side) * half, half, axis)
        return own, far

    def scan_back(grads, saved, starts, channels):
        return pl.pallas_call(
            scan_back_kernel,
            grid=(blocks,),
            in_specs=[
                rows_spec(half, back), stack_spec(7, half, back),
                stack_spec(2, half, back, size_of=chunks), whole((8, half)),
            ],
            out_specs=[stack_spec(3, half, back), whole((8, half))],
            out_shape=[shape((3, length, half), BF16), shape((8, half), F32)],
            scratch_shapes=[pltpu.VMEM((block, half), F32)] * 3
            + [pltpu.VMEM((8, half), F32), pltpu.VMEM((5, chunks + 8, half), F32)],
            compiler_params=params(48),
            name="scan_back",
        )(grads, saved, starts, channels)

    mixed_own, mixed_far = halves(mixed, 1)
    a_sum = gradients(
        (1, 0, 2, 4, 8), [((mix2, 0), (dpre_far, None), (dpre_own, None))], 512, "channel_key_gradient"
    )
    d_values, a_sum.send, a_sum.keep = together(d_values, a_sum.send, a_sum.keep)
    b_sum = gradients(
        (1, 2, 4, 8, 0), [((d_values, None), (h_far, None), (h_own, None))], 512, "channel_value_gradient"
    )
    d_att, b_sum.send, b_sum.keep = together(d_att, b_sum.send, b_sum.keep)
    c_sum = gradients(
        (1, 4, 8, 2, 0),
        [((d_att, None), (gated_far, None), (gated_own, None)), ((mix2, 1), (rec_far, None), (rec_own, None))],
        half, "output_gradient",
    )
    got_a, got_b, mixed_in, c_sum.send, c_sum.keep, dg_far, dg_own = together(
        a_sum.exchange(), b_sum.exchange(), swapped(mixed_far), c_sum.send, c_sum.keep, dg_far, dg_own
    )
    a_sum.add(got_a)
    b_sum.add(got_b)
    d_far, channel_sums_far = scan_back(dg_far, save_far, start_far, far_channels)
    got_c, d_far, dg_own, a_sum.send, b_sum.send = together(
        c_sum.exchange(), d_far, dg_own, a_sum.send, b_sum.send
    )
    c_sum.add(got_c)
    d_own, channel_sums_own = scan_back(dg_own, save_own, start_own, own_channels)
    d_sum = gradients(
        (1, 2, 4, 8, 0), [((mix1, n), (d_far, n), (d_own, n)) for n in range(3)], half, "projection_gradient"
    )
    d_middle, d_sum.send, d_sum.keep = together(d_middle, d_sum.send, d_sum.keep)
    grad_part, sums1 = pl.pallas_call(
        last_kernel,
        grid_spec=pltpu.PrefetchScalarGridSpec(
            num_scalar_prefetch=1,
            grid=(blocks,),
            in_specs=[
                segment_spec(back), rows_spec(width, back), stack_spec(3, half, back), stack_spec(3, half, back),
                whole((width, half)), whole((width, half)), whole((width, half)), whole((3, width, half)),
                bound_spec(back), whole((8, width)),
            ],
            out_specs=[rows_spec(width, back), whole((8, width))],
            scratch_shapes=[pltpu.VMEM((1, width), F32)],
        ),
        out_shape=[shape((length, width), BF16), shape((8, width), F32)],
        compiler_params=params(48),
        name="time_mix_back",
    )(
        meta, tokens, d_middle, d_own, d_far, key_weight, value_weight, receptance_weight, far_kvr,
        bounds1, vectors1,
    )

    def both(own, far):
        return jnp.where(side == 0, jnp.stack([own, far]), jnp.stack([far, own]))

    def full(own, far):
        return jnp.where(side == 0, jnp.concatenate([own, far]), jnp.concatenate([far, own]))

    small = jnp.concatenate([
        sums1[0:2], sums2[0:2], sums1[2:5], sums2[2:4],
        jnp.stack([full(channel_sums_own[n], channel_sums_far[n]) for n in range(2)]),
    ])
    sums = [a_sum, b_sum, c_sum, d_sum]
    got_a, got_b, got_c, d_sum.send, grad_part, small = together(
        a_sum.exchange(), b_sum.exchange(), c_sum.exchange(), d_sum.send, grad_part, small
    )
    for item, got in zip(sums, (got_a, got_b, got_c)):
        item.add(got)
    first, second = grad_part[: length // 2], grad_part[length // 2 :]
    last_rows = jnp.concatenate([last_att, last_ffn])

    def round_of(extra, extra_keep, parts):
        gots, extra, extra_keep, keeps = together(
            [item.exchange() for item in parts], extra, extra_keep, [item.send for item in sums]
        )
        for item, keep in zip(sums, keeps):
            item.send = keep
        for item, got in zip(parts, gots):
            item.add(got)
        return extra, extra_keep

    def small_round(bit):
        return crossed(small, size, bit) if bit else swapped(small)

    (first_in, got), (second, last_rows, final_far) = round_of(
        (swapped(first), small_round(1)), (second, last_rows, final_far), sums
    )
    small = small + got
    (second_in, got), (last_rows, final_far) = round_of(
        (swapped(second), small_round(0)), (last_rows, final_far), sums
    )
    small = small + got
    (last_in, back_states, got), _ = round_of(
        (swapped(last_rows), swapped(final_far), small_round(2)), (), sums
    )
    small = small + got
    bit = 4
    while bit < size or d_sum.steps:
        got = small_round(bit) if bit < size else jnp.zeros_like(small)
        (got,), _ = round_of((got,), (), [item for item in sums if item.steps])
        small = small + got
        bit *= 2
    grad_tokens = both(grad_part, jnp.concatenate([first_in, second_in])).astype(F32)
    mixed_out = both(mixed_own, mixed_in)
    finals = [both(final_own[n], back_states[n]) for n in range(3)]
    last_rows = both(last_rows, last_in)
    g_ck, g_cv, g_other, g_kvr = (item.result() for item in sums)
    return (
        (mixed_out, grad_tokens, *finals, last_rows[:, 0], last_rows[:, 1])
        + tuple(small[n] for n in range(11))
        + tuple(g_kvr[:, n * half : (n + 1) * half] for n in range(3))
        + (g_other[:, :half].T, g_ck, g_other[:, half:], g_cv.T)
    )


def solution(mesh):
    split = P("dp", "tensor")
    turned = P("tensor", "dp")
    return jax.shard_map(
        functools.partial(shards, mesh.shape["dp"]),
        mesh=mesh,
        in_specs=(P("dp"), P("dp"), P("dp"), P("dp"), split, split, split)
        + (P(),) * 9
        + (P("tensor"), P("tensor"))
        + (P(None, "tensor"),) * 3
        + (P("tensor"), P(None, "tensor"), P(None, "tensor"), P("tensor")),
        out_specs=(P("dp", None, "tensor"), P("dp"), split, split, split, P("dp"), P("dp"))
        + (P(),) * 11
        + (split, split, split, turned, split, split, turned),
        check_vma=False,
    )
```

```python
import functools

import jax
import jax.numpy as jnp
from jax import lax
from jax.experimental import pallas as pl
from jax.experimental.pallas import tpu as pltpu
from jax.sharding import PartitionSpec as P

F32 = jnp.float32
BF16 = jnp.bfloat16
STEP = 8
MIB = 1 << 20
TILE = 768


def nn(left, right):
    return jnp.dot(left, right, preferred_element_type=F32)


def nt(left, right):
    return lax.dot_general(left, right, (((1,), (1,)), ((), ())), preferred_element_type=F32)


def sigmoid(x):
    return 1.0 / (1.0 + jnp.exp(-x))


def row_sum(x):
    return jnp.sum(x, axis=0, keepdims=True)


def lane_mean(x):
    return jnp.mean(x, axis=-1, keepdims=True)


def normalize(x):
    center = x - lane_mean(x)
    scale = lax.rsqrt(lane_mean(center * center) + 1e-05)
    return center * scale, scale


def order_matrix(count, turned=False):
    chunks = count // STEP
    row = lax.broadcasted_iota(jnp.int32, (count, count), 1 if turned else 0)
    token = lax.broadcasted_iota(jnp.int32, (count, count), 0 if turned else 1)
    return (token == (row % chunks) * STEP + row // chunks).astype(BF16)


def row_before(x, first):
    chunks = x.shape[0] // STEP
    ends = x[-chunks:, :]
    rows = lax.broadcasted_iota(jnp.int32, ends.shape, 0)
    head = jnp.where(rows == 0, first, pltpu.roll(ends, 1, 0))
    return jnp.concatenate([head, x[:-chunks, :]])


def row_after(x, last):
    chunks = x.shape[0] // STEP
    starts = x[:chunks, :]
    rows = lax.broadcasted_iota(jnp.int32, starts.shape, 0)
    tail = jnp.where(rows == chunks - 1, last, pltpu.roll(starts, chunks - 1, 0))
    return jnp.concatenate([x[chunks:, :], tail])


def put_quarters(meta, target, pieces):
    core, side = meta[1] % 2, (meta[1] // 2) % 2
    rows = target.shape[-2] // 4
    spots = (2 * core + side, 2 * core + 1 - side, 2 - 2 * core + side, 3 - 2 * core - side)
    for spot, piece in zip(spots, pieces):
        at = pl.ds(pl.multiple_of(spot * rows, rows), rows)
        if len(target.shape) == 3:
            target[:, at, :] = piece[...]
        else:
            target[at, :] = piece[...]


def put_halves(meta, target, mine, other):
    core = meta[1] % 2
    half = target.shape[0] // 2
    for start, pieces in ((core * half, mine), ((1 - core) * half, other)):
        for piece in pieces:
            rows = piece.shape[0]
            target[pl.ds(pl.multiple_of(start, 16), rows), :] = piece[...]
            start = start + rows


def wkv_forward(segment, first_block, k_ref, channel_ref, save_ref, start_ref, final_ref, carry, work):
    chunks = start_ref.shape[1]
    rate = jnp.exp(channel_ref[0:1, :])
    boost = channel_ref[1:2, :]

    @pl.when(first_block)
    def _():
        for n in range(3):
            carry[n : n + 1, :] = channel_ref[pl.ds(2 + 2 * n + segment, 1), :]

    def keys(step):
        return k_ref[step * chunks : (step + 1) * chunks, :]

    peak = keys(STEP - 1)
    for step in range(STEP - 1):
        peak = jnp.maximum(peak, keys(step) - (STEP - 1.0 - step) * rate)
    number = jnp.zeros_like(peak)
    weight = jnp.zeros_like(peak)
    for step in range(STEP):
        part = jnp.exp(keys(step) - (STEP - 1.0 - step) * rate - peak)
        number = number + part * save_ref[0, step * chunks : (step + 1) * chunks, :]
        weight = weight + part
    work[0, 0:chunks, :] = peak
    top = carry[2:3, :]
    for chunk in range(chunks):
        work[1, chunk : chunk + 1, :] = top
        top = jnp.maximum(top - STEP * rate, work[0, chunk : chunk + 1, :])
    work[1, chunks : chunks + 1, :] = top
    tops = work[1, 0:chunks, :]
    later = work[1, 1 : chunks + 1, :]
    fresh = jnp.exp(peak - later)
    work[0, 0:chunks, :] = jnp.exp(tops - STEP * rate - later)
    work[2, 0:chunks, :] = fresh * number
    work[3, 0:chunks, :] = fresh * weight
    num = carry[0:1, :]
    den = carry[1:2, :]
    for chunk in range(chunks):
        at = slice(chunk, chunk + 1)
        start_ref[0, at, :] = num
        start_ref[1, at, :] = den
        num = work[0, at, :] * num + work[2, at, :]
        den = work[0, at, :] * den + work[3, at, :]
    carry[0:1, :] = num
    carry[1:2, :] = den
    carry[2:3, :] = top
    final_ref[0:3, :] = carry[0:3, :]

    num = start_ref[0, :, :]
    den = start_ref[1, :, :]
    top = tops
    for step in range(STEP):
        at = slice(step * chunks, (step + 1) * chunks)
        key = keys(step)
        value = save_ref[0, at, :]
        gap = top - (boost + key)
        small = jnp.exp(-jnp.abs(gap))
        state_wins = gap > 0
        old = jnp.where(state_wins, 1.0, small)
        now = jnp.where(state_wins, small, 1.0)
        inverse = 1.0 / (old * den + now)
        old = old * inverse
        now = now * inverse
        save_ref[1, at, :] = old * num + now * value
        save_ref[3, at, :] = old
        save_ref[4, at, :] = now
        faded = top - rate
        gap = faded - key
        small = jnp.exp(-jnp.abs(gap))
        state_wins = gap > 0
        keep = jnp.where(state_wins, 1.0, small)
        fresh = jnp.where(state_wins, small, 1.0)
        save_ref[5, at, :] = keep
        save_ref[6, at, :] = fresh
        num = keep * num + fresh * value
        den = keep * den + fresh
        top = jnp.maximum(faded, key)


def project_and_scan(segment, inputs, weights, channel_ref, gated_ref, save_ref, start_ref, final_ref, k_ref, carry, work):
    k_ref[...] = nn(inputs[0], weights[0])
    save_ref[0, :, :] = nn(inputs[1], weights[1])
    gate = sigmoid(nn(inputs[2], weights[2]))
    save_ref[2, :, :] = gate
    wkv_forward(segment, pl.program_id(0) == 0, k_ref, channel_ref, save_ref, start_ref, final_ref, carry, work)
    gated_ref[...] = (gate * save_ref[1, :, :]).astype(BF16)


def first_kernel(
    meta, tokens_ref, vector_ref, wk_ref, wv_ref, wr_ref, channel_ref,
    mix_ref, bound_ref, last_ref, gated_ref, save_ref, start_ref, final_ref,
    k_ref, carry, work, row,
):
    @pl.when(pl.program_id(0) == 0)
    def _():
        row[...] = vector_ref[pl.ds(9 + meta[0], 1), :]

    tokens = nn(order_matrix(tokens_ref.shape[0]), tokens_ref[...])
    hat, _ = normalize(tokens)
    normed = hat * vector_ref[0:1, :] + vector_ref[1:2, :]
    first = row[...]
    bound_ref[0, :, :] = jnp.broadcast_to(first, bound_ref.shape[1:])
    before = row_before(normed, first)
    step = normed - before
    count = normed.shape[0]
    row[...] = normed[count - 1 : count, :]
    last_ref[...] = normed[count - 1 : count, :]
    mixed = [(before + step * vector_ref[2 + n : 3 + n, :]).astype(BF16) for n in range(3)]
    for n in range(3):
        mix_ref[n, :, :] = mixed[n]
    project_and_scan(
        meta[0], mixed, (wk_ref[...], wv_ref[...], wr_ref[...]), channel_ref,
        gated_ref, save_ref, start_ref, final_ref, k_ref, carry, work,
    )


def second_kernel(
    meta, mix_ref, one_ref, two_ref, three_ref, four_ref, channel_ref,
    weight_ref, wo_ref, gated_ref, save_ref, start_ref, final_ref, k_ref, carry, work,
):
    @pl.when(pl.program_id(0) == 0)
    def _():
        pieces = (one_ref, two_ref, three_ref, four_ref)
        put_quarters(meta, weight_ref, [piece.at[0:3] for piece in pieces])
        rows, half = wo_ref.shape[0] // 4, weight_ref.shape[2]
        for n in range(2):
            put_quarters(
                meta, wo_ref.at[:, n * half : (n + 1) * half],
                [piece.at[3, n * rows : (n + 1) * rows, :] for piece in pieces],
            )

    project_and_scan(
        meta[0], [mix_ref[n, :, :] for n in range(3)], [weight_ref[n, :, :] for n in range(3)], channel_ref,
        gated_ref, save_ref, start_ref, final_ref, k_ref, carry, work,
    )


def middle_kernel(
    meta, tokens_ref, own_ref, far_ref, wo_own_ref, wo_far_ref, vector_ref,
    middle_ref, mix_ref, bound_ref, last_ref, row,
):
    @pl.when(pl.program_id(0) == 0)
    def _():
        row[...] = vector_ref[pl.ds(11 + meta[0], 1), :]

    middle = (
        nn(order_matrix(tokens_ref.shape[0]), tokens_ref[...])
        + nn(own_ref[...], wo_own_ref[...])
        + nn(far_ref[...], wo_far_ref[...])
    )
    middle_ref[...] = middle
    hat, _ = normalize(middle)
    normed = hat * vector_ref[5:6, :] + vector_ref[6:7, :]
    first = row[...]
    bound_ref[0, :, :] = jnp.broadcast_to(first, bound_ref.shape[1:])
    before = row_before(normed, first)
    step = normed - before
    count = normed.shape[0]
    row[...] = normed[count - 1 : count, :]
    last_ref[...] = normed[count - 1 : count, :]
    for n in range(2):
        mix_ref[n, :, :] = (before + step * vector_ref[7 + n : 8 + n, :]).astype(BF16)


def norm_backward(x, vectors, bound, grads, weights, row, sums_ref):
    gain, bias = vectors
    hat, scale = normalize(x)
    normed = hat * gain + bias
    step = normed - row_before(normed, bound)
    total = grads[0]
    current = grads[0] * weights[0]
    sums_ref[2:3, :] += row_sum(grads[0] * step)
    for n in range(1, len(grads)):
        total = total + grads[n]
        current = current + grads[n] * weights[n]
        sums_ref[2 + n : 3 + n, :] += row_sum(grads[n] * step)
    shifted = total - current
    flow = current + row_after(shifted, row[...])
    row[...] = shifted[0:1, :]
    sums_ref[0:1, :] += row_sum(flow * hat)
    sums_ref[1:2, :] += row_sum(flow)
    inner = flow * gain
    return scale * (inner - lane_mean(inner) - hat * lane_mean(inner * hat))


def channel_kernel(
    meta, cot_ref, middle_ref, mix_ref, bound_ref, vector_ref,
    ck_own_ref, cr_own_ref, one_ref, two_ref, three_ref, four_ref,
    cv_own_ref, cv_near_ref, cv_next_ref, cv_other_ref, cv_last_ref, wo_own_ref, wo_far_ref,
    mixed_own_ref, mixed_far_ref, h_own_ref, h_far_ref, dp_own_ref, dp_far_ref, dval_ref, drec_own_ref, drec_far_ref,
    dmid_ref, datt_ref, dg_own_ref, dg_far_ref, sums_ref, row, ck_far_ref, cr_ref, cv_far_ref,
):
    @pl.when(pl.program_id(0) == 0)
    def _():
        row[...] = jnp.zeros_like(row)
        sums_ref[...] = jnp.zeros_like(sums_ref)
        units, half = ck_own_ref.shape[1], cr_own_ref.shape[1]
        pieces = (one_ref, two_ref, three_ref, four_ref)
        put_quarters(meta, ck_far_ref, [piece.at[:, :units] for piece in pieces])
        own_at = pl.ds(pl.multiple_of(meta[0] * half, 128), half)
        far_at = pl.ds(pl.multiple_of((1 - meta[0]) * half, 128), half)
        cr_ref[:, own_at] = cr_own_ref[...]
        put_quarters(meta, cr_ref.at[:, far_at], [piece.at[:, units:] for piece in pieces])
        put_halves(meta, cv_far_ref, (cv_near_ref, cv_next_ref), (cv_other_ref, cv_last_ref))

    key_in = mix_ref[0, :, :]
    relu_own = jnp.maximum(nn(key_in, ck_own_ref[...]), 0.0)
    hidden = (relu_own * relu_own).astype(BF16)
    h_own_ref[...] = hidden
    values = nn(hidden, cv_own_ref[...])
    relu_far = jnp.maximum(nn(key_in, ck_far_ref[...]), 0.0)
    hidden = (relu_far * relu_far).astype(BF16)
    h_far_ref[...] = hidden
    values = values + nn(hidden, cv_far_ref[...])
    gate = sigmoid(nn(mix_ref[1, :, :], cr_ref[...]))
    middle = middle_ref[...]
    count = middle.shape[0]
    mixed = (middle + gate * values).astype(BF16)
    mixed = nn(order_matrix(count, True), mixed)
    half = mixed_own_ref.shape[1]
    first, second = mixed[:, :half], mixed[:, half:]
    mixed_own_ref[...] = jnp.where(meta[0] == 0, first, second).astype(BF16)
    mixed_far_ref[...] = jnp.where(meta[0] == 0, second, first).astype(BF16)
    grad = nn(order_matrix(count), cot_ref[...])
    passed = grad * gate
    d_values = passed.astype(BF16)
    dval_ref[...] = d_values
    d_rec = (passed * values * (1.0 - gate)).astype(BF16)
    low, high = d_rec[:, : drec_own_ref.shape[1]], d_rec[:, drec_own_ref.shape[1] :]
    drec_own_ref[...] = jnp.where(meta[0] == 0, low, high)
    drec_far_ref[...] = jnp.where(meta[0] == 0, high, low)
    d_pre = (2.0 * relu_own * nt(d_values, cv_own_ref[...])).astype(BF16)
    dp_own_ref[...] = d_pre
    d_key = nt(d_pre, ck_own_ref[...])
    d_pre = (2.0 * relu_far * nt(d_values, cv_far_ref[...])).astype(BF16)
    dp_far_ref[...] = d_pre
    d_key = d_key + nt(d_pre, ck_far_ref[...])
    d_recept = nt(d_rec, cr_ref[...])
    d_middle = grad + norm_backward(
        middle, (vector_ref[5:6, :], vector_ref[6:7, :]), bound_ref[0, 0:1, :],
        (d_key, d_recept), (vector_ref[7:8, :], vector_ref[8:9, :]), row, sums_ref,
    )
    dmid_ref[...] = d_middle
    d_att = d_middle.astype(BF16)
    datt_ref[...] = d_att
    dg_own_ref[...] = nt(d_att, wo_own_ref[...])
    dg_far_ref[...] = nt(d_att, wo_far_ref[...])


def scan_back_kernel(
    dg_ref, save_ref, start_ref, channel_ref, out_ref, sums_ref, dy_ref, dk_ref, dv_ref, carry, work
):
    chunks = start_ref.shape[1]

    @pl.when(pl.program_id(0) == 0)
    def _():
        carry[...] = jnp.zeros_like(carry)
        sums_ref[...] = jnp.zeros_like(sums_ref)

    gate = save_ref[2, :, :]
    dy = dg_ref[...] * gate
    dy_ref[...] = dy
    out_ref[2, :, :] = (dy * save_ref[1, :, :] * (1.0 - gate)).astype(BF16)

    def at(step):
        return slice(step * chunks, (step + 1) * chunks)

    gn = jnp.zeros((chunks, dy.shape[1]), F32)
    gd = jnp.zeros_like(gn)
    product = jnp.ones_like(gn)
    for step in reversed(range(STEP)):
        part = save_ref[3, at(step), :] * dy_ref[at(step), :]
        keep = save_ref[5, at(step), :]
        gn = part + keep * gn
        gd = keep * gd - part * save_ref[1, at(step), :]
        product = product * keep
    work[0, 0:chunks, :] = gn
    work[1, 0:chunks, :] = gd
    work[2, 0:chunks, :] = product
    gn = carry[0:1, :]
    gd = carry[1:2, :]
    for chunk in reversed(range(chunks)):
        row = slice(chunk, chunk + 1)
        work[3, row, :] = gn
        work[4, row, :] = gd
        gn = work[0, row, :] + work[2, row, :] * gn
        gd = work[1, row, :] + work[2, row, :] * gd
    carry[0:1, :] = gn
    carry[1:2, :] = gd
    work[0, 0:chunks, :] = start_ref[0, :, :]
    work[1, 0:chunks, :] = start_ref[1, :, :]
    work[0, chunks : chunks + 1, :] = carry[2:3, :]
    work[1, chunks : chunks + 1, :] = carry[3:4, :]
    carry[2:3, :] = start_ref[0, 0:1, :]
    carry[3:4, :] = start_ref[1, 0:1, :]
    gn = work[3, 0:chunks, :]
    gd = work[4, 0:chunks, :]
    decay = STEP * (gn * work[0, 1 : chunks + 1, :] + gd * work[1, 1 : chunks + 1, :])
    first = jnp.zeros_like(gn)
    for step in reversed(range(STEP)):
        place = at(step)
        dy = dy_ref[place, :]
        value = save_ref[0, place, :]
        wkv = save_ref[1, place, :]
        share = save_ref[4, place, :] * dy
        bonus = share * (value - wkv)
        fresh = save_ref[6, place, :]
        through = fresh * (gn * value + gd)
        d_key = bonus + through
        dk_ref[place, :] = d_key
        dv_ref[place, :] = share + fresh * gn
        first = first + bonus
        decay = decay - through - float(step) * d_key
        part = save_ref[3, place, :] * dy
        keep = save_ref[5, place, :]
        gn = part + keep * gn
        gd = keep * gd - part * wkv
    sums_ref[0:1, :] -= row_sum(decay) * jnp.exp(channel_ref[0:1, :])
    sums_ref[1:2, :] += row_sum(first)
    out_ref[0, :, :] = dk_ref[...].astype(BF16)
    out_ref[1, :, :] = dv_ref[...].astype(BF16)


def last_kernel(
    meta, tokens_ref, dmid_ref, own_ref, far_ref, wk_ref, wv_ref, wr_ref, weight_ref, bound_ref,
    vector_ref, grad_ref, sums_ref, row,
):
    @pl.when(pl.program_id(0) == 0)
    def _():
        row[...] = jnp.zeros_like(row)
        sums_ref[...] = jnp.zeros_like(sums_ref)

    grads = [
        nt(own_ref[n, :, :], w_ref[...]) + nt(far_ref[n, :, :], weight_ref[n, :, :])
        for n, w_ref in enumerate((wk_ref, wv_ref, wr_ref))
    ]
    part = norm_backward(
        nn(order_matrix(tokens_ref.shape[0]), tokens_ref[...]), (vector_ref[0:1, :], vector_ref[1:2, :]), bound_ref[0, 0:1, :],
        grads, [vector_ref[2 + n : 3 + n, :] for n in range(3)], row, sums_ref,
    )
    grad = (dmid_ref[...] + part).astype(BF16)
    grad_ref[...] = nn(order_matrix(grad.shape[0], True), grad).astype(BF16)


def weight_gradient_kernel(order, groups, meta, *refs):
    *refs, send_ref, keep_ref, turned, placed = refs
    count = len(refs) // 3
    lefts, fars, owns = refs[:count], refs[count : 2 * count], refs[2 * count :]
    at, side, tile = (pl.program_id(n) for n in range(3))
    whole = turned.shape[0]

    def turn(left_ref):
        for col in range(0, whole, 128):
            turned[col : col + 128, :] = left_ref[:, col : col + 128].T
        if groups > 1:
            rows = whole // groups
            for spot, other in enumerate(order):
                start = pl.multiple_of((meta[1] ^ other) * rows, rows)
                placed[spot * rows : (spot + 1) * rows, :] = turned[pl.ds(start, rows), :]

    source = placed if groups > 1 else turned

    def product(right_ref):
        part = nn(source[...], right_ref[...]).astype(BF16)
        keep_ref[0, :, :] = part[: whole // 2, :]
        send_ref[0, :, :] = part[whole // 2 :, :]

    for index in range(count):
        pl.when((at == index) & (side == 0) & (tile == 0))(functools.partial(turn, lefts[index]))
        pl.when((at == index) & (side == 0))(functools.partial(product, fars[index]))
        pl.when((at == index) & (side == 1))(functools.partial(product, owns[index]))


def params(mib, steps=None):
    return pltpu.CompilerParams(vmem_limit_bytes=mib * MIB, dimension_semantics=steps)


def whole(shape):
    return pl.BlockSpec(shape, lambda *_: (0,) * len(shape), pipeline_mode=pl.Buffered(1))


def weight_gradient(order, groups, meta, tasks, tile, name):
    lefts, fars, owns = zip(*tasks)
    length, width = lefts[0][0].shape[-2:]
    wide = fars[0][0].shape[-1]
    tiles = wide // tile
    count = len(tasks)

    def spec(item, columns, index):
        array, lead = item
        if lead is None:
            return pl.BlockSpec((length, columns), lambda *ids: (0, index(*ids[:3])))
        return pl.BlockSpec((None, length, columns), lambda *ids: (lead, 0, index(*ids[:3])))

    def far_tile(task):
        def index(at, side, n):
            now = jnp.where(side == 0, n, tiles - 1)
            return jnp.where(at == task, now, jnp.where(at < task, 0, tiles - 1))
        return index

    def own_tile(task):
        def index(at, side, n):
            now = jnp.where(side == 1, n, 0)
            return jnp.where(at == task, now, jnp.where(at < task, 0, tiles - 1))
        return index

    half_spec = pl.BlockSpec((1, width // 2, tile), lambda at, side, n, meta: (side, 0, at * tiles + n))
    half_shape = jax.ShapeDtypeStruct((2, width // 2, count * wide), BF16)
    return pl.pallas_call(
        functools.partial(weight_gradient_kernel, order, groups),
        grid_spec=pltpu.PrefetchScalarGridSpec(
            num_scalar_prefetch=1,
            grid=(count, 2, tiles),
            in_specs=[spec(item, width, lambda *_: 0) for item in lefts]
            + [spec(item, tile, far_tile(n)) for n, item in enumerate(fars)]
            + [spec(item, tile, own_tile(n)) for n, item in enumerate(owns)],
            out_specs=[half_spec, half_spec],
            scratch_shapes=[pltpu.VMEM((width, length), BF16), pltpu.VMEM((width, length), BF16)],
        ),
        out_shape=[half_shape, half_shape],
        compiler_params=params(48),
        cost_estimate=pl.CostEstimate(
            flops=4 * count * length * width * wide, bytes_accessed=8 * count * length * width, transcendentals=0
        ),
        name=name,
    )(meta, *[item[0] for item in lefts + fars + owns])


def together(*trees):
    return lax.optimization_barrier(trees)


def swapped(array):
    return lax.ppermute(array, "tensor", [(0, 1), (1, 0)])


def crossed(array, size, bit):
    return lax.ppermute(array, "dp", [(n, n ^ bit) for n in range(size)])


def added(mine, theirs, kind):
    return (mine.astype(F32) + theirs.astype(F32)).astype(kind)


def part_of(array, part, parts, axis=0):
    rows = array.shape[axis] // parts
    return lax.dynamic_slice_in_dim(array, part * rows, rows, axis)


def halving_steps(size, steps):
    steps = [bit for bit in steps if bit < size]
    known = max(steps)
    while known * 2 < size:
        known *= 2
        steps.append(known)
    return steps


def halving_order(size, steps):
    order = []
    for spot in range(size):
        other = 0
        for bit in reversed([bit for bit in steps if bit]):
            other |= bit * (spot % 2)
            spot //= 2
        order.append(other)
    return order


class Halving:
    def __init__(self, send, keep, size, steps, groups):
        self.size, self.steps, self.groups = size, steps if groups > 1 else [], groups
        self.send, self.keep = (send, keep) if groups > 1 else (None, jnp.concatenate([keep, send], axis=1))

    def exchange(self):
        bit = self.steps[0]
        return crossed(self.send, self.size, bit) if bit else swapped(self.send)

    def result(self):
        if self.groups == 1:
            total = self.keep[1].astype(F32) + swapped(self.keep[0]).astype(F32)
            return lax.psum_scatter(total, "dp", scatter_dimension=0, tiled=True)
        assert not self.steps
        return self.keep


def add_kernel(forms, *refs):
    ins, outs = list(refs[: 2 * len(forms)]), list(refs[2 * len(forms) :])
    for form, lead in forms:
        total = ins.pop(0)[...].astype(F32) + ins.pop(0)[...].astype(F32)
        if lead is not None:
            targets = [ref.at[lead] for ref in (outs[:2] if lead == 0 else done)]
            done, outs = (outs[:2], outs[2:]) if lead == 0 else (done, outs)
        else:
            targets, outs = (outs[:1], outs[1:]) if form == "last" else (outs[:2], outs[2:])
        if form == "last":
            targets[0][...] = total
        elif form == "tensor":
            targets[0][...] = total[0].astype(BF16)
            targets[1][...] = total[1].astype(BF16)
        else:
            rows = total.shape[-2] // 2
            targets[0][...] = total[..., rows:, :].astype(BF16)
            targets[1][...] = total[..., :rows, :].astype(BF16)


def add_all(items, gots, join):
    items = [item for item in items]
    if not items:
        return items
    tiles = 3
    forms, operands, in_specs, shapes, out_specs = [], [], [], [], []

    def spec(dims):
        dims = dims[:-1] + (dims[-1] // tiles,)
        return pl.BlockSpec(dims, lambda n, lead=len(dims) - 1: (0,) * lead + (n,))

    for index, (item, got) in enumerate(zip(items, gots)):
        left = item.steps[1:]
        form = "last" if not left else "tensor" if left[0] == 0 else "rows"
        dims = item.keep.shape
        operands += [item.keep, got]
        in_specs += [spec(dims)] * 2
        if form == "tensor":
            dims = dims[1:]
        elif form == "rows":
            dims = dims[:-2] + (dims[-2] // 2, dims[-1])
        lead = index if join and index < 2 else None
        forms.append((form, lead))
        if lead == 1:
            continue
        if lead == 0:
            dims = (2,) + dims
        copies = 1 if form == "last" else 2
        shapes += [jax.ShapeDtypeStruct(dims, F32 if form == "last" else BF16)] * copies
        out_specs += [spec(dims)] * copies
    outs = list(pl.pallas_call(
        functools.partial(add_kernel, forms),
        grid=(tiles,),
        in_specs=in_specs,
        out_specs=out_specs,
        out_shape=shapes,
        compiler_params=params(32),
        name="sum_parts",
    )(*operands))
    rest = []
    for item, (form, lead) in zip(items, forms):
        if lead == 1:
            continue
        item.steps = item.steps[1:]
        item.send = None if form == "last" else outs.pop(0)
        item.keep = outs.pop(0)
        rest.append(item)
    return rest


def shards(
    size, tokens, cotangent, prev_att, prev_ffn, numerator_state, denominator_state, exponent_offset_state,
    ln1_gain, ln1_bias, ln2_gain, ln2_bias, mix_key, mix_value, mix_recept, mix2_key, mix2_recept,
    time_decay, time_first, key_weight, value_weight, receptance_weight, output_weight,
    channel_key_weight, channel_receptance_weight, channel_value_weight,
):
    _, length, width = tokens.shape
    half = key_weight.shape[1]
    units = channel_key_weight.shape[1]
    block = min(256, length)
    blocks = length // block
    chunks = block // STEP
    side = lax.axis_index("tensor")
    place = lax.axis_index("dp")
    core = place % 2
    meta = jnp.stack([side, place]).astype(jnp.int32)
    rows = width // size
    groups = size if rows % 16 == 0 else 1
    own_channels = jnp.concatenate(
        [time_decay[None], time_first[None], numerator_state, denominator_state, exponent_offset_state]
    )
    vectors = (ln1_gain, ln1_bias, mix_key, mix_value, mix_recept, ln2_gain, ln2_bias, mix2_key, mix2_recept)
    vectors = jnp.concatenate([item[None] for item in vectors] + [prev_att, prev_ffn, jnp.zeros((3, width), F32)])

    quarter = 2 * core + (place // 2) % 2
    projections = jnp.stack(
        [part_of(item, quarter, 4) for item in (key_weight, value_weight, receptance_weight)]
        + [part_of(output_weight, quarter, 4).reshape(-1, 2, half).swapaxes(0, 1).reshape(-1, half)]
    )
    def segment_spec(index=lambda i: i):
        return pl.BlockSpec((None, block, width), lambda i, meta: (meta[0], index(i), 0))

    def rows_spec(columns, index=lambda i: i):
        return pl.BlockSpec((block, columns), lambda i, *_: (index(i), 0))

    def stack_spec(count, columns, index=lambda i: i, size_of=block):
        return pl.BlockSpec((count, size_of, columns), lambda i, *_: (0, index(i), 0))

    def bound_spec(index=lambda i: i):
        return pl.BlockSpec((1, 8, width), lambda i, *_: (index(i), 0, 0))

    def back(i):
        return blocks - 1 - i

    def shape(dims, kind):
        return jax.ShapeDtypeStruct(dims, kind)

    scan_shapes = [
        shape((length, half), BF16), shape((7, length, half), F32),
        shape((2, length // STEP, half), F32), shape((8, half), F32),
    ]
    scan_specs = [rows_spec(half), stack_spec(7, half), stack_spec(2, half, size_of=chunks), whole((8, half))]
    scan_scratch = [
        pltpu.VMEM((block, half), F32), pltpu.VMEM((8, half), F32), pltpu.VMEM((4, chunks + 8, half), F32),
    ]
    mix1, bounds1, last_att, gated_own, save_own, start_own, final_own = pl.pallas_call(
        first_kernel,
        grid_spec=pltpu.PrefetchScalarGridSpec(
            num_scalar_prefetch=1,
            grid=(blocks,),
            in_specs=[segment_spec(), whole((16, width))] + [whole((width, half))] * 3 + [whole((8, half))],
            out_specs=[stack_spec(3, width), bound_spec(), whole((1, width))] + scan_specs,
            scratch_shapes=scan_scratch + [pltpu.VMEM((1, width), F32)],
        ),
        out_shape=[
            shape((3, length, width), BF16), shape((blocks, 8, width), F32), shape((1, width), F32),
        ] + scan_shapes,
        compiler_params=params(48),
        name="time_mix_own",
    )(meta, tokens, vectors, key_weight, value_weight, receptance_weight, own_channels)

    channel_weights, mix1 = together(
        (channel_key_weight, channel_receptance_weight, channel_value_weight), mix1
    )
    ckr_part = jnp.concatenate([part_of(item, quarter, 4) for item in channel_weights[:2]], axis=1)
    proj_one, far_channels, mix1, ckr_part, cv_weight = together(
        swapped(projections), swapped(own_channels), mix1, ckr_part, channel_weights[2]
    )
    cut = units // 2 * 5 // 8
    start = core * (units // 2)
    cv_parts = [
        lax.dynamic_slice_in_dim(cv_weight, start, cut, 0),
        lax.dynamic_slice_in_dim(cv_weight, start + cut, units // 2 - cut, 0),
    ]
    proj_two, proj_three, ckr_one, cv_parts = together(
        crossed(proj_one, size, 2), crossed(proj_one, size, 1), swapped(ckr_part), cv_parts
    )
    proj_four, ckr_three, ckr_one, mix1, cv_parts = together(
        crossed(proj_two, size, 1), crossed(ckr_one, size, 1), ckr_one, mix1, cv_parts
    )
    ckr_two = crossed(ckr_one, size, 2)
    cv_near = swapped(cv_parts[0])
    far_kvr, wo_far, gated_far, save_far, start_far, final_far = pl.pallas_call(
        second_kernel,
        grid_spec=pltpu.PrefetchScalarGridSpec(
            num_scalar_prefetch=1,
            grid=(blocks,),
            in_specs=[stack_spec(3, width)] + [whole((4, width // 4, half))] * 4 + [whole((8, half))],
            out_specs=[whole((3, width, half)), whole((half, width))] + scan_specs,
            scratch_shapes=scan_scratch,
        ),
        out_shape=[shape((3, width, half), BF16), shape((half, width), BF16)] + scan_shapes,
        compiler_params=params(48),
        name="time_mix_far",
    )(meta, mix1, proj_one, proj_two, proj_three, proj_four, far_channels)

    middle, mix2, bounds2, last_ffn = pl.pallas_call(
        middle_kernel,
        grid_spec=pltpu.PrefetchScalarGridSpec(
            num_scalar_prefetch=1,
            grid=(blocks,),
            in_specs=[segment_spec(), rows_spec(half), rows_spec(half)]
            + [whole((half, width))] * 2 + [whole((16, width))],
            out_specs=[rows_spec(width), stack_spec(2, width), bound_spec(), whole((1, width))],
            scratch_shapes=[pltpu.VMEM((1, width), F32)],
        ),
        out_shape=[
            shape((length, width), F32), shape((2, length, width), BF16),
            shape((blocks, 8, width), F32), shape((1, width), F32),
        ],
        compiler_params=params(48),
        name="middle",
    )(meta, tokens, gated_own, gated_far, output_weight, wo_far, vectors)
    ckr_two, cv_near, mix2, cv_rest = together(ckr_two, cv_near, mix2, cv_parts[1])
    ckr_four, cv_next, cv_other = together(crossed(ckr_two, size, 1), swapped(cv_rest), crossed(cv_near, size, 1))
    cv_last = crossed(cv_next, size, 1)

    (
        mixed_own, mixed_far, h_own, h_far, dpre_own, dpre_far, d_values, rec_own, rec_far, d_middle, d_att, dg_own, dg_far, sums2,
    ) = pl.pallas_call(
        channel_kernel,
        grid_spec=pltpu.PrefetchScalarGridSpec(
            num_scalar_prefetch=1,
            grid=(blocks,),
            in_specs=[
                segment_spec(back), rows_spec(width, back), stack_spec(2, width, back), bound_spec(back),
                whole((16, width)), whole((width, units)), whole((width, half)),
            ] + [whole((width // 4, units + half))] * 4 + [
                whole((units, width)), whole((cut, width)), whole((units // 2 - cut, width)),
                whole((cut, width)), whole((units // 2 - cut, width)),
                whole((half, width)), whole((half, width)),
            ],
            out_specs=[
                rows_spec(half, back), rows_spec(half, back), rows_spec(units, back), rows_spec(units, back),
                rows_spec(units, back), rows_spec(units, back), rows_spec(width, back),
                rows_spec(half, back), rows_spec(half, back), rows_spec(width, back), rows_spec(width, back),
                rows_spec(half, back), rows_spec(half, back), whole((8, width)),
            ],
            scratch_shapes=[
                pltpu.VMEM((1, width), F32), pltpu.VMEM((width, units), BF16),
                pltpu.VMEM((width, width), BF16), pltpu.VMEM((units, width), BF16),
            ],
        ),
        out_shape=[
            shape((length, half), BF16), shape((length, half), BF16),
            shape((length, units), BF16), shape((length, units), BF16),
            shape((length, units), BF16), shape((length, units), BF16), shape((length, width), BF16),
            shape((length, half), BF16), shape((length, half), BF16),
            shape((length, width), F32), shape((length, width), BF16),
            shape((length, half), F32), shape((length, half), F32), shape((8, width), F32),
        ],
        compiler_params=params(60),
        name="channel_mix",
    )(
        meta, cotangent, middle, mix2, bounds2, vectors, channel_key_weight, channel_receptance_weight,
        ckr_one, ckr_two, ckr_three, ckr_four, channel_value_weight, cv_near, cv_next, cv_other, cv_last,
        output_weight, wo_far,
    )

    def gradients(steps, tasks, tile, name):
        steps = halving_steps(size, steps)
        send, keep = weight_gradient(halving_order(size, steps), groups, meta, tasks, tile, name)
        return Halving(send, keep, size, steps, groups)

    def scan_back(grads, saved, starts, channels):
        return pl.pallas_call(
            scan_back_kernel,
            grid=(blocks,),
            in_specs=[
                rows_spec(half, back), stack_spec(7, half, back),
                stack_spec(2, half, back, size_of=chunks), whole((8, half)),
            ],
            out_specs=[stack_spec(3, half, back), whole((8, half))],
            out_shape=[shape((3, length, half), BF16), shape((8, half), F32)],
            scratch_shapes=[pltpu.VMEM((block, half), F32)] * 3
            + [pltpu.VMEM((8, half), F32), pltpu.VMEM((5, chunks + 8, half), F32)],
            compiler_params=params(48),
            name="scan_back",
        )(grads, saved, starts, channels)

    a_sum = gradients(
        (1, 0, 2, 4, 8), [((mix2, 0), (dpre_far, None), (dpre_own, None))], TILE, "channel_key_gradient"
    )
    d_values, a_sum.send, a_sum.keep = together(d_values, a_sum.send, a_sum.keep)
    b_sum = gradients(
        (1, 2, 0, 4, 8), [((d_values, None), (h_far, None), (h_own, None))], TILE, "channel_value_gradient"
    )
    def round_of(parts, extra, keep, join=False):
        gots, sends, extra, keep = together(
            [item.exchange() for item in parts], [(item.send, item.keep) for item in parts], extra, keep
        )
        for item, (send, kept) in zip(parts, sends):
            item.send, item.keep = send, kept
        return add_all(parts, gots, join), extra, keep

    def active(*items):
        return [item for item in items if item.steps]

    _, mixed_in, (d_att, a_sum.send, b_sum.send) = round_of(
        [], swapped(mixed_far), (d_att, a_sum.send, b_sum.send)
    )
    c_sum = gradients(
        (1, 4, 8, 2, 0),
        [((d_att, None), (gated_far, None), (gated_own, None)), ((mix2, 1), (rec_far, None), (rec_own, None))],
        half, "output_gradient",
    )
    _, (c_sum.send, c_sum.keep), dgs = round_of(
        active(a_sum, b_sum), (c_sum.send, c_sum.keep), (dg_far, dg_own)
    )
    d_far, channel_sums_far = scan_back(dgs[0], save_far, start_far, far_channels)
    d_own, channel_sums_own = scan_back(dgs[1], save_own, start_own, own_channels)
    d_sum = gradients(
        (1, 2, 4, 8, 0), [((mix1, n), (d_far, n), (d_own, n)) for n in range(3)], half, "projection_gradient"
    )
    _, (d_sum.send, d_sum.keep), d_middle = round_of(
        active(a_sum, b_sum, c_sum), (d_sum.send, d_sum.keep), d_middle
    )
    grad_part, sums1 = pl.pallas_call(
        last_kernel,
        grid_spec=pltpu.PrefetchScalarGridSpec(
            num_scalar_prefetch=1,
            grid=(blocks,),
            in_specs=[
                segment_spec(back), rows_spec(width, back), stack_spec(3, half, back), stack_spec(3, half, back),
                whole((width, half)), whole((width, half)), whole((width, half)), whole((3, width, half)),
                bound_spec(back), whole((16, width)),
            ],
            out_specs=[rows_spec(width, back), whole((8, width))],
            scratch_shapes=[pltpu.VMEM((1, width), F32)],
        ),
        out_shape=[shape((length, width), BF16), shape((8, width), F32)],
        compiler_params=params(48),
        name="time_mix_back",
    )(
        meta, tokens, d_middle, d_own, d_far, key_weight, value_weight, receptance_weight, far_kvr,
        bounds1, vectors,
    )

    def both(own, far):
        return jnp.where(side == 0, jnp.stack([own, far]), jnp.stack([far, own]))

    def full(own, far):
        return jnp.where(side == 0, jnp.concatenate([own, far]), jnp.concatenate([far, own]))

    small = jnp.concatenate([
        sums1[0:2], sums2[0:2], sums1[2:5], sums2[2:4],
        jnp.stack([full(channel_sums_own[n], channel_sums_far[n]) for n in range(2)]),
    ])
    last_rows = jnp.concatenate([last_att, last_ffn])
    (ab_sum, *_), (grad_part, small), (last_rows, final_far) = round_of(
        active(a_sum, b_sum, c_sum, d_sum), (grad_part, small), (last_rows, final_far), True
    ) if groups > 1 else ([a_sum], (grad_part, small), (last_rows, final_far))
    first, second = grad_part[: length // 2], grad_part[length // 2 :]

    def live():
        return active(ab_sum, c_sum, d_sum)

    def small_parts(bits):
        return [crossed(small, size, bit) if bit else swapped(small) for bit in bits]

    _, (first_in, got), (second, last_rows, final_far) = round_of(
        live(), (swapped(first), small_parts([1])), (second, last_rows, final_far)
    )
    small = small + got[0]
    _, (second_in, got), (last_rows, final_far) = round_of(
        live(), (swapped(second), small_parts([2])), (last_rows, final_far)
    )
    small = small + got[0]
    _, (last_in, back_states, got), _ = round_of(
        live(), (swapped(last_rows), swapped(final_far), small_parts([0])), ()
    )
    small = small + got[0]
    bit = 4
    while bit < size:
        pair = bit * 2 < size
        _, got, _ = round_of(live(), small_parts([bit, 2 * bit, 3 * bit] if pair else [bit]), ())
        small = small + got[0]
        if pair:
            small = small + (got[1] + got[2])
        bit *= 4
    while live():
        round_of(live(), (), ())
    grad_tokens = both(grad_part, jnp.concatenate([first_in, second_in])).astype(F32)
    mixed_out = both(mixed_own, mixed_in)
    finals = [both(final_own[n], back_states[n]) for n in range(3)]
    last_rows = both(last_rows, last_in)
    g_ck, g_cv = (a_sum.result(), b_sum.result()) if groups == 1 else ab_sum.result()
    g_other, g_kvr = c_sum.result(), d_sum.result()
    return (
        (mixed_out, grad_tokens, *finals, last_rows[:, 0], last_rows[:, 1])
        + tuple(small[n] for n in range(11))
        + tuple(g_kvr[:, n * half : (n + 1) * half] for n in range(3))
        + (g_other[:, :half].T, g_ck, g_other[:, half:], g_cv.T)
    )


def solution(mesh):
    split = P("dp", "tensor")
    turned = P("tensor", "dp")
    return jax.shard_map(
        functools.partial(shards, mesh.shape["dp"]),
        mesh=mesh,
        in_specs=(P("dp"), P("dp"), P("dp"), P("dp"), split, split, split)
        + (P(),) * 9
        + (P("tensor"), P("tensor"))
        + (P(None, "tensor"),) * 3
        + (P("tensor"), P(None, "tensor"), P(None, "tensor"), P("tensor")),
        out_specs=(P("dp", None, "tensor"), P("dp"), split, split, split, P("dp"), P("dp"))
        + (P(),) * 11
        + (split, split, split, turned, split, split, turned),
        check_vma=False,
    )
```

```python
import functools

import jax
import jax.numpy as jnp
from jax import lax
from jax.experimental import pallas as pl
from jax.experimental.pallas import tpu as pltpu
from jax.sharding import PartitionSpec as P

F32 = jnp.float32
BF16 = jnp.bfloat16
STEP = 8
MIB = 1 << 20
HIDDEN = 512


def nn(left, right):
    return jnp.dot(left, right, preferred_element_type=F32)


def nt(left, right):
    return lax.dot_general(left, right, (((1,), (1,)), ((), ())), preferred_element_type=F32)


def sigmoid(x):
    return 1.0 / (1.0 + jnp.exp(-x))


def row_sum(x):
    return jnp.sum(x, axis=0, keepdims=True)


def lane_mean(x):
    return jnp.mean(x, axis=-1, keepdims=True)


def normalize(x):
    center = x - lane_mean(x)
    scale = lax.rsqrt(lane_mean(center * center) + 1e-05)
    return center * scale, scale


def order_matrix(count, turned=False):
    chunks = count // STEP
    row = lax.broadcasted_iota(jnp.int32, (count, count), 1 if turned else 0)
    token = lax.broadcasted_iota(jnp.int32, (count, count), 0 if turned else 1)
    return (token == (row % chunks) * STEP + row // chunks).astype(BF16)


def row_before(x, first):
    chunks = x.shape[0] // STEP
    ends = x[-chunks:, :]
    rows = lax.broadcasted_iota(jnp.int32, ends.shape, 0)
    head = jnp.where(rows == 0, first, pltpu.roll(ends, 1, 0))
    return jnp.concatenate([head, x[:-chunks, :]])


def row_after(x, last):
    chunks = x.shape[0] // STEP
    starts = x[:chunks, :]
    rows = lax.broadcasted_iota(jnp.int32, starts.shape, 0)
    tail = jnp.where(rows == chunks - 1, last, pltpu.roll(starts, chunks - 1, 0))
    return jnp.concatenate([x[chunks:, :], tail])


def put_quarters(meta, target, pieces):
    core, side = meta[1] % 2, (meta[1] // 2) % 2
    rows = target.shape[-2] // 4
    spots = (2 * core + side, 2 * core + 1 - side, 2 - 2 * core + side, 3 - 2 * core - side)
    for spot, piece in zip(spots, pieces):
        at = pl.ds(pl.multiple_of(spot * rows, rows), rows)
        if len(target.shape) == 3:
            target[:, at, :] = piece[...]
        else:
            target[at, :] = piece[...]


def put_halves(meta, target, mine, other):
    core = meta[1] % 2
    half = target.shape[0] // 2
    for start, pieces in ((core * half, mine), ((1 - core) * half, other)):
        for piece in pieces:
            rows = piece.shape[0]
            target[pl.ds(pl.multiple_of(start, 16), rows), :] = piece[...]
            start = start + rows


def wkv_forward(segment, first_block, k_ref, channel_ref, save_ref, start_ref, final_ref, carry, work):
    chunks = start_ref.shape[1]
    rate = jnp.exp(channel_ref[0:1, :])
    boost = channel_ref[1:2, :]

    @pl.when(first_block)
    def _():
        for n in range(3):
            carry[n : n + 1, :] = channel_ref[pl.ds(2 + 2 * n + segment, 1), :]

    def keys(step):
        return k_ref[step * chunks : (step + 1) * chunks, :]

    peak = keys(STEP - 1)
    for step in range(STEP - 1):
        peak = jnp.maximum(peak, keys(step) - (STEP - 1.0 - step) * rate)
    number = jnp.zeros_like(peak)
    weight = jnp.zeros_like(peak)
    for step in range(STEP):
        part = jnp.exp(keys(step) - (STEP - 1.0 - step) * rate - peak)
        number = number + part * save_ref[0, step * chunks : (step + 1) * chunks, :]
        weight = weight + part
    work[0, 0:chunks, :] = peak
    top = carry[2:3, :]
    for chunk in range(chunks):
        work[1, chunk : chunk + 1, :] = top
        top = jnp.maximum(top - STEP * rate, work[0, chunk : chunk + 1, :])
    work[1, chunks : chunks + 1, :] = top
    tops = work[1, 0:chunks, :]
    later = work[1, 1 : chunks + 1, :]
    fresh = jnp.exp(peak - later)
    work[0, 0:chunks, :] = jnp.exp(tops - STEP * rate - later)
    work[2, 0:chunks, :] = fresh * number
    work[3, 0:chunks, :] = fresh * weight
    num = carry[0:1, :]
    den = carry[1:2, :]
    for chunk in range(chunks):
        at = slice(chunk, chunk + 1)
        start_ref[0, at, :] = num
        start_ref[1, at, :] = den
        num = work[0, at, :] * num + work[2, at, :]
        den = work[0, at, :] * den + work[3, at, :]
    carry[0:1, :] = num
    carry[1:2, :] = den
    carry[2:3, :] = top
    final_ref[0:3, :] = carry[0:3, :]

    num = start_ref[0, :, :]
    den = start_ref[1, :, :]
    top = tops
    for step in range(STEP):
        at = slice(step * chunks, (step + 1) * chunks)
        key = keys(step)
        value = save_ref[0, at, :]
        gap = top - (boost + key)
        small = jnp.exp(-jnp.abs(gap))
        state_wins = gap > 0
        old = jnp.where(state_wins, 1.0, small)
        now = jnp.where(state_wins, small, 1.0)
        inverse = 1.0 / (old * den + now)
        old = old * inverse
        now = now * inverse
        save_ref[1, at, :] = old * num + now * value
        save_ref[3, at, :] = old
        save_ref[4, at, :] = now
        faded = top - rate
        gap = faded - key
        small = jnp.exp(-jnp.abs(gap))
        state_wins = gap > 0
        keep = jnp.where(state_wins, 1.0, small)
        fresh = jnp.where(state_wins, small, 1.0)
        save_ref[5, at, :] = keep
        save_ref[6, at, :] = fresh
        num = keep * num + fresh * value
        den = keep * den + fresh
        top = jnp.maximum(faded, key)


def project_and_scan(segment, inputs, weights, channel_ref, gated_ref, save_ref, start_ref, final_ref, k_ref, carry, work):
    k_ref[...] = nn(inputs[0], weights[0])
    save_ref[0, :, :] = nn(inputs[1], weights[1])
    gate = sigmoid(nn(inputs[2], weights[2]))
    save_ref[2, :, :] = gate
    wkv_forward(segment, pl.program_id(0) == 0, k_ref, channel_ref, save_ref, start_ref, final_ref, carry, work)
    gated_ref[...] = (gate * save_ref[1, :, :]).astype(BF16)


def first_kernel(
    meta, tokens_ref, vector_ref, wk_ref, wv_ref, wr_ref, channel_ref,
    mix_ref, bound_ref, last_ref, gated_ref, save_ref, start_ref, final_ref,
    k_ref, carry, work, row,
):
    @pl.when(pl.program_id(0) == 0)
    def _():
        row[...] = vector_ref[pl.ds(9 + meta[0], 1), :]

    tokens = nn(order_matrix(tokens_ref.shape[0]), tokens_ref[...])
    hat, _ = normalize(tokens)
    normed = hat * vector_ref[0:1, :] + vector_ref[1:2, :]
    first = row[...]
    bound_ref[0, :, :] = jnp.broadcast_to(first, bound_ref.shape[1:])
    before = row_before(normed, first)
    step = normed - before
    count = normed.shape[0]
    row[...] = normed[count - 1 : count, :]
    last_ref[...] = normed[count - 1 : count, :]
    mixed = [(before + step * vector_ref[2 + n : 3 + n, :]).astype(BF16) for n in range(3)]
    for n in range(3):
        mix_ref[n, :, :] = mixed[n]
    project_and_scan(
        meta[0], mixed, (wk_ref[...], wv_ref[...], wr_ref[...]), channel_ref,
        gated_ref, save_ref, start_ref, final_ref, k_ref, carry, work,
    )


def second_kernel(
    meta, mix_ref, one_ref, two_ref, three_ref, four_ref, channel_ref,
    weight_ref, wo_ref, gated_ref, save_ref, start_ref, final_ref, k_ref, carry, work,
):
    @pl.when(pl.program_id(0) == 0)
    def _():
        pieces = (one_ref, two_ref, three_ref, four_ref)
        put_quarters(meta, weight_ref, [piece.at[0:3] for piece in pieces])
        rows, half = wo_ref.shape[0] // 4, weight_ref.shape[2]
        for n in range(2):
            put_quarters(
                meta, wo_ref.at[:, n * half : (n + 1) * half],
                [piece.at[3, n * rows : (n + 1) * rows, :] for piece in pieces],
            )

    project_and_scan(
        meta[0], [mix_ref[n, :, :] for n in range(3)], [weight_ref[n, :, :] for n in range(3)], channel_ref,
        gated_ref, save_ref, start_ref, final_ref, k_ref, carry, work,
    )


def middle_kernel(
    meta, tokens_ref, own_ref, far_ref, wo_own_ref, wo_far_ref, vector_ref,
    middle_ref, mix_ref, bound_ref, last_ref, row,
):
    @pl.when(pl.program_id(0) == 0)
    def _():
        row[...] = vector_ref[pl.ds(11 + meta[0], 1), :]

    middle = (
        nn(order_matrix(tokens_ref.shape[0]), tokens_ref[...])
        + nn(own_ref[...], wo_own_ref[...])
        + nn(far_ref[...], wo_far_ref[...])
    )
    middle_ref[...] = middle
    hat, _ = normalize(middle)
    normed = hat * vector_ref[5:6, :] + vector_ref[6:7, :]
    first = row[...]
    bound_ref[0, :, :] = jnp.broadcast_to(first, bound_ref.shape[1:])
    before = row_before(normed, first)
    step = normed - before
    count = normed.shape[0]
    row[...] = normed[count - 1 : count, :]
    last_ref[...] = normed[count - 1 : count, :]
    for n in range(2):
        mix_ref[n, :, :] = (before + step * vector_ref[7 + n : 8 + n, :]).astype(BF16)


def norm_backward(x, vectors, bound, grads, weights, row, sums_ref):
    gain, bias = vectors
    hat, scale = normalize(x)
    normed = hat * gain + bias
    step = normed - row_before(normed, bound)
    total = grads[0]
    current = grads[0] * weights[0]
    sums_ref[2:3, :] += row_sum(grads[0] * step)
    for n in range(1, len(grads)):
        total = total + grads[n]
        current = current + grads[n] * weights[n]
        sums_ref[2 + n : 3 + n, :] += row_sum(grads[n] * step)
    shifted = total - current
    flow = current + row_after(shifted, row[...])
    row[...] = shifted[0:1, :]
    sums_ref[0:1, :] += row_sum(flow * hat)
    sums_ref[1:2, :] += row_sum(flow)
    inner = flow * gain
    return scale * (inner - lane_mean(inner) - hat * lane_mean(inner * hat))


def hidden_kernel(mix_ref, ck_ref, cv_ref, hidden_ref, values_ref):
    relu = jnp.maximum(nn(mix_ref[...], ck_ref[...]), 0.0)
    hidden = (relu * relu).astype(BF16)
    hidden_ref[...] = hidden
    part = nn(hidden, cv_ref[...])

    @pl.when(pl.program_id(0) == 0)
    def _():
        values_ref[...] = part

    @pl.when(pl.program_id(0) > 0)
    def _():
        values_ref[...] += part


def turn_rows(meta, order, groups, source, turned, placed):
    whole = turned.shape[0]
    target = turned if groups > 1 else placed
    for col in range(0, whole, 128):
        target[col : col + 128, :] = source[:, col : col + 128].T
    if groups > 1:
        rows = whole // groups
        for spot, other in enumerate(order):
            start = pl.multiple_of((meta[1] ^ other) * rows, rows)
            placed[spot * rows : (spot + 1) * rows, :] = turned[pl.ds(start, rows), :]


def channel_kernel(
    orders, groups, block, meta, cot_ref, middle_ref, mix_ref, own_values_ref, hidden_ref, ck_ref, cv_ref, cr_own_ref,
    one_ref, two_ref, three_ref, four_ref, near_ref, next_ref, other_ref, last_ref,
    mixed_own_ref, mixed_far_ref, rec_own_ref, rec_far_ref, cr_ref, d_key_ref,
    key_send_ref, key_keep_ref, value_send_ref, value_keep_ref,
    ck_far_ref, cv_far_ref, h_far_ref, values_ref, d_values_ref, turned_ref, key_turned_ref, value_turned_ref,
):
    step = pl.program_id(0)
    tile = hidden_ref.shape[1]
    units = ck_far_ref.shape[1]
    count = units // tile
    length, width = values_ref.shape
    half = cr_own_ref.shape[1]

    @pl.when(step == 0)
    def _():
        pieces = (one_ref, two_ref, three_ref, four_ref)
        put_quarters(meta, ck_far_ref, [piece.at[:, :units] for piece in pieces])
        own_at = pl.ds(pl.multiple_of(meta[0] * half, 128), half)
        far_at = pl.ds(pl.multiple_of((1 - meta[0]) * half, 128), half)
        cr_ref[:, own_at] = cr_own_ref[...]
        put_quarters(meta, cr_ref.at[:, far_at], [piece.at[:, units:] for piece in pieces])
        put_halves(meta, cv_far_ref, (near_ref, next_ref), (other_ref, last_ref))
        values_ref[...] = own_values_ref[...]
        turn_rows(meta, orders[0], groups, mix_ref.at[0], turned_ref, key_turned_ref)

    @pl.when(step < count)
    def _():
        at = pl.ds(pl.multiple_of(step * tile, tile), tile)
        relu = jnp.maximum(nn(mix_ref[0, :, :], ck_far_ref[:, at]), 0.0)
        hidden = (relu * relu).astype(BF16)
        h_far_ref[:, at] = hidden
        values_ref[...] += nn(hidden, cv_far_ref[at, :])

    @pl.when(step == count - 1)
    def _():
        def rows_of(n, _):
            at = pl.ds(pl.multiple_of(n * block, block), block)
            values = values_ref[at, :]
            gate = sigmoid(nn(mix_ref[1, at, :], cr_ref[...]))
            mixed = (middle_ref[at, :] + gate * values).astype(BF16)
            mixed = nn(order_matrix(block, True), mixed)
            low, high = mixed[:, :half], mixed[:, half:]
            mixed_own_ref[at, :] = jnp.where(meta[0] == 0, low, high).astype(BF16)
            mixed_far_ref[at, :] = jnp.where(meta[0] == 0, high, low).astype(BF16)
            passed = nn(order_matrix(block), cot_ref[at, :]) * gate
            d_values_ref[at, :] = passed.astype(BF16)
            d_rec = passed * values * (1.0 - gate)
            low, high = d_rec[:, :half], d_rec[:, half:]
            rec_own_ref[at, :] = jnp.where(meta[0] == 0, low, high).astype(BF16)
            rec_far_ref[at, :] = jnp.where(meta[0] == 0, high, low).astype(BF16)
            return 0

        lax.fori_loop(0, length // block, rows_of, 0)
        turn_rows(meta, orders[1], groups, d_values_ref, turned_ref, value_turned_ref)
        d_key_ref[...] = jnp.zeros_like(d_key_ref)

    def backward(hidden, ck, cv):
        slope = 2.0 * jnp.sqrt(hidden.astype(F32))
        d_pre = (slope * nt(d_values_ref[...], cv)).astype(BF16)
        d_key_ref[...] += nt(d_pre, ck)
        for turned, right, send_ref, keep_ref in (
            (value_turned_ref, hidden, value_send_ref, value_keep_ref),
            (key_turned_ref, d_pre, key_send_ref, key_keep_ref),
        ):
            part = nn(turned[...], right).astype(BF16)
            keep_ref[0, :, :] = part[: width // 2, :]
            send_ref[0, :, :] = part[width // 2 :, :]

    @pl.when((step >= count) & (step < 2 * count))
    def _():
        at = pl.ds(pl.multiple_of((step - count) * tile, tile), tile)
        backward(h_far_ref[:, at], ck_far_ref[:, at], cv_far_ref[at, :])

    @pl.when(step >= 2 * count)
    def _():
        backward(hidden_ref[...], ck_ref[...], cv_ref[...])


def middle_back_kernel(
    meta, cot_ref, middle_ref, d_key_ref, rec_own_ref, rec_far_ref, cr_ref, bound_ref, vector_ref, wo_own_ref, wo_far_ref,
    dmid_ref, datt_ref, dg_own_ref, dg_far_ref, sums_ref, row,
):
    @pl.when(pl.program_id(0) == 0)
    def _():
        row[...] = jnp.zeros_like(row)
        sums_ref[...] = jnp.zeros_like(sums_ref)

    half = rec_own_ref.shape[1]
    own, far = rec_own_ref[...], rec_far_ref[...]
    low, high = jnp.where(meta[0] == 0, own, far), jnp.where(meta[0] == 0, far, own)
    d_recept = nt(low, cr_ref[:, :half]) + nt(high, cr_ref[:, half:])
    grad = nn(order_matrix(cot_ref.shape[0]), cot_ref[...])
    d_middle = grad + norm_backward(
        middle_ref[...], (vector_ref[5:6, :], vector_ref[6:7, :]), bound_ref[0, 0:1, :],
        (d_key_ref[...], d_recept), (vector_ref[7:8, :], vector_ref[8:9, :]), row, sums_ref,
    )
    dmid_ref[...] = d_middle
    d_att = d_middle.astype(BF16)
    datt_ref[...] = d_att
    dg_own_ref[...] = nt(d_att, wo_own_ref[...])
    dg_far_ref[...] = nt(d_att, wo_far_ref[...])


def scan_back_kernel(
    dg_ref, save_ref, start_ref, channel_ref, out_ref, sums_ref, dy_ref, dk_ref, dv_ref, carry, work
):
    chunks = start_ref.shape[1]

    @pl.when(pl.program_id(0) == 0)
    def _():
        carry[...] = jnp.zeros_like(carry)
        sums_ref[...] = jnp.zeros_like(sums_ref)

    gate = save_ref[2, :, :]
    dy = dg_ref[...] * gate
    dy_ref[...] = dy
    out_ref[2, :, :] = (dy * save_ref[1, :, :] * (1.0 - gate)).astype(BF16)

    def at(step):
        return slice(step * chunks, (step + 1) * chunks)

    gn = jnp.zeros((chunks, dy.shape[1]), F32)
    gd = jnp.zeros_like(gn)
    product = jnp.ones_like(gn)
    for step in reversed(range(STEP)):
        part = save_ref[3, at(step), :] * dy_ref[at(step), :]
        keep = save_ref[5, at(step), :]
        gn = part + keep * gn
        gd = keep * gd - part * save_ref[1, at(step), :]
        product = product * keep
    work[0, 0:chunks, :] = gn
    work[1, 0:chunks, :] = gd
    work[2, 0:chunks, :] = product
    gn = carry[0:1, :]
    gd = carry[1:2, :]
    for chunk in reversed(range(chunks)):
        row = slice(chunk, chunk + 1)
        work[3, row, :] = gn
        work[4, row, :] = gd
        gn = work[0, row, :] + work[2, row, :] * gn
        gd = work[1, row, :] + work[2, row, :] * gd
    carry[0:1, :] = gn
    carry[1:2, :] = gd
    work[0, 0:chunks, :] = start_ref[0, :, :]
    work[1, 0:chunks, :] = start_ref[1, :, :]
    work[0, chunks : chunks + 1, :] = carry[2:3, :]
    work[1, chunks : chunks + 1, :] = carry[3:4, :]
    carry[2:3, :] = start_ref[0, 0:1, :]
    carry[3:4, :] = start_ref[1, 0:1, :]
    gn = work[3, 0:chunks, :]
    gd = work[4, 0:chunks, :]
    decay = STEP * (gn * work[0, 1 : chunks + 1, :] + gd * work[1, 1 : chunks + 1, :])
    first = jnp.zeros_like(gn)
    for step in reversed(range(STEP)):
        place = at(step)
        dy = dy_ref[place, :]
        value = save_ref[0, place, :]
        wkv = save_ref[1, place, :]
        share = save_ref[4, place, :] * dy
        bonus = share * (value - wkv)
        fresh = save_ref[6, place, :]
        through = fresh * (gn * value + gd)
        d_key = bonus + through
        dk_ref[place, :] = d_key
        dv_ref[place, :] = share + fresh * gn
        first = first + bonus
        decay = decay - through - float(step) * d_key
        part = save_ref[3, place, :] * dy
        keep = save_ref[5, place, :]
        gn = part + keep * gn
        gd = keep * gd - part * wkv
    sums_ref[0:1, :] -= row_sum(decay) * jnp.exp(channel_ref[0:1, :])
    sums_ref[1:2, :] += row_sum(first)
    out_ref[0, :, :] = dk_ref[...].astype(BF16)
    out_ref[1, :, :] = dv_ref[...].astype(BF16)


def last_kernel(
    meta, tokens_ref, dmid_ref, own_ref, far_ref, wk_ref, wv_ref, wr_ref, weight_ref, bound_ref,
    vector_ref, grad_ref, sums_ref, row,
):
    @pl.when(pl.program_id(0) == 0)
    def _():
        row[...] = jnp.zeros_like(row)
        sums_ref[...] = jnp.zeros_like(sums_ref)

    grads = [
        nt(own_ref[n, :, :], w_ref[...]) + nt(far_ref[n, :, :], weight_ref[n, :, :])
        for n, w_ref in enumerate((wk_ref, wv_ref, wr_ref))
    ]
    part = norm_backward(
        nn(order_matrix(tokens_ref.shape[0]), tokens_ref[...]), (vector_ref[0:1, :], vector_ref[1:2, :]), bound_ref[0, 0:1, :],
        grads, [vector_ref[2 + n : 3 + n, :] for n in range(3)], row, sums_ref,
    )
    grad = (dmid_ref[...] + part).astype(BF16)
    grad_ref[...] = nn(order_matrix(grad.shape[0], True), grad).astype(BF16)


def weight_gradient_kernel(order, groups, tasks, meta, *refs):
    *refs, send_ref, keep_ref, left_buf, right_buf, sems, turned, placed = refs
    step = pl.program_id(0)
    half = right_buf.shape[2] // 2
    whole = turned.shape[0]

    def copies(index):
        pairs = []
        for n, (spot, lead) in enumerate(tasks[index]):
            source = refs[spot] if lead is None else refs[spot].at[lead]
            slot = index % 2
            target = left_buf.at[slot] if n == 0 else right_buf.at[slot, :, (n - 1) * half : n * half]
            pairs.append(pltpu.make_async_copy(source, target, sems.at[slot, n]))
        return pairs

    @pl.when(step == 0)
    def _():
        for item in copies(0):
            item.start()

    for index in range(len(tasks)):
        @pl.when(step == index)
        def _(index=index):
            if index + 1 < len(tasks):
                for item in copies(index + 1):
                    item.start()
            for item in copies(index):
                item.wait()
            slot = index % 2
            turn_rows(meta, order, groups, left_buf.at[slot], turned, placed)
            part = nn(placed[...], right_buf[slot, :, :]).astype(BF16)
            for side in range(2):
                keep_ref[side, :, :] = part[: whole // 2, side * half : (side + 1) * half]
                send_ref[side, :, :] = part[whole // 2 :, side * half : (side + 1) * half]


def in_hbm(*arrays):
    return [
        pltpu.with_memory_space_constraint(item, pltpu.HBM) if item.size > 1 << 16 else item for item in arrays
    ]


def shape_of(dims, kind):
    large = functools.reduce(lambda a, b: a * b, dims) > 1 << 16
    return (pltpu.HBM if large else jax.ShapeDtypeStruct)(dims, kind)


def params(mib, steps=None):
    return pltpu.CompilerParams(vmem_limit_bytes=mib * MIB, dimension_semantics=steps)


def whole(shape):
    return pl.BlockSpec(shape, lambda *_: (0,) * len(shape), pipeline_mode=pl.Buffered(1))


def weight_gradient(order, groups, meta, arrays, tasks, name):
    length, width = arrays[tasks[0][0][0]].shape[-2:]
    half = arrays[tasks[0][1][0]].shape[-1]
    spec = pl.BlockSpec((2, width // 2, half), lambda n, meta: (0, 0, n))
    shape = shape_of((2, width // 2, len(tasks) * half), BF16)
    return pl.pallas_call(
        functools.partial(weight_gradient_kernel, order, groups, tasks),
        grid_spec=pltpu.PrefetchScalarGridSpec(
            num_scalar_prefetch=1,
            grid=(len(tasks),),
            in_specs=[pl.BlockSpec(memory_space=pl.ANY)] * len(arrays),
            out_specs=[spec, spec],
            scratch_shapes=[
                pltpu.VMEM((2, length, width), BF16), pltpu.VMEM((2, length, 2 * half), BF16),
                pltpu.SemaphoreType.DMA((2, 3)),
                pltpu.VMEM((width, length), BF16), pltpu.VMEM((width, length), BF16),
            ],
        ),
        out_shape=[shape, shape],
        compiler_params=params(40),
        name=name,
    )(meta, *arrays)


def together(*trees):
    return lax.optimization_barrier(trees)


def swapped(array):
    return lax.ppermute(array, "tensor", [(0, 1), (1, 0)])


def crossed(array, size, bit):
    return lax.ppermute(array, "dp", [(n, n ^ bit) for n in range(size)])


def added(mine, theirs, kind):
    return (mine.astype(F32) + theirs.astype(F32)).astype(kind)


def part_of(array, part, parts, axis=0):
    rows = array.shape[axis] // parts
    return lax.dynamic_slice_in_dim(array, part * rows, rows, axis)


def halving_steps(size, steps):
    steps = [bit for bit in steps if bit < size]
    known = max(steps)
    while known * 2 < size:
        known *= 2
        steps.append(known)
    return steps


def halving_order(size, steps):
    order = []
    for spot in range(size):
        other = 0
        for bit in reversed([bit for bit in steps if bit]):
            other |= bit * (spot % 2)
            spot //= 2
        order.append(other)
    return order


class Halving:
    def __init__(self, send, keep, size, steps, groups):
        self.size, self.steps, self.groups = size, steps if groups > 1 else [], groups
        self.send, self.keep = (send, keep) if groups > 1 else (None, jnp.concatenate([keep, send], axis=1))

    def exchange(self):
        bit = self.steps[0]
        return crossed(self.send, self.size, bit) if bit else swapped(self.send)

    def result(self):
        if self.groups == 1:
            total = self.keep[1].astype(F32) + swapped(self.keep[0]).astype(F32)
            return lax.psum_scatter(total, "dp", scatter_dimension=0, tiled=True)
        assert not self.steps
        return self.keep


def add_kernel(forms, *refs):
    ins, outs = list(refs[: 2 * len(forms)]), list(refs[2 * len(forms) :])
    for form, lead in forms:
        total = ins.pop(0)[...].astype(F32) + ins.pop(0)[...].astype(F32)
        if lead is not None:
            targets = [ref.at[lead] for ref in (outs[:2] if lead == 0 else done)]
            done, outs = (outs[:2], outs[2:]) if lead == 0 else (done, outs)
        else:
            targets, outs = (outs[:1], outs[1:]) if form == "last" else (outs[:2], outs[2:])
        if form == "last":
            targets[0][...] = total
        elif form == "tensor":
            targets[0][...] = total[0].astype(BF16)
            targets[1][...] = total[1].astype(BF16)
        else:
            rows = total.shape[-2] // 2
            targets[0][...] = total[..., rows:, :].astype(BF16)
            targets[1][...] = total[..., :rows, :].astype(BF16)


def add_all(items, gots, join, pin):
    items = [item for item in items]
    if not items:
        return items
    tiles = 3 if sum(item.keep.size for item in items) > 1 << 20 else 1
    forms, operands, in_specs, shapes, out_specs = [], [], [], [], []

    def spec(dims):
        dims = dims[:-1] + (dims[-1] // tiles,)
        return pl.BlockSpec(dims, lambda n, lead=len(dims) - 1: (0,) * lead + (n,))

    for index, (item, got) in enumerate(zip(items, gots)):
        left = item.steps[1:]
        form = "last" if not left else "tensor" if left[0] == 0 else "rows"
        dims = item.keep.shape
        operands += [item.keep, got]
        in_specs += [spec(dims)] * 2
        if form == "tensor":
            dims = dims[1:]
        elif form == "rows":
            dims = dims[:-2] + (dims[-2] // 2, dims[-1])
        lead = index if join and index < 2 else None
        forms.append((form, lead))
        if lead == 1:
            continue
        if lead == 0:
            dims = (2,) + dims
        copies = 1 if form == "last" else 2
        kind = pltpu.HBM if pin == 2 else jax.ShapeDtypeStruct
        shapes += [kind(dims, F32 if form == "last" else BF16)] * copies
        out_specs += [spec(dims)] * copies
    outs = list(pl.pallas_call(
        functools.partial(add_kernel, forms),
        grid=(tiles,),
        in_specs=in_specs,
        out_specs=out_specs,
        out_shape=shapes,
        compiler_params=params(32),
        name="sum_parts",
    )(*(in_hbm(*operands) if pin else operands)))
    rest = []
    for item, (form, lead) in zip(items, forms):
        if lead == 1:
            continue
        item.steps = item.steps[1:]
        item.send = None if form == "last" else outs.pop(0)
        item.keep = outs.pop(0)
        rest.append(item)
    return rest


def shards(
    size, tokens, cotangent, prev_att, prev_ffn, numerator_state, denominator_state, exponent_offset_state,
    ln1_gain, ln1_bias, ln2_gain, ln2_bias, mix_key, mix_value, mix_recept, mix2_key, mix2_recept,
    time_decay, time_first, key_weight, value_weight, receptance_weight, output_weight,
    channel_key_weight, channel_receptance_weight, channel_value_weight,
):
    _, length, width = tokens.shape
    half = key_weight.shape[1]
    units = channel_key_weight.shape[1]
    block = min(256, length)
    blocks = length // block
    chunks = block // STEP
    side = lax.axis_index("tensor")
    place = lax.axis_index("dp")
    core = place % 2
    meta = jnp.stack([side, place]).astype(jnp.int32)
    rows = width // size
    groups = size if rows % 16 == 0 else 1
    own_channels = jnp.concatenate(
        [time_decay[None], time_first[None], numerator_state, denominator_state, exponent_offset_state]
    )
    vectors = (ln1_gain, ln1_bias, mix_key, mix_value, mix_recept, ln2_gain, ln2_bias, mix2_key, mix2_recept)
    vectors = jnp.concatenate([item[None] for item in vectors] + [prev_att, prev_ffn, jnp.zeros((3, width), F32)])

    quarter = 2 * core + (place // 2) % 2
    projections = jnp.stack(
        [part_of(item, quarter, 4) for item in (key_weight, value_weight, receptance_weight)]
        + [part_of(output_weight, quarter, 4).reshape(-1, 2, half).swapaxes(0, 1).reshape(-1, half)]
    )
    def segment_spec(index=lambda i: i):
        return pl.BlockSpec((None, block, width), lambda i, meta: (meta[0], index(i), 0))

    def rows_spec(columns, index=lambda i: i):
        return pl.BlockSpec((block, columns), lambda i, *_: (index(i), 0))

    def stack_spec(count, columns, index=lambda i: i, size_of=block):
        return pl.BlockSpec((count, size_of, columns), lambda i, *_: (0, index(i), 0))

    def bound_spec(index=lambda i: i):
        return pl.BlockSpec((1, 8, width), lambda i, *_: (index(i), 0, 0))

    def back(i):
        return blocks - 1 - i

    def shape(dims, kind):
        return jax.ShapeDtypeStruct(dims, kind)

    scan_shapes = [
        shape((length, half), BF16), shape((7, length, half), F32),
        shape((2, length // STEP, half), F32), shape((8, half), F32),
    ]
    scan_specs = [rows_spec(half), stack_spec(7, half), stack_spec(2, half, size_of=chunks), whole((8, half))]
    scan_scratch = [
        pltpu.VMEM((block, half), F32), pltpu.VMEM((8, half), F32), pltpu.VMEM((4, chunks + 8, half), F32),
    ]
    mix1, bounds1, last_att, gated_own, save_own, start_own, final_own = pl.pallas_call(
        first_kernel,
        grid_spec=pltpu.PrefetchScalarGridSpec(
            num_scalar_prefetch=1,
            grid=(blocks,),
            in_specs=[segment_spec(), whole((16, width))] + [whole((width, half))] * 3 + [whole((8, half))],
            out_specs=[stack_spec(3, width), bound_spec(), whole((1, width))] + scan_specs,
            scratch_shapes=scan_scratch + [pltpu.VMEM((1, width), F32)],
        ),
        out_shape=[
            shape((3, length, width), BF16), shape((blocks, 8, width), F32), shape((1, width), F32),
        ] + scan_shapes,
        compiler_params=params(48),
        name="time_mix_own",
    )(meta, tokens, vectors, key_weight, value_weight, receptance_weight, own_channels)

    channel_weights, mix1 = together(
        (channel_key_weight, channel_receptance_weight, channel_value_weight), mix1
    )
    ckr_part = jnp.concatenate([part_of(item, quarter, 4) for item in channel_weights[:2]], axis=1)
    proj_one, far_channels, mix1, ckr_part, cv_weight = together(
        swapped(projections), swapped(own_channels), mix1, ckr_part, channel_weights[2]
    )
    cut = units // 2 * 5 // 8
    start = core * (units // 2)
    cv_parts = [
        lax.dynamic_slice_in_dim(cv_weight, start, cut, 0),
        lax.dynamic_slice_in_dim(cv_weight, start + cut, units // 2 - cut, 0),
    ]
    proj_two, proj_three, ckr_one, cv_parts = together(
        crossed(proj_one, size, 2), crossed(proj_one, size, 1), swapped(ckr_part), cv_parts
    )
    proj_four, ckr_three, ckr_one, mix1, cv_parts = together(
        crossed(proj_two, size, 1), crossed(ckr_one, size, 1), ckr_one, mix1, cv_parts
    )
    ckr_two = crossed(ckr_one, size, 2)
    cv_near = swapped(cv_parts[0])
    far_kvr, wo_far, gated_far, save_far, start_far, final_far = pl.pallas_call(
        second_kernel,
        grid_spec=pltpu.PrefetchScalarGridSpec(
            num_scalar_prefetch=1,
            grid=(blocks,),
            in_specs=[stack_spec(3, width)] + [whole((4, width // 4, half))] * 4 + [whole((8, half))],
            out_specs=[whole((3, width, half)), whole((half, width))] + scan_specs,
            scratch_shapes=scan_scratch,
        ),
        out_shape=[shape((3, width, half), BF16), shape((half, width), BF16)] + scan_shapes,
        compiler_params=params(48),
        name="time_mix_far",
    )(meta, mix1, proj_one, proj_two, proj_three, proj_four, far_channels)

    middle, mix2, bounds2, last_ffn = pl.pallas_call(
        middle_kernel,
        grid_spec=pltpu.PrefetchScalarGridSpec(
            num_scalar_prefetch=1,
            grid=(blocks,),
            in_specs=[segment_spec(), rows_spec(half), rows_spec(half)]
            + [whole((half, width))] * 2 + [whole((16, width))],
            out_specs=[rows_spec(width), stack_spec(2, width), bound_spec(), whole((1, width))],
            scratch_shapes=[pltpu.VMEM((1, width), F32)],
        ),
        out_shape=[
            shape((length, width), F32), shape((2, length, width), BF16),
            shape((blocks, 8, width), F32), shape((1, width), F32),
        ],
        compiler_params=params(48),
        name="middle",
    )(meta, tokens, gated_own, gated_far, output_weight, wo_far, vectors)
    ckr_two, cv_near, mix2, cv_rest = together(ckr_two, cv_near, mix2, cv_parts[1])
    h_own, own_values = pl.pallas_call(
        hidden_kernel,
        grid=(units // HIDDEN,),
        in_specs=[
            pl.BlockSpec((None, length, width), lambda j: (0, 0, 0)),
            pl.BlockSpec((width, HIDDEN), lambda j: (0, j)),
            pl.BlockSpec((HIDDEN, width), lambda j: (j, 0)),
        ],
        out_specs=[pl.BlockSpec((length, HIDDEN), lambda j: (0, j)), whole((length, width))],
        out_shape=[shape((length, units), BF16), shape((length, width), F32)],
        compiler_params=params(48),
        name="hidden_own",
    )(mix2, channel_key_weight, channel_value_weight)
    ckr_four, cv_next, cv_other, own_values = together(
        crossed(ckr_two, size, 1), swapped(cv_rest), crossed(cv_near, size, 1), own_values
    )
    cv_last = crossed(cv_next, size, 1)

    count = units // HIDDEN
    key_steps = halving_steps(size, (1, 0, 2, 4, 8))
    value_steps = halving_steps(size, (1, 2, 0, 4, 8))

    def own_tile(step):
        return jnp.clip(step - 2 * count, 0, count - 1)

    def out_tile(step, *_):
        step = jnp.maximum(step - count, 0)
        return (step // count, 0, step % count)

    part_shape = pltpu.HBM((2, width // 2, units), BF16)
    part_spec = pl.BlockSpec((1, width // 2, HIDDEN), out_tile)
    (
        mixed_own, mixed_far, rec_own, rec_far, cr, d_key, key_send, key_keep, value_send, value_keep,
    ) = pl.pallas_call(
        functools.partial(
            channel_kernel, [halving_order(size, steps) for steps in (key_steps, value_steps)], groups, block
        ),
        grid_spec=pltpu.PrefetchScalarGridSpec(
            num_scalar_prefetch=1,
            grid=(3 * count,),
            in_specs=[
                pl.BlockSpec(
                    (None, length, width), lambda step, meta: (meta[0], 0, 0), pipeline_mode=pl.Buffered(1)
                ),
                whole((length, width)), whole((2, length, width)), whole((length, width)),
                pl.BlockSpec((length, HIDDEN), lambda step, meta: (0, own_tile(step))),
                pl.BlockSpec((width, HIDDEN), lambda step, meta: (0, own_tile(step))),
                pl.BlockSpec((HIDDEN, width), lambda step, meta: (own_tile(step), 0)),
                whole((width, half)),
            ] + [whole((width // 4, units + half))] * 4 + [
                whole((cut, width)), whole((units // 2 - cut, width)),
                whole((cut, width)), whole((units // 2 - cut, width)),
            ],
            out_specs=[whole((length, half))] * 4 + [whole((width, width)), whole((length, width))] + [part_spec] * 4,
            scratch_shapes=[
                pltpu.VMEM((width, units), BF16), pltpu.VMEM((units, width), BF16), pltpu.VMEM((length, units), BF16),
                pltpu.VMEM((length, width), F32), pltpu.VMEM((length, width), BF16),
            ] + [pltpu.VMEM((width, length), BF16)] * 3,
        ),
        out_shape=[shape_of((length, half), BF16)] * 4
        + [shape_of((width, width), BF16), shape_of((length, width), F32)] + [part_shape] * 4,
        compiler_params=params(62),
        name="channel_mix",
    )(
        meta, cotangent, middle, mix2, own_values, h_own, channel_key_weight, channel_value_weight,
        channel_receptance_weight, ckr_one, ckr_two, ckr_three, ckr_four, cv_near, cv_next, cv_other, cv_last,
    )
    a_sum = Halving(key_send, key_keep, size, key_steps, groups)
    b_sum = Halving(value_send, value_keep, size, value_steps, groups)

    d_middle, d_att, dg_own, dg_far, sums2 = pl.pallas_call(
        middle_back_kernel,
        grid_spec=pltpu.PrefetchScalarGridSpec(
            num_scalar_prefetch=1,
            grid=(blocks,),
            in_specs=[
                segment_spec(back), rows_spec(width, back), rows_spec(width, back), rows_spec(half, back),
                rows_spec(half, back), whole((width, width)), bound_spec(back), whole((16, width)),
                whole((half, width)), whole((half, width)),
            ],
            out_specs=[
                rows_spec(width, back), rows_spec(width, back), rows_spec(half, back), rows_spec(half, back),
                whole((8, width)),
            ],
            scratch_shapes=[pltpu.VMEM((1, width), F32)],
        ),
        out_shape=[
            shape_of((length, width), F32), shape_of((length, width), BF16),
            shape_of((length, half), F32), shape_of((length, half), F32), shape((8, width), F32),
        ],
        compiler_params=params(48),
        name="middle_back",
    )(*in_hbm(meta, cotangent, middle, d_key, rec_own, rec_far, cr, bounds2, vectors, output_weight, wo_far))

    def scan_back(grads, saved, starts, channels):
        return pl.pallas_call(
            scan_back_kernel,
            grid=(blocks,),
            in_specs=[
                rows_spec(half, back), stack_spec(7, half, back),
                stack_spec(2, half, back, size_of=chunks), whole((8, half)),
            ],
            out_specs=[stack_spec(3, half, back), whole((8, half))],
            out_shape=[shape((3, length, half), BF16), shape((8, half), F32)],
            scratch_shapes=[pltpu.VMEM((block, half), F32)] * 3
            + [pltpu.VMEM((8, half), F32), pltpu.VMEM((5, chunks + 8, half), F32)],
            compiler_params=params(48),
            name="scan_back",
        )(grads, saved, starts, channels)

    def round_of(parts, extra, keep, join=False, pin=0):
        gots, sends, extra, keep = together(
            [item.exchange() for item in parts], [(item.send, item.keep) for item in parts], extra, keep
        )
        for item, (send, kept) in zip(parts, sends):
            item.send, item.keep = send, kept
        return add_all(parts, gots, join, pin), extra, keep

    def active(*items):
        return [item for item in items if item.steps]

    def gradients(steps, arrays, tasks, name):
        steps = halving_steps(size, steps)
        send, keep = weight_gradient(halving_order(size, steps), groups, meta, arrays, tasks, name)
        return Halving(send, keep, size, steps, groups)

    c_sum = gradients(
        (1, 4, 8, 2, 0), [d_att, gated_far, gated_own, mix2, rec_far, rec_own],
        [((0, None), (1, None), (2, None)), ((3, 1), (4, None), (5, None))], "output_gradients",
    )
    _, (mixed_in, c_sum.send, c_sum.keep), dgs = round_of(
        active(a_sum, b_sum), (swapped(mixed_far), c_sum.send, c_sum.keep), (dg_far, dg_own), pin=2
    )
    d_far, channel_sums_far = scan_back(dgs[0], save_far, start_far, far_channels)
    d_own, channel_sums_own = scan_back(dgs[1], save_own, start_own, own_channels)
    d_sum = gradients(
        (1, 2, 4, 8, 0), [mix1, d_far, d_own], [((0, n), (1, n), (2, n)) for n in range(3)], "projection_gradients"
    )
    _, (d_sum.send, d_sum.keep), d_middle = round_of(
        active(a_sum, b_sum, c_sum), (d_sum.send, d_sum.keep), d_middle, pin=2
    )
    grad_part, sums1 = pl.pallas_call(
        last_kernel,
        grid_spec=pltpu.PrefetchScalarGridSpec(
            num_scalar_prefetch=1,
            grid=(blocks,),
            in_specs=[
                segment_spec(back), rows_spec(width, back), stack_spec(3, half, back), stack_spec(3, half, back),
                whole((width, half)), whole((width, half)), whole((width, half)), whole((3, width, half)),
                bound_spec(back), whole((16, width)),
            ],
            out_specs=[rows_spec(width, back), whole((8, width))],
            scratch_shapes=[pltpu.VMEM((1, width), F32)],
        ),
        out_shape=[shape((length, width), BF16), shape((8, width), F32)],
        compiler_params=params(48),
        name="time_mix_back",
    )(
        meta, tokens, d_middle, d_own, d_far, key_weight, value_weight, receptance_weight, far_kvr,
        bounds1, vectors,
    )

    def both(own, far):
        return jnp.where(side == 0, jnp.stack([own, far]), jnp.stack([far, own]))

    def full(own, far):
        return jnp.where(side == 0, jnp.concatenate([own, far]), jnp.concatenate([far, own]))

    small = jnp.concatenate([
        sums1[0:2], sums2[0:2], sums1[2:5], sums2[2:4],
        jnp.stack([full(channel_sums_own[n], channel_sums_far[n]) for n in range(2)]),
    ])
    last_rows = jnp.concatenate([last_att, last_ffn])
    (ab_sum, *_), (grad_part, small), (last_rows, final_far) = round_of(
        active(a_sum, b_sum, c_sum, d_sum), (grad_part, small), (last_rows, final_far), True, 1
    ) if groups > 1 else ([a_sum], (grad_part, small), (last_rows, final_far))
    first, second = grad_part[: length // 2], grad_part[length // 2 :]

    def live():
        return active(ab_sum, c_sum, d_sum)

    def small_parts(bits):
        return [crossed(small, size, bit) if bit else swapped(small) for bit in bits]

    _, (first_in, got), (second, last_rows, final_far) = round_of(
        live(), (swapped(first), small_parts([1])), (second, last_rows, final_far)
    )
    small = small + got[0]
    _, (second_in, got), (last_rows, final_far) = round_of(
        live(), (swapped(second), small_parts([2])), (last_rows, final_far)
    )
    small = small + got[0]
    _, (last_in, back_states, got), _ = round_of(
        live(), (swapped(last_rows), swapped(final_far), small_parts([0])), ()
    )
    small = small + got[0]
    bit = 4
    while bit < size:
        pair = bit * 2 < size
        _, got, _ = round_of(live(), small_parts([bit, 2 * bit, 3 * bit] if pair else [bit]), ())
        small = small + got[0]
        if pair:
            small = small + (got[1] + got[2])
        bit *= 4
    while live():
        round_of(live(), (), ())
    grad_tokens = both(grad_part, jnp.concatenate([first_in, second_in])).astype(F32)
    mixed_out = both(mixed_own, mixed_in)
    finals = [both(final_own[n], back_states[n]) for n in range(3)]
    last_rows = both(last_rows, last_in)
    g_ck, g_cv = (a_sum.result(), b_sum.result()) if groups == 1 else ab_sum.result()
    g_other, g_kvr = c_sum.result(), d_sum.result()
    return (
        (mixed_out, grad_tokens, *finals, last_rows[:, 0], last_rows[:, 1])
        + tuple(small[n] for n in range(11))
        + tuple(g_kvr[:, n * half : (n + 1) * half] for n in range(3))
        + (g_other[:, :half].T, g_ck, g_other[:, half:], g_cv.T)
    )


def solution(mesh):
    split = P("dp", "tensor")
    turned = P("tensor", "dp")
    return jax.shard_map(
        functools.partial(shards, mesh.shape["dp"]),
        mesh=mesh,
        in_specs=(P("dp"), P("dp"), P("dp"), P("dp"), split, split, split)
        + (P(),) * 9
        + (P("tensor"), P("tensor"))
        + (P(None, "tensor"),) * 3
        + (P("tensor"), P(None, "tensor"), P(None, "tensor"), P("tensor")),
        out_specs=(P("dp", None, "tensor"), P("dp"), split, split, split, P("dp"), P("dp"))
        + (P(),) * 11
        + (split, split, split, turned, split, split, turned),
        check_vma=False,
    )
```

```python
import functools

import jax
import jax.numpy as jnp
from jax import lax
from jax.experimental import pallas as pl
from jax.experimental.pallas import tpu as pltpu
from jax.sharding import PartitionSpec as P

F32 = jnp.float32
BF16 = jnp.bfloat16
STEP = 8
MIB = 1 << 20
HIDDEN = 512


def nn(left, right):
    return jnp.dot(left, right, preferred_element_type=F32)


def nt(left, right):
    return lax.dot_general(left, right, (((1,), (1,)), ((), ())), preferred_element_type=F32)


def sigmoid(x):
    return 1.0 / (1.0 + jnp.exp(-x))


def row_sum(x):
    return jnp.sum(x, axis=0, keepdims=True)


def lane_mean(x):
    return jnp.mean(x, axis=-1, keepdims=True)


def normalize(x):
    center = x - lane_mean(x)
    scale = lax.rsqrt(lane_mean(center * center) + 1e-05)
    return center * scale, scale


def order_matrix(count, turned=False):
    chunks = count // STEP
    row = lax.broadcasted_iota(jnp.int32, (count, count), 1 if turned else 0)
    token = lax.broadcasted_iota(jnp.int32, (count, count), 0 if turned else 1)
    return (token == (row % chunks) * STEP + row // chunks).astype(BF16)


def row_before(x, first):
    chunks = x.shape[0] // STEP
    ends = x[-chunks:, :]
    rows = lax.broadcasted_iota(jnp.int32, ends.shape, 0)
    head = jnp.where(rows == 0, first, pltpu.roll(ends, 1, 0))
    return jnp.concatenate([head, x[:-chunks, :]])


def row_after(x, last):
    chunks = x.shape[0] // STEP
    starts = x[:chunks, :]
    rows = lax.broadcasted_iota(jnp.int32, starts.shape, 0)
    tail = jnp.where(rows == chunks - 1, last, pltpu.roll(starts, chunks - 1, 0))
    return jnp.concatenate([x[chunks:, :], tail])


def put_quarters(meta, target, pieces):
    core, side = meta[1] % 2, (meta[1] // 2) % 2
    rows = target.shape[-2] // 4
    spots = (2 * core + side, 2 * core + 1 - side, 2 - 2 * core + side, 3 - 2 * core - side)
    for spot, piece in zip(spots, pieces):
        at = pl.ds(pl.multiple_of(spot * rows, rows), rows)
        if len(target.shape) == 3:
            target[:, at, :] = piece[...]
        else:
            target[at, :] = piece[...]


def put_halves(meta, target, mine, other):
    core = meta[1] % 2
    half = target.shape[0] // 2
    for start, pieces in ((core * half, mine), ((1 - core) * half, other)):
        for piece in pieces:
            rows = piece.shape[0]
            target[pl.ds(pl.multiple_of(start, 16), rows), :] = piece[...]
            start = start + rows


def wkv_forward(segment, first_block, k_ref, channel_ref, save_ref, start_ref, final_ref, carry, work):
    chunks = start_ref.shape[1]
    rate = jnp.exp(channel_ref[0:1, :])
    boost = channel_ref[1:2, :]

    @pl.when(first_block)
    def _():
        for n in range(3):
            carry[n : n + 1, :] = channel_ref[pl.ds(2 + 2 * n + segment, 1), :]

    def keys(step):
        return k_ref[step * chunks : (step + 1) * chunks, :]

    peak = keys(STEP - 1)
    for step in range(STEP - 1):
        peak = jnp.maximum(peak, keys(step) - (STEP - 1.0 - step) * rate)
    number = jnp.zeros_like(peak)
    weight = jnp.zeros_like(peak)
    for step in range(STEP):
        part = jnp.exp(keys(step) - (STEP - 1.0 - step) * rate - peak)
        number = number + part * save_ref[0, step * chunks : (step + 1) * chunks, :]
        weight = weight + part
    work[0, 0:chunks, :] = peak
    top = carry[2:3, :]
    for chunk in range(chunks):
        work[1, chunk : chunk + 1, :] = top
        top = jnp.maximum(top - STEP * rate, work[0, chunk : chunk + 1, :])
    work[1, chunks : chunks + 1, :] = top
    tops = work[1, 0:chunks, :]
    later = work[1, 1 : chunks + 1, :]
    fresh = jnp.exp(peak - later)
    work[0, 0:chunks, :] = jnp.exp(tops - STEP * rate - later)
    work[2, 0:chunks, :] = fresh * number
    work[3, 0:chunks, :] = fresh * weight
    num = carry[0:1, :]
    den = carry[1:2, :]
    for chunk in range(chunks):
        at = slice(chunk, chunk + 1)
        start_ref[0, at, :] = num
        start_ref[1, at, :] = den
        num = work[0, at, :] * num + work[2, at, :]
        den = work[0, at, :] * den + work[3, at, :]
    carry[0:1, :] = num
    carry[1:2, :] = den
    carry[2:3, :] = top
    final_ref[0:3, :] = carry[0:3, :]

    num = start_ref[0, :, :]
    den = start_ref[1, :, :]
    top = tops
    for step in range(STEP):
        at = slice(step * chunks, (step + 1) * chunks)
        key = keys(step)
        value = save_ref[0, at, :]
        gap = top - (boost + key)
        small = jnp.exp(-jnp.abs(gap))
        state_wins = gap > 0
        old = jnp.where(state_wins, 1.0, small)
        now = jnp.where(state_wins, small, 1.0)
        inverse = 1.0 / (old * den + now)
        old = old * inverse
        now = now * inverse
        save_ref[1, at, :] = old * num + now * value
        save_ref[3, at, :] = old
        save_ref[4, at, :] = now
        faded = top - rate
        gap = faded - key
        small = jnp.exp(-jnp.abs(gap))
        state_wins = gap > 0
        keep = jnp.where(state_wins, 1.0, small)
        fresh = jnp.where(state_wins, small, 1.0)
        save_ref[5, at, :] = keep
        save_ref[6, at, :] = fresh
        num = keep * num + fresh * value
        den = keep * den + fresh
        top = jnp.maximum(faded, key)


def project_and_scan(segment, inputs, weights, channel_ref, gated_ref, save_ref, start_ref, final_ref, k_ref, carry, work):
    k_ref[...] = nn(inputs[0], weights[0])
    save_ref[0, :, :] = nn(inputs[1], weights[1])
    gate = sigmoid(nn(inputs[2], weights[2]))
    save_ref[2, :, :] = gate
    wkv_forward(segment, pl.program_id(0) == 0, k_ref, channel_ref, save_ref, start_ref, final_ref, carry, work)
    gated_ref[...] = (gate * save_ref[1, :, :]).astype(BF16)


def first_kernel(
    meta, tokens_ref, vector_ref, wk_ref, wv_ref, wr_ref, channel_ref,
    mix_ref, bound_ref, last_ref, gated_ref, save_ref, start_ref, final_ref,
    k_ref, carry, work, row,
):
    @pl.when(pl.program_id(0) == 0)
    def _():
        row[...] = vector_ref[pl.ds(9 + meta[0], 1), :]

    tokens = nn(order_matrix(tokens_ref.shape[0]), tokens_ref[...])
    hat, _ = normalize(tokens)
    normed = hat * vector_ref[0:1, :] + vector_ref[1:2, :]
    first = row[...]
    bound_ref[0, :, :] = jnp.broadcast_to(first, bound_ref.shape[1:])
    before = row_before(normed, first)
    step = normed - before
    count = normed.shape[0]
    row[...] = normed[count - 1 : count, :]
    last_ref[...] = normed[count - 1 : count, :]
    mixed = [(before + step * vector_ref[2 + n : 3 + n, :]).astype(BF16) for n in range(3)]
    for n in range(3):
        mix_ref[n, :, :] = mixed[n]
    project_and_scan(
        meta[0], mixed, (wk_ref[...], wv_ref[...], wr_ref[...]), channel_ref,
        gated_ref, save_ref, start_ref, final_ref, k_ref, carry, work,
    )


def second_kernel(
    meta, mix_ref, one_ref, two_ref, three_ref, four_ref, channel_ref,
    weight_ref, wo_ref, gated_ref, save_ref, start_ref, final_ref, k_ref, carry, work,
):
    @pl.when(pl.program_id(0) == 0)
    def _():
        pieces = (one_ref, two_ref, three_ref, four_ref)
        put_quarters(meta, weight_ref, [piece.at[0:3] for piece in pieces])
        rows, half = wo_ref.shape[0] // 4, weight_ref.shape[2]
        for n in range(2):
            put_quarters(
                meta, wo_ref.at[:, n * half : (n + 1) * half],
                [piece.at[3, n * rows : (n + 1) * rows, :] for piece in pieces],
            )

    project_and_scan(
        meta[0], [mix_ref[n, :, :] for n in range(3)], [weight_ref[n, :, :] for n in range(3)], channel_ref,
        gated_ref, save_ref, start_ref, final_ref, k_ref, carry, work,
    )


def middle_kernel(
    meta, tokens_ref, own_ref, far_ref, wo_own_ref, wo_far_ref, vector_ref,
    middle_ref, mix_ref, bound_ref, last_ref, row,
):
    @pl.when(pl.program_id(0) == 0)
    def _():
        row[...] = vector_ref[pl.ds(11 + meta[0], 1), :]

    middle = (
        nn(order_matrix(tokens_ref.shape[0]), tokens_ref[...])
        + nn(own_ref[...], wo_own_ref[...])
        + nn(far_ref[...], wo_far_ref[...])
    )
    middle_ref[...] = middle
    hat, _ = normalize(middle)
    normed = hat * vector_ref[5:6, :] + vector_ref[6:7, :]
    first = row[...]
    bound_ref[0, :, :] = jnp.broadcast_to(first, bound_ref.shape[1:])
    before = row_before(normed, first)
    step = normed - before
    count = normed.shape[0]
    row[...] = normed[count - 1 : count, :]
    last_ref[...] = normed[count - 1 : count, :]
    for n in range(2):
        mix_ref[n, :, :] = (before + step * vector_ref[7 + n : 8 + n, :]).astype(BF16)


def norm_backward(x, vectors, bound, grads, weights, row, sums_ref):
    gain, bias = vectors
    hat, scale = normalize(x)
    normed = hat * gain + bias
    step = normed - row_before(normed, bound)
    total = grads[0]
    current = grads[0] * weights[0]
    sums_ref[2:3, :] += row_sum(grads[0] * step)
    for n in range(1, len(grads)):
        total = total + grads[n]
        current = current + grads[n] * weights[n]
        sums_ref[2 + n : 3 + n, :] += row_sum(grads[n] * step)
    shifted = total - current
    flow = current + row_after(shifted, row[...])
    row[...] = shifted[0:1, :]
    sums_ref[0:1, :] += row_sum(flow * hat)
    sums_ref[1:2, :] += row_sum(flow)
    inner = flow * gain
    return scale * (inner - lane_mean(inner) - hat * lane_mean(inner * hat))


def hidden_kernel(mix_ref, ck_ref, cv_ref, hidden_ref, values_ref):
    relu = jnp.maximum(nn(mix_ref[...], ck_ref[...]), 0.0)
    hidden = (relu * relu).astype(BF16)
    hidden_ref[...] = hidden
    part = nn(hidden, cv_ref[...])

    @pl.when(pl.program_id(0) == 0)
    def _():
        values_ref[...] = part

    @pl.when(pl.program_id(0) > 0)
    def _():
        values_ref[...] += part


def turn_rows(meta, order, groups, source, turned, placed):
    whole = turned.shape[0]
    target = turned if groups > 1 else placed
    for col in range(0, whole, 128):
        target[col : col + 128, :] = source[:, col : col + 128].T
    if groups > 1:
        rows = whole // groups
        for spot, other in enumerate(order):
            start = pl.multiple_of((meta[1] ^ other) * rows, rows)
            placed[spot * rows : (spot + 1) * rows, :] = turned[pl.ds(start, rows), :]


def channel_kernel(
    orders, groups, block, meta, cot_hbm, middle_hbm, mix_hbm, own_values_hbm, hidden_ref, ck_ref, cv_ref, cr_hbm,
    one_hbm, two_hbm, three_hbm, four_hbm, near_hbm, next_hbm, other_hbm, last_hbm,
    mixed_own_ref, mixed_far_ref, rec_own_ref, rec_far_ref, cr_ref, d_key_ref,
    key_send_ref, key_keep_ref, value_send_ref, value_keep_ref,
    ck_far_ref, cv_far_ref, h_far_ref, values_ref, d_values_ref, turned_ref, key_turned_ref, value_turned_ref,
    cot_ref, middle_ref, mix_ref, sems,
):
    step = pl.program_id(0)
    tile = hidden_ref.shape[1]
    units = ck_far_ref.shape[1]
    count = units // tile
    length, width = values_ref.shape
    half = cr_hbm.shape[1]
    core, side = meta[1] % 2, (meta[1] // 2) % 2
    far_at = pl.ds(pl.multiple_of((1 - meta[0]) * half, 128), half)
    own_at = pl.ds(pl.multiple_of(meta[0] * half, 128), half)
    quarter = width // 4
    spots = (2 * core + side, 2 * core + 1 - side, 2 - 2 * core + side, 3 - 2 * core - side)
    at = [pl.ds(pl.multiple_of(spot * quarter, quarter), quarter) for spot in spots]
    pieces = (one_hbm, two_hbm, three_hbm, four_hbm)
    pairs = [(mix_hbm.at[0], mix_ref.at[0])]
    pairs += [(piece.at[:, 0:units], ck_far_ref.at[rows, :]) for piece, rows in zip(pieces, at)]
    for start, parts in ((core, (near_hbm, next_hbm)), (1 - core, (other_hbm, last_hbm))):
        start = start * (units // 2)
        for part in parts:
            rows = part.shape[0]
            pairs.append((part, cv_far_ref.at[pl.ds(pl.multiple_of(start, 16), rows), :]))
            start = start + rows
    pairs += [(own_values_hbm, values_ref), (mix_hbm.at[1], mix_ref.at[1]), (cr_hbm, cr_ref.at[:, own_at])]
    pairs += [(piece.at[:, units : units + half], cr_ref.at[rows, far_at]) for piece, rows in zip(pieces, at)]
    pairs += [(middle_hbm, middle_ref), (cot_hbm.at[meta[0]], cot_ref)]
    copies = [pltpu.make_async_copy(source, target, sems.at[n]) for n, (source, target) in enumerate(pairs)]

    def far_forward(index):
        at = slice(index * tile, (index + 1) * tile)
        if index == 0:
            for item in copies[:10]:
                item.start()
            for item in copies[:5]:
                item.wait()
        relu = jnp.maximum(nn(mix_ref[0, :, :], ck_far_ref[:, at]), 0.0)
        hidden = (relu * relu).astype(BF16)
        h_far_ref[:, at] = hidden
        if index == 0:
            for item in copies[5:10]:
                item.wait()
        values_ref[...] += nn(hidden, cv_far_ref[at, :])
        if index == 0:
            for item in copies[10:]:
                item.start()
            turn_rows(meta, orders[0], groups, mix_ref.at[0], turned_ref, key_turned_ref)
        if index == count - 1:
            for item in copies[10:]:
                item.wait()

    for index in range(count):
        pl.when(step == index)(functools.partial(far_forward, index))

    @pl.when(step == count - 1)
    def _():
        def rows_of(n, _):
            at = pl.ds(pl.multiple_of(n * block, block), block)
            values = values_ref[at, :]
            gate = sigmoid(nn(mix_ref[1, at, :], cr_ref[...]))
            mixed = (middle_ref[at, :] + gate * values).astype(BF16)
            mixed = nn(order_matrix(block, True), mixed)
            low, high = mixed[:, :half], mixed[:, half:]
            mixed_own_ref[at, :] = jnp.where(meta[0] == 0, low, high).astype(BF16)
            mixed_far_ref[at, :] = jnp.where(meta[0] == 0, high, low).astype(BF16)
            passed = nn(order_matrix(block), cot_ref[at, :]) * gate
            d_values_ref[at, :] = passed.astype(BF16)
            d_rec = passed * values * (1.0 - gate)
            low, high = d_rec[:, :half], d_rec[:, half:]
            rec_own_ref[at, :] = jnp.where(meta[0] == 0, low, high).astype(BF16)
            rec_far_ref[at, :] = jnp.where(meta[0] == 0, high, low).astype(BF16)
            return 0

        lax.fori_loop(0, length // block, rows_of, 0)
        turn_rows(meta, orders[1], groups, d_values_ref, turned_ref, value_turned_ref)
        d_key_ref[...] = jnp.zeros_like(d_key_ref)

    def backward(hidden, ck, cv):
        slope = 2.0 * jnp.sqrt(hidden.astype(F32))
        d_pre = (slope * nt(d_values_ref[...], cv)).astype(BF16)
        d_key_ref[...] += nt(d_pre, ck)
        for turned, right, send_ref, keep_ref in (
            (value_turned_ref, hidden, value_send_ref, value_keep_ref),
            (key_turned_ref, d_pre, key_send_ref, key_keep_ref),
        ):
            part = nn(turned[...], right).astype(BF16)
            keep_ref[0, :, :] = part[: width // 2, :]
            send_ref[0, :, :] = part[width // 2 :, :]

    @pl.when((step >= count) & (step < 2 * count))
    def _():
        at = pl.ds(pl.multiple_of((step - count) * tile, tile), tile)
        backward(h_far_ref[:, at], ck_far_ref[:, at], cv_far_ref[at, :])

    @pl.when(step >= 2 * count)
    def _():
        backward(hidden_ref[...], ck_ref[...], cv_ref[...])


def middle_back_kernel(
    meta, cot_ref, middle_ref, d_key_ref, rec_own_ref, rec_far_ref, cr_ref, bound_ref, vector_ref, wo_own_ref, wo_far_ref,
    dmid_ref, datt_ref, dg_own_ref, dg_far_ref, sums_ref, row,
):
    @pl.when(pl.program_id(0) == 0)
    def _():
        row[...] = jnp.zeros_like(row)
        sums_ref[...] = jnp.zeros_like(sums_ref)

    half = rec_own_ref.shape[1]
    own, far = rec_own_ref[...], rec_far_ref[...]
    low, high = jnp.where(meta[0] == 0, own, far), jnp.where(meta[0] == 0, far, own)
    d_recept = nt(low, cr_ref[:, :half]) + nt(high, cr_ref[:, half:])
    grad = nn(order_matrix(cot_ref.shape[0]), cot_ref[...])
    d_middle = grad + norm_backward(
        middle_ref[...], (vector_ref[5:6, :], vector_ref[6:7, :]), bound_ref[0, 0:1, :],
        (d_key_ref[...], d_recept), (vector_ref[7:8, :], vector_ref[8:9, :]), row, sums_ref,
    )
    dmid_ref[...] = d_middle
    d_att = d_middle.astype(BF16)
    datt_ref[...] = d_att
    dg_own_ref[...] = nt(d_att, wo_own_ref[...])
    dg_far_ref[...] = nt(d_att, wo_far_ref[...])


def scan_back_kernel(
    dg_ref, save_ref, start_ref, channel_ref, out_ref, sums_ref, dy_ref, dk_ref, dv_ref, carry, work
):
    chunks = start_ref.shape[1]

    @pl.when(pl.program_id(0) == 0)
    def _():
        carry[...] = jnp.zeros_like(carry)
        sums_ref[...] = jnp.zeros_like(sums_ref)

    gate = save_ref[2, :, :]
    dy = dg_ref[...] * gate
    dy_ref[...] = dy
    out_ref[2, :, :] = (dy * save_ref[1, :, :] * (1.0 - gate)).astype(BF16)

    def at(step):
        return slice(step * chunks, (step + 1) * chunks)

    gn = jnp.zeros((chunks, dy.shape[1]), F32)
    gd = jnp.zeros_like(gn)
    product = jnp.ones_like(gn)
    for step in reversed(range(STEP)):
        part = save_ref[3, at(step), :] * dy_ref[at(step), :]
        keep = save_ref[5, at(step), :]
        gn = part + keep * gn
        gd = keep * gd - part * save_ref[1, at(step), :]
        product = product * keep
    work[0, 0:chunks, :] = gn
    work[1, 0:chunks, :] = gd
    work[2, 0:chunks, :] = product
    gn = carry[0:1, :]
    gd = carry[1:2, :]
    for chunk in reversed(range(chunks)):
        row = slice(chunk, chunk + 1)
        work[3, row, :] = gn
        work[4, row, :] = gd
        gn = work[0, row, :] + work[2, row, :] * gn
        gd = work[1, row, :] + work[2, row, :] * gd
    carry[0:1, :] = gn
    carry[1:2, :] = gd
    work[0, 0:chunks, :] = start_ref[0, :, :]
    work[1, 0:chunks, :] = start_ref[1, :, :]
    work[0, chunks : chunks + 1, :] = carry[2:3, :]
    work[1, chunks : chunks + 1, :] = carry[3:4, :]
    carry[2:3, :] = start_ref[0, 0:1, :]
    carry[3:4, :] = start_ref[1, 0:1, :]
    gn = work[3, 0:chunks, :]
    gd = work[4, 0:chunks, :]
    decay = STEP * (gn * work[0, 1 : chunks + 1, :] + gd * work[1, 1 : chunks + 1, :])
    first = jnp.zeros_like(gn)
    for step in reversed(range(STEP)):
        place = at(step)
        dy = dy_ref[place, :]
        value = save_ref[0, place, :]
        wkv = save_ref[1, place, :]
        share = save_ref[4, place, :] * dy
        bonus = share * (value - wkv)
        fresh = save_ref[6, place, :]
        through = fresh * (gn * value + gd)
        d_key = bonus + through
        dk_ref[place, :] = d_key
        dv_ref[place, :] = share + fresh * gn
        first = first + bonus
        decay = decay - through - float(step) * d_key
        part = save_ref[3, place, :] * dy
        keep = save_ref[5, place, :]
        gn = part + keep * gn
        gd = keep * gd - part * wkv
    sums_ref[0:1, :] -= row_sum(decay) * jnp.exp(channel_ref[0:1, :])
    sums_ref[1:2, :] += row_sum(first)
    out_ref[0, :, :] = dk_ref[...].astype(BF16)
    out_ref[1, :, :] = dv_ref[...].astype(BF16)


def last_kernel(
    meta, tokens_ref, dmid_ref, own_ref, far_ref, wk_ref, wv_ref, wr_ref, weight_ref, bound_ref,
    vector_ref, grad_ref, sums_ref, row,
):
    @pl.when(pl.program_id(0) == 0)
    def _():
        row[...] = jnp.zeros_like(row)
        sums_ref[...] = jnp.zeros_like(sums_ref)

    grads = [
        nt(own_ref[n, :, :], w_ref[...]) + nt(far_ref[n, :, :], weight_ref[n, :, :])
        for n, w_ref in enumerate((wk_ref, wv_ref, wr_ref))
    ]
    part = norm_backward(
        nn(order_matrix(tokens_ref.shape[0]), tokens_ref[...]), (vector_ref[0:1, :], vector_ref[1:2, :]), bound_ref[0, 0:1, :],
        grads, [vector_ref[2 + n : 3 + n, :] for n in range(3)], row, sums_ref,
    )
    grad = (dmid_ref[...] + part).astype(BF16)
    grad_ref[...] = nn(order_matrix(grad.shape[0], True), grad).astype(BF16)


def weight_gradient_kernel(order, groups, tasks, meta, *refs):
    *refs, send_ref, keep_ref, left_buf, right_buf, sems, turned, placed = refs
    step = pl.program_id(0)
    half = right_buf.shape[2] // 2
    whole = turned.shape[0]

    def copies(index):
        pairs = []
        for n, (spot, lead) in enumerate(tasks[index]):
            source = refs[spot] if lead is None else refs[spot].at[lead]
            slot = index % 2
            target = left_buf.at[slot] if n == 0 else right_buf.at[slot, :, (n - 1) * half : n * half]
            pairs.append(pltpu.make_async_copy(source, target, sems.at[slot, n]))
        return pairs

    @pl.when(step == 0)
    def _():
        for item in copies(0):
            item.start()

    for index in range(len(tasks)):
        @pl.when(step == index)
        def _(index=index):
            if index + 1 < len(tasks):
                for item in copies(index + 1):
                    item.start()
            for item in copies(index):
                item.wait()
            slot = index % 2
            turn_rows(meta, order, groups, left_buf.at[slot], turned, placed)
            part = nn(placed[...], right_buf[slot, :, :]).astype(BF16)
            for side in range(2):
                keep_ref[side, :, :] = part[: whole // 2, side * half : (side + 1) * half]
                send_ref[side, :, :] = part[whole // 2 :, side * half : (side + 1) * half]


def in_hbm(*arrays):
    return [
        pltpu.with_memory_space_constraint(item, pltpu.HBM) if item.size > 1 << 16 else item for item in arrays
    ]


def shape_of(dims, kind):
    large = functools.reduce(lambda a, b: a * b, dims) > 1 << 16
    return (pltpu.HBM if large else jax.ShapeDtypeStruct)(dims, kind)


def params(mib, steps=None):
    return pltpu.CompilerParams(vmem_limit_bytes=mib * MIB, dimension_semantics=steps)


def whole(shape):
    return pl.BlockSpec(shape, lambda *_: (0,) * len(shape), pipeline_mode=pl.Buffered(1))


def weight_gradient(order, groups, meta, arrays, tasks, name):
    length, width = arrays[tasks[0][0][0]].shape[-2:]
    half = arrays[tasks[0][1][0]].shape[-1]
    spec = pl.BlockSpec((2, width // 2, half), lambda n, meta: (0, 0, n))
    shape = shape_of((2, width // 2, len(tasks) * half), BF16)
    return pl.pallas_call(
        functools.partial(weight_gradient_kernel, order, groups, tasks),
        grid_spec=pltpu.PrefetchScalarGridSpec(
            num_scalar_prefetch=1,
            grid=(len(tasks),),
            in_specs=[pl.BlockSpec(memory_space=pl.ANY)] * len(arrays),
            out_specs=[spec, spec],
            scratch_shapes=[
                pltpu.VMEM((2, length, width), BF16), pltpu.VMEM((2, length, 2 * half), BF16),
                pltpu.SemaphoreType.DMA((2, 3)),
                pltpu.VMEM((width, length), BF16), pltpu.VMEM((width, length), BF16),
            ],
        ),
        out_shape=[shape, shape],
        compiler_params=params(40),
        name=name,
    )(meta, *arrays)


def together(*trees):
    return lax.optimization_barrier(trees)


def swapped(array):
    return lax.ppermute(array, "tensor", [(0, 1), (1, 0)])


def crossed(array, size, bit):
    return lax.ppermute(array, "dp", [(n, n ^ bit) for n in range(size)])


def added(mine, theirs, kind):
    return (mine.astype(F32) + theirs.astype(F32)).astype(kind)


def part_of(array, part, parts, axis=0):
    rows = array.shape[axis] // parts
    return lax.dynamic_slice_in_dim(array, part * rows, rows, axis)


def halving_steps(size, steps):
    steps = [bit for bit in steps if bit < size]
    known = max(steps)
    while known * 2 < size:
        known *= 2
        steps.append(known)
    return steps


def halving_order(size, steps):
    order = []
    for spot in range(size):
        other = 0
        for bit in reversed([bit for bit in steps if bit]):
            other |= bit * (spot % 2)
            spot //= 2
        order.append(other)
    return order


class Halving:
    def __init__(self, send, keep, size, steps, groups):
        self.size, self.steps, self.groups = size, steps if groups > 1 else [], groups
        self.send, self.keep = (send, keep) if groups > 1 else (None, jnp.concatenate([keep, send], axis=1))

    def exchange(self):
        bit = self.steps[0]
        return crossed(self.send, self.size, bit) if bit else swapped(self.send)

    def result(self):
        if self.groups == 1:
            total = self.keep[1].astype(F32) + swapped(self.keep[0]).astype(F32)
            return lax.psum_scatter(total, "dp", scatter_dimension=0, tiled=True)
        assert not self.steps
        return self.keep


def add_kernel(forms, *refs):
    ins, outs = list(refs[: 2 * len(forms)]), list(refs[2 * len(forms) :])
    for form, lead in forms:
        total = ins.pop(0)[...].astype(F32) + ins.pop(0)[...].astype(F32)
        if lead is not None:
            targets = [ref.at[lead] for ref in (outs[:2] if lead == 0 else done)]
            done, outs = (outs[:2], outs[2:]) if lead == 0 else (done, outs)
        else:
            targets, outs = (outs[:1], outs[1:]) if form == "last" else (outs[:2], outs[2:])
        if form == "last":
            targets[0][...] = total
        elif form == "tensor":
            targets[0][...] = total[0].astype(BF16)
            targets[1][...] = total[1].astype(BF16)
        else:
            rows = total.shape[-2] // 2
            targets[0][...] = total[..., rows:, :].astype(BF16)
            targets[1][...] = total[..., :rows, :].astype(BF16)


def add_all(items, gots, join, pin):
    items = [item for item in items]
    if not items:
        return items
    tiles = 3 if sum(item.keep.size for item in items) > 1 << 20 else 1
    forms, operands, in_specs, shapes, out_specs = [], [], [], [], []

    def spec(dims):
        dims = dims[:-1] + (dims[-1] // tiles,)
        return pl.BlockSpec(dims, lambda n, lead=len(dims) - 1: (0,) * lead + (n,))

    for index, (item, got) in enumerate(zip(items, gots)):
        left = item.steps[1:]
        form = "last" if not left else "tensor" if left[0] == 0 else "rows"
        dims = item.keep.shape
        operands += [*(in_hbm(item.keep) if pin else [item.keep]), got]
        in_specs += [spec(dims)] * 2
        if form == "tensor":
            dims = dims[1:]
        elif form == "rows":
            dims = dims[:-2] + (dims[-2] // 2, dims[-1])
        lead = index if join and index < 2 else None
        forms.append((form, lead))
        if lead == 1:
            continue
        if lead == 0:
            dims = (2,) + dims
        copies = 1 if form == "last" else 2
        kind = pltpu.HBM if pin == 2 else jax.ShapeDtypeStruct
        shapes += [kind(dims, F32 if form == "last" else BF16)] * copies
        out_specs += [spec(dims)] * copies
    outs = list(pl.pallas_call(
        functools.partial(add_kernel, forms),
        grid=(tiles,),
        in_specs=in_specs,
        out_specs=out_specs,
        out_shape=shapes,
        compiler_params=params(32),
        name="sum_parts",
    )(*(in_hbm(*operands) if pin == 1 else operands)))
    rest = []
    for item, (form, lead) in zip(items, forms):
        if lead == 1:
            continue
        item.steps = item.steps[1:]
        item.send = None if form == "last" else outs.pop(0)
        item.keep = outs.pop(0)
        rest.append(item)
    return rest


def shards(
    size, tokens, cotangent, prev_att, prev_ffn, numerator_state, denominator_state, exponent_offset_state,
    ln1_gain, ln1_bias, ln2_gain, ln2_bias, mix_key, mix_value, mix_recept, mix2_key, mix2_recept,
    time_decay, time_first, key_weight, value_weight, receptance_weight, output_weight,
    channel_key_weight, channel_receptance_weight, channel_value_weight,
):
    _, length, width = tokens.shape
    half = key_weight.shape[1]
    units = channel_key_weight.shape[1]
    block = min(256, length)
    blocks = length // block
    chunks = block // STEP
    side = lax.axis_index("tensor")
    place = lax.axis_index("dp")
    core = place % 2
    meta = jnp.stack([side, place]).astype(jnp.int32)
    rows = width // size
    groups = size if rows % 16 == 0 else 1
    own_channels = jnp.concatenate(
        [time_decay[None], time_first[None], numerator_state, denominator_state, exponent_offset_state]
    )
    vectors = (ln1_gain, ln1_bias, mix_key, mix_value, mix_recept, ln2_gain, ln2_bias, mix2_key, mix2_recept)
    vectors = jnp.concatenate([item[None] for item in vectors] + [prev_att, prev_ffn, jnp.zeros((3, width), F32)])

    quarter = 2 * core + (place // 2) % 2
    projections = jnp.stack(
        [part_of(item, quarter, 4) for item in (key_weight, value_weight, receptance_weight)]
        + [part_of(output_weight, quarter, 4).reshape(-1, 2, half).swapaxes(0, 1).reshape(-1, half)]
    )
    def segment_spec(index=lambda i: i):
        return pl.BlockSpec((None, block, width), lambda i, meta: (meta[0], index(i), 0))

    def rows_spec(columns, index=lambda i: i):
        return pl.BlockSpec((block, columns), lambda i, *_: (index(i), 0))

    def stack_spec(count, columns, index=lambda i: i, size_of=block):
        return pl.BlockSpec((count, size_of, columns), lambda i, *_: (0, index(i), 0))

    def bound_spec(index=lambda i: i):
        return pl.BlockSpec((1, 8, width), lambda i, *_: (index(i), 0, 0))

    def back(i):
        return blocks - 1 - i

    def shape(dims, kind):
        return jax.ShapeDtypeStruct(dims, kind)

    scan_shapes = [
        shape((length, half), BF16), shape((7, length, half), F32),
        shape((2, length // STEP, half), F32), shape((8, half), F32),
    ]
    scan_specs = [rows_spec(half), stack_spec(7, half), stack_spec(2, half, size_of=chunks), whole((8, half))]
    scan_scratch = [
        pltpu.VMEM((block, half), F32), pltpu.VMEM((8, half), F32), pltpu.VMEM((4, chunks + 8, half), F32),
    ]
    mix1, bounds1, last_att, gated_own, save_own, start_own, final_own = pl.pallas_call(
        first_kernel,
        grid_spec=pltpu.PrefetchScalarGridSpec(
            num_scalar_prefetch=1,
            grid=(blocks,),
            in_specs=[segment_spec(), whole((16, width))] + [whole((width, half))] * 3 + [whole((8, half))],
            out_specs=[stack_spec(3, width), bound_spec(), whole((1, width))] + scan_specs,
            scratch_shapes=scan_scratch + [pltpu.VMEM((1, width), F32)],
        ),
        out_shape=[
            shape((3, length, width), BF16), shape((blocks, 8, width), F32), shape((1, width), F32),
        ] + scan_shapes,
        compiler_params=params(48),
        name="time_mix_own",
    )(meta, tokens, vectors, key_weight, value_weight, receptance_weight, own_channels)

    channel_weights, mix1 = together(
        (channel_key_weight, channel_receptance_weight, channel_value_weight), mix1
    )
    ckr_part = jnp.concatenate([part_of(item, quarter, 4) for item in channel_weights[:2]], axis=1)
    proj_one, far_channels, mix1, ckr_part, cv_weight = together(
        swapped(projections), swapped(own_channels), mix1, ckr_part, channel_weights[2]
    )
    cut = units // 2 * 5 // 8
    start = core * (units // 2)
    cv_parts = [
        lax.dynamic_slice_in_dim(cv_weight, start, cut, 0),
        lax.dynamic_slice_in_dim(cv_weight, start + cut, units // 2 - cut, 0),
    ]
    proj_two, proj_three, ckr_one, cv_parts = together(
        crossed(proj_one, size, 2), crossed(proj_one, size, 1), swapped(ckr_part), cv_parts
    )
    proj_four, ckr_three, ckr_one, mix1, cv_parts = together(
        crossed(proj_two, size, 1), crossed(ckr_one, size, 1), ckr_one, mix1, cv_parts
    )
    ckr_two = crossed(ckr_one, size, 2)
    cv_near = swapped(cv_parts[0])
    far_kvr, wo_far, gated_far, save_far, start_far, final_far = pl.pallas_call(
        second_kernel,
        grid_spec=pltpu.PrefetchScalarGridSpec(
            num_scalar_prefetch=1,
            grid=(blocks,),
            in_specs=[stack_spec(3, width)] + [whole((4, width // 4, half))] * 4 + [whole((8, half))],
            out_specs=[whole((3, width, half)), whole((half, width))] + scan_specs,
            scratch_shapes=scan_scratch,
        ),
        out_shape=[shape((3, width, half), BF16), shape((half, width), BF16)] + scan_shapes,
        compiler_params=params(48),
        name="time_mix_far",
    )(meta, mix1, proj_one, proj_two, proj_three, proj_four, far_channels)

    middle, mix2, bounds2, last_ffn = pl.pallas_call(
        middle_kernel,
        grid_spec=pltpu.PrefetchScalarGridSpec(
            num_scalar_prefetch=1,
            grid=(blocks,),
            in_specs=[segment_spec(), rows_spec(half), rows_spec(half)]
            + [whole((half, width))] * 2 + [whole((16, width))],
            out_specs=[rows_spec(width), stack_spec(2, width), bound_spec(), whole((1, width))],
            scratch_shapes=[pltpu.VMEM((1, width), F32)],
        ),
        out_shape=[
            shape((length, width), F32), shape((2, length, width), BF16),
            shape((blocks, 8, width), F32), shape((1, width), F32),
        ],
        compiler_params=params(48),
        name="middle",
    )(meta, tokens, gated_own, gated_far, output_weight, wo_far, vectors)
    ckr_two, cv_near, mix2, cv_rest = together(ckr_two, cv_near, mix2, cv_parts[1])
    h_own, own_values = pl.pallas_call(
        hidden_kernel,
        grid=(units // HIDDEN,),
        in_specs=[
            pl.BlockSpec((None, length, width), lambda j: (0, 0, 0)),
            pl.BlockSpec((width, HIDDEN), lambda j: (0, j)),
            pl.BlockSpec((HIDDEN, width), lambda j: (j, 0)),
        ],
        out_specs=[pl.BlockSpec((length, HIDDEN), lambda j: (0, j)), whole((length, width))],
        out_shape=[shape((length, units), BF16), shape((length, width), F32)],
        compiler_params=params(48),
        name="hidden_own",
    )(mix2, channel_key_weight, channel_value_weight)
    ckr_four, cv_next, cv_other, own_values = together(
        crossed(ckr_two, size, 1), swapped(cv_rest), crossed(cv_near, size, 1), own_values
    )
    cv_last = crossed(cv_next, size, 1)

    count = units // HIDDEN
    key_steps = halving_steps(size, (1, 0, 2, 4, 8))
    value_steps = halving_steps(size, (1, 2, 0, 4, 8))

    def own_tile(step):
        return jnp.clip(step - 2 * count, 0, count - 1)

    def out_tile(step, *_):
        step = jnp.maximum(step - count, 0)
        return (step // count, 0, step % count)

    part_shape = pltpu.HBM((2, width // 2, units), BF16)
    part_spec = pl.BlockSpec((1, width // 2, HIDDEN), out_tile)
    (
        mixed_own, mixed_far, rec_own, rec_far, cr, d_key, key_send, key_keep, value_send, value_keep,
    ) = pl.pallas_call(
        functools.partial(
            channel_kernel, [halving_order(size, steps) for steps in (key_steps, value_steps)], groups, block
        ),
        grid_spec=pltpu.PrefetchScalarGridSpec(
            num_scalar_prefetch=1,
            grid=(3 * count,),
            in_specs=[pl.BlockSpec(memory_space=pl.ANY)] * 4 + [
                pl.BlockSpec((length, HIDDEN), lambda step, meta: (0, own_tile(step))),
                pl.BlockSpec((width, HIDDEN), lambda step, meta: (0, own_tile(step))),
                pl.BlockSpec((HIDDEN, width), lambda step, meta: (own_tile(step), 0)),
            ] + [pl.BlockSpec(memory_space=pl.ANY)] * 9,
            out_specs=[whole((length, half))] * 4 + [whole((width, width)), whole((length, width))] + [part_spec] * 4,
            scratch_shapes=[
                pltpu.VMEM((width, units), BF16), pltpu.VMEM((units, width), BF16), pltpu.VMEM((length, units), BF16),
                pltpu.VMEM((length, width), F32), pltpu.VMEM((length, width), BF16),
            ] + [pltpu.VMEM((width, length), BF16)] * 3 + [
                pltpu.VMEM((length, width), BF16), pltpu.VMEM((length, width), F32),
                pltpu.VMEM((2, length, width), BF16), pltpu.SemaphoreType.DMA((18,)),
            ],
        ),
        out_shape=[shape_of((length, half), BF16)] * 4
        + [shape_of((width, width), BF16), shape_of((length, width), F32)] + [part_shape] * 4,
        compiler_params=params(62),
        name="channel_mix",
    )(
        meta, cotangent, middle, mix2, own_values, h_own, channel_key_weight, channel_value_weight,
        channel_receptance_weight, ckr_one, ckr_two, ckr_three, ckr_four, cv_near, cv_next, cv_other, cv_last,
    )
    a_sum = Halving(key_send, key_keep, size, key_steps, groups)
    b_sum = Halving(value_send, value_keep, size, value_steps, groups)

    d_middle, d_att, dg_own, dg_far, sums2 = pl.pallas_call(
        middle_back_kernel,
        grid_spec=pltpu.PrefetchScalarGridSpec(
            num_scalar_prefetch=1,
            grid=(blocks,),
            in_specs=[
                segment_spec(back), rows_spec(width, back), rows_spec(width, back), rows_spec(half, back),
                rows_spec(half, back), whole((width, width)), bound_spec(back), whole((16, width)),
                whole((half, width)), whole((half, width)),
            ],
            out_specs=[
                rows_spec(width, back), rows_spec(width, back), rows_spec(half, back), rows_spec(half, back),
                whole((8, width)),
            ],
            scratch_shapes=[pltpu.VMEM((1, width), F32)],
        ),
        out_shape=[
            shape_of((length, width), F32), shape_of((length, width), BF16),
            shape_of((length, half), F32), shape_of((length, half), F32), shape((8, width), F32),
        ],
        compiler_params=params(48),
        name="middle_back",
    )(*in_hbm(meta, cotangent, middle, d_key, rec_own, rec_far, cr, bounds2, vectors, output_weight, wo_far))

    def scan_back(grads, saved, starts, channels):
        return pl.pallas_call(
            scan_back_kernel,
            grid=(blocks,),
            in_specs=[
                rows_spec(half, back), stack_spec(7, half, back),
                stack_spec(2, half, back, size_of=chunks), whole((8, half)),
            ],
            out_specs=[stack_spec(3, half, back), whole((8, half))],
            out_shape=[shape((3, length, half), BF16), shape((8, half), F32)],
            scratch_shapes=[pltpu.VMEM((block, half), F32)] * 3
            + [pltpu.VMEM((8, half), F32), pltpu.VMEM((5, chunks + 8, half), F32)],
            compiler_params=params(48),
            name="scan_back",
        )(grads, saved, starts, channels)

    def round_of(parts, extra, keep, join=False, pin=0):
        gots, sends, extra, keep = together(
            [item.exchange() for item in parts], [(item.send, item.keep) for item in parts], extra, keep
        )
        for item, (send, kept) in zip(parts, sends):
            item.send, item.keep = send, kept
        return add_all(parts, gots, join, pin), extra, keep

    def active(*items):
        return [item for item in items if item.steps]

    def gradients(steps, arrays, tasks, name):
        steps = halving_steps(size, steps)
        send, keep = weight_gradient(halving_order(size, steps), groups, meta, arrays, tasks, name)
        return Halving(send, keep, size, steps, groups)

    c_sum = gradients(
        (1, 4, 8, 2, 0), [d_att, gated_far, gated_own, mix2, rec_far, rec_own],
        [((0, None), (1, None), (2, None)), ((3, 1), (4, None), (5, None))], "output_gradients",
    )
    _, (mixed_in, c_sum.send, c_sum.keep), dgs = round_of(
        active(a_sum, b_sum), (swapped(mixed_far), c_sum.send, c_sum.keep), (dg_far, dg_own), pin=2
    )
    d_far, channel_sums_far = scan_back(dgs[0], save_far, start_far, far_channels)
    d_own, channel_sums_own = scan_back(dgs[1], save_own, start_own, own_channels)
    d_sum = gradients(
        (1, 2, 4, 8, 0), [mix1, d_far, d_own], [((0, n), (1, n), (2, n)) for n in range(3)], "projection_gradients"
    )
    _, (d_sum.send, d_sum.keep), d_middle = round_of(
        active(a_sum, b_sum, c_sum), (d_sum.send, d_sum.keep), d_middle, pin=2
    )
    grad_part, sums1 = pl.pallas_call(
        last_kernel,
        grid_spec=pltpu.PrefetchScalarGridSpec(
            num_scalar_prefetch=1,
            grid=(blocks,),
            in_specs=[
                segment_spec(back), rows_spec(width, back), stack_spec(3, half, back), stack_spec(3, half, back),
                whole((width, half)), whole((width, half)), whole((width, half)), whole((3, width, half)),
                bound_spec(back), whole((16, width)),
            ],
            out_specs=[rows_spec(width, back), whole((8, width))],
            scratch_shapes=[pltpu.VMEM((1, width), F32)],
        ),
        out_shape=[shape((length, width), BF16), shape((8, width), F32)],
        compiler_params=params(48),
        name="time_mix_back",
    )(
        meta, tokens, d_middle, d_own, d_far, key_weight, value_weight, receptance_weight, far_kvr,
        bounds1, vectors,
    )

    def both(own, far):
        return jnp.where(side == 0, jnp.stack([own, far]), jnp.stack([far, own]))

    def full(own, far):
        return jnp.where(side == 0, jnp.concatenate([own, far]), jnp.concatenate([far, own]))

    small = jnp.concatenate([
        sums1[0:2], sums2[0:2], sums1[2:5], sums2[2:4],
        jnp.stack([full(channel_sums_own[n], channel_sums_far[n]) for n in range(2)]),
    ])
    last_rows = jnp.concatenate([last_att, last_ffn])
    (ab_sum, *_), (grad_part, small), (last_rows, final_far) = round_of(
        active(a_sum, b_sum, c_sum, d_sum), (grad_part, small), (last_rows, final_far), True, 1
    ) if groups > 1 else ([a_sum], (grad_part, small), (last_rows, final_far))
    first, second = grad_part[: length // 2], grad_part[length // 2 :]

    def live():
        return active(ab_sum, c_sum, d_sum)

    def small_parts(bits):
        return [crossed(small, size, bit) if bit else swapped(small) for bit in bits]

    _, (first_in, got), (second, last_rows, final_far) = round_of(
        live(), (swapped(first), small_parts([1])), (second, last_rows, final_far)
    )
    small = small + got[0]
    _, (second_in, got), (last_rows, final_far) = round_of(
        live(), (swapped(second), small_parts([2])), (last_rows, final_far)
    )
    small = small + got[0]
    _, (last_in, back_states, got), _ = round_of(
        live(), (swapped(last_rows), swapped(final_far), small_parts([0])), ()
    )
    small = small + got[0]
    bit = 4
    while bit < size:
        pair = bit * 2 < size
        _, got, _ = round_of(live(), small_parts([bit, 2 * bit, 3 * bit] if pair else [bit]), ())
        small = small + got[0]
        if pair:
            small = small + (got[1] + got[2])
        bit *= 4
    while live():
        round_of(live(), (), ())
    grad_tokens = both(grad_part, jnp.concatenate([first_in, second_in])).astype(F32)
    mixed_out = both(mixed_own, mixed_in)
    finals = [both(final_own[n], back_states[n]) for n in range(3)]
    last_rows = both(last_rows, last_in)
    g_ck, g_cv = (a_sum.result(), b_sum.result()) if groups == 1 else ab_sum.result()
    g_other, g_kvr = c_sum.result(), d_sum.result()
    return (
        (mixed_out, grad_tokens, *finals, last_rows[:, 0], last_rows[:, 1])
        + tuple(small[n] for n in range(11))
        + tuple(g_kvr[:, n * half : (n + 1) * half] for n in range(3))
        + (g_other[:, :half].T, g_ck, g_other[:, half:], g_cv.T)
    )


def solution(mesh):
    split = P("dp", "tensor")
    turned = P("tensor", "dp")
    return jax.shard_map(
        functools.partial(shards, mesh.shape["dp"]),
        mesh=mesh,
        in_specs=(P("dp"), P("dp"), P("dp"), P("dp"), split, split, split)
        + (P(),) * 9
        + (P("tensor"), P("tensor"))
        + (P(None, "tensor"),) * 3
        + (P("tensor"), P(None, "tensor"), P(None, "tensor"), P("tensor")),
        out_specs=(P("dp", None, "tensor"), P("dp"), split, split, split, P("dp"), P("dp"))
        + (P(),) * 11
        + (split, split, split, turned, split, split, turned),
        check_vma=False,
    )
```
